256 devices in a mesh: section: 8 (over x, z_lo), dp: 32 (over z_hi, y, core).
Axes of the slice: x: 4, y: 4, z: 8 (z_hi: 4, z_lo: 2; z = z_hi * 2 + z_lo), core: 2. Of those that a mesh axis runs over, the one named last changes fastest.
Arguments:
- entries: bfloat16 [2, 3, 1024, 3072], P(None, None, 'dp'), may hold values from -6 to 6
- cotangents: bfloat16 [2, 3, 1024, 3072], P(None, None, 'dp'), may hold values from -6 to 6
- scales: bfloat16 [8, 2, 3072], P('section', None, 'dp'), may hold values from 0.5 to 1.5
- key_weight: bfloat16 [8, 3072, 256], P('section', 'dp'), may hold values from -0.109375 to 0.109375
- rate_weight: bfloat16 [8, 3072, 24], P('section', 'dp'), may hold values from -0.109375 to 0.109375
- rate_bias: bfloat16 [8, 24], P('section'), may hold values from -7 to -3
Outputs:
- grad_scales: float32 [8, 2, 3072], P('section', None, 'dp')
- grad_keys: float32 [8, 3072, 256], P('section', 'dp')
- grad_rates: float32 [8, 3072, 24], P('section', 'dp')
- grad_bias: float32 [8, 24], P('section')
The draws below stay inside these ranges and needn't reach their ends.
All inputs are finite; a program needn't handle non-finite values.
Results may differ from the reference program's by a relative error of at most 0.025.
Values may be sent and summed in bfloat16 or wider, within the bound.
No kernel may reach another device: no remote copies, remote signals or barrier semaphores. Data moves between devices by JAX's collectives and lax.ppermute only.
A program may use at most 128 MiB of HBM per device.

```python
import jax
import jax.numpy as jnp
from jax import lax

D = 3072
HEAD = 128
HEADS = 24
SEQ = 32
MICRO = 3
TOKENS = 1024
LAYERS = 8


def with_spikes(values, key, source, target, blocks, factor):
    def block_of(axis_at):
        return (jnp.arange(values.shape[axis_at]) // (values.shape[axis_at] // blocks)).reshape((-1,) + (1,) * (values.ndim - 1 - axis_at))

    near = jax.random.permutation(key, blocks)[block_of(target)]
    far = (block_of(target) + blocks // 2) % blocks
    return jnp.where((block_of(source) == near) | (block_of(source) == far), factor * values, values)


def levels(key, extent, cuts, smallest, largest):
    gain = 1.0
    for dim, blocks in cuts:
        draws = jax.random.uniform(jax.random.fold_in(jax.random.fold_in(key, 6), dim), (blocks,), jnp.float32, smallest / len(cuts), largest / len(cuts))
        gain = gain * jnp.repeat(jnp.exp(draws), extent[dim] // blocks).reshape((-1,) + (1,) * (len(extent) - 1 - dim))
    return gain


def noise(stream_key, extent, scale, limit, pieces=(), held_as=jnp.bfloat16):
    values = scale * jax.random.normal(stream_key, extent, jnp.float32)
    if pieces:
        values = values * levels(stream_key, extent, pieces, -0.22, 0.18)
    return jnp.clip(values, -limit, limit).astype(held_as)


def gaussian_with(rng, dims, width, most, cuts, heavy, held_as=jnp.bfloat16):
    values = width * jax.random.normal(rng, dims, jnp.float32)
    if cuts:
        values = values * levels(rng, dims, cuts, -0.22, 0.18)
    return jnp.clip(with_spikes(values, jax.random.fold_in(rng, 3), *heavy), -most, most).astype(held_as)


def setup_inputs(seed: int = 0) -> dict:
    streams_of = jax.random.split(jax.random.key(seed), 7)
    entries = noise(streams_of[0], (2, MICRO, TOKENS, D), 1.0, 6.0, ((2, 32),))
    cotangents = gaussian_with(streams_of[1], (2, MICRO, TOKENS, D), 1.0, 6.0, ((2, 32),), (2, 3, 32, 2.75))
    scales = jnp.clip(0.5 + 1.0 * jax.random.uniform(streams_of[2], (LAYERS, 2, D), jnp.float32) ** levels(streams_of[2], (LAYERS, 2, D), ((0, 8), (2, 32)), -0.2, 0.2), 0.5, 1.5).astype(jnp.bfloat16)
    key_weight = noise(streams_of[3], (LAYERS, D, 2 * HEAD), D ** -0.5, 0.109375, ((0, 8), (1, 32)))
    rate_weight = noise(streams_of[4], (LAYERS, D, HEADS), D ** -0.5, 0.109375, ((0, 8), (1, 32)))
    rate_bias = jnp.clip(-7.0 + 4.0 * jax.random.uniform(streams_of[5], (LAYERS, HEADS), jnp.float32) ** levels(streams_of[5], (LAYERS, HEADS), ((0, 8),), -0.2, 0.2), -7.0, -3.0).astype(jnp.bfloat16)
    return {"entries": entries, "cotangents": cotangents, "scales": scales, "key_weight": key_weight, "rate_weight": rate_weight, "rate_bias": rate_bias}


highest = lax.Precision.HIGHEST

def normalize(stream_f, gain_row):
    return stream_f * lax.rsqrt(lax.optimization_barrier(jnp.mean(stream_f * stream_f, axis=-1, keepdims=True)) + 1e-05) * gain_row

def mixer(stream_f, values_f, key_query, rate_logits, out_scale, bias_row):
    batch_size, seq_len, width_all = stream_f.shape
    head_count = rate_logits.shape[-1]
    head_size = key_query.shape[-1] // 2
    key_rows = key_query[..., :head_size]
    query_rows = key_query[..., head_size:]
    unit_keys = key_rows * lax.rsqrt(lax.optimization_barrier(jnp.sum(key_rows * key_rows, axis=-1, keepdims=True)) + 1e-06)
    step_rate = jax.nn.softplus(rate_logits + bias_row)
    log_keep = -jnp.log1p(step_rate)
    write_rate = step_rate / (1.0 + step_rate)
    log_total = jnp.swapaxes(jnp.cumsum(log_keep, axis=1), 1, 2)
    write_heads = jnp.swapaxes(write_rate, 1, 2)
    scores = jnp.einsum('btc,bsc->bts', query_rows, unit_keys, precision=highest)
    row_pos = lax.broadcasted_iota(jnp.int32, (seq_len, seq_len), 0)
    col_pos = lax.broadcasted_iota(jnp.int32, (seq_len, seq_len), 1)
    causal = row_pos >= col_pos
    decay_gap = jnp.where(causal, log_total[:, :, :, None] - log_total[:, :, None, :], jnp.zeros_like(log_total[:, :, :, None]))
    mixing = jnp.where(causal, jnp.exp(decay_gap) * write_heads[:, :, None, :] * scores[:, None, :, :], jnp.zeros_like(decay_gap))
    per_head = values_f.reshape(batch_size, seq_len, head_count, head_size)
    output = jnp.einsum('bhts,bshc->bthc', mixing, per_head, precision=highest)
    return stream_f + out_scale * output.reshape(batch_size, seq_len, width_all)

def make_normed(stream, params):
    stream_f = stream.astype(jnp.float32)
    gain_row = params[0][0].astype(jnp.float32)
    normed = normalize(stream_f, gain_row).astype(jnp.bfloat16)
    return lax.optimization_barrier(normed)

def layer_forward(stream, normed, params):
    scales, key_weight, rate_weight, rate_bias = params
    batch_size, seq_len, width_all = stream.shape
    flat_rows = normed.reshape(batch_size * seq_len, width_all)
    key_query = jnp.dot(flat_rows, key_weight, preferred_element_type=jnp.float32).reshape(batch_size, seq_len, -1)
    rate_logits = jnp.dot(flat_rows, rate_weight, preferred_element_type=jnp.float32).reshape(batch_size, seq_len, -1)
    mixed = mixer(stream.astype(jnp.float32), normed.astype(jnp.float32), key_query, rate_logits, scales[1].astype(jnp.float32), rate_bias.astype(jnp.float32))
    return mixed.astype(jnp.bfloat16)

def layer_backward(stream, normed, params, cotangent):
    scales, key_weight, rate_weight, rate_bias = params
    batch_size, seq_len, width_all = stream.shape
    row_count = batch_size * seq_len
    stream_f = stream.astype(jnp.float32)
    gain_row = scales[0].astype(jnp.float32)
    flat_rows = normed.reshape(row_count, width_all)
    key_query = jnp.dot(flat_rows, key_weight, preferred_element_type=jnp.float32).reshape(batch_size, seq_len, -1)
    rate_logits = jnp.dot(flat_rows, rate_weight, preferred_element_type=jnp.float32).reshape(batch_size, seq_len, -1)
    unused, pull_mix = jax.vjp(mixer, stream_f, normed.astype(jnp.float32), key_query, rate_logits, scales[1].astype(jnp.float32), rate_bias.astype(jnp.float32))
    d_stream, d_values, d_keyq, d_rates, d_out, d_bias = pull_mix(cotangent.astype(jnp.float32))
    keyq_low = d_keyq.astype(jnp.bfloat16).reshape(row_count, -1)
    rates_low = d_rates.astype(jnp.bfloat16).reshape(row_count, -1)
    contract_rows = (((0,), (0,)), ((), ()))
    grad_keys = lax.dot_general(flat_rows, keyq_low, contract_rows, preferred_element_type=jnp.float32)
    grad_rates = lax.dot_general(flat_rows, rates_low, contract_rows, preferred_element_type=jnp.float32)
    contract_cols = (((1,), (1,)), ((), ()))
    back_normed = lax.dot_general(keyq_low, key_weight, contract_cols, preferred_element_type=jnp.float32)
    back_normed = back_normed + lax.dot_general(rates_low, rate_weight, contract_cols, preferred_element_type=jnp.float32)
    d_normed = d_values + back_normed.reshape(batch_size, seq_len, width_all)
    unused_norm, pull_norm = jax.vjp(normalize, stream_f, gain_row)
    d_input, d_gain = pull_norm(d_normed)
    d_total = (d_stream + d_input).astype(jnp.bfloat16)
    return (d_total, (jnp.stack([d_gain, d_out]), grad_keys, grad_rates, d_bias))

def reference(entries, cotangents, scales, key_weight, rate_weight, rate_bias):
    section_count = scales.shape[0]
    stream = entries.reshape(-1, SEQ, D)
    inputs_kept = []
    normed_kept = []
    for layer_num in range(section_count):
        params = (scales[layer_num], key_weight[layer_num], rate_weight[layer_num], rate_bias[layer_num])
        normed = make_normed(stream, params)
        inputs_kept.append(stream)
        normed_kept.append(normed)
        if layer_num + 1 < section_count:
            stream = layer_forward(stream, normed, params)
    back = cotangents.reshape(-1, SEQ, D)
    layer_grads = [None] * section_count
    for layer_num in reversed(range(section_count)):
        params = (scales[layer_num], key_weight[layer_num], rate_weight[layer_num], rate_bias[layer_num])
        back, layer_grads[layer_num] = layer_backward(inputs_kept[layer_num], normed_kept[layer_num], params, back)
    return (jnp.stack([entry_grads[0] for entry_grads in layer_grads]), jnp.stack([entry_grads[1] for entry_grads in layer_grads]), jnp.stack([entry_grads[2] for entry_grads in layer_grads]), jnp.stack([entry_grads[3] for entry_grads in layer_grads]))
```

```python
import functools

import jax
import jax.numpy as jnp
from jax import lax
from jax.experimental import pallas as pl
from jax.experimental.pallas import tpu as pltpu
from jax.sharding import Mesh, PartitionSpec as P

F32 = jnp.float32
BF16 = jnp.bfloat16
HIGH = lax.Precision.HIGHEST
SECTION = ("x", "zl")
DP = ("zh", "y", "c")

T = 32
D = 3072
C = 128
H = 24
GROUPS = H // 4
W = H * T
LAYERS = 8
SEQS = 6
ROWS = 96
PIECE = 112
CHUNK = 2
CHUNKS = LAYERS // CHUNK
TOK = LAYERS * T
BLOCK = 384
PAY = 48


def iota(shape, axis):
    return lax.broadcasted_iota(jnp.int32, shape, axis)


def nt(a, b, precision=None):
    return lax.dot_general(
        a, b, (((1,), (1,)), ((), ())), precision=precision, preferred_element_type=F32
    )


def tn(a, b, precision=None):
    return lax.dot_general(
        a, b, (((0,), (0,)), ((), ())), precision=precision, preferred_element_type=F32
    )


def nn(a, b, precision=None):
    return jnp.dot(a, b, precision=precision, preferred_element_type=F32)


def split3(a):
    hi = a.astype(BF16)
    rest = a - hi.astype(F32)
    mid = rest.astype(BF16)
    low = (rest - mid.astype(F32)).astype(BF16)
    return jnp.concatenate([hi, mid, low, jnp.zeros_like(hi)], axis=1)


def masks():
    row = iota((T, W), 0)
    col = iota((T, W), 1) % T
    spread = (iota((C, W), 0) % T == iota((C, W), 1) // T) & (iota((C, W), 0) < 3 * T)
    spread = jnp.where(spread, 1.0, 0.0).astype(BF16)
    block = iota((C, C), 0) // T == iota((C, C), 1) // T
    tri = jnp.where(iota((T, T), 0) >= iota((T, T), 1), 1.0, 0.0).astype(F32)
    return row >= col, row == col, spread, block, tri


def mix_terms(key_query, logits, consts):
    causal, diag, spread, block, tri = consts
    head = iota((T, T), 1) < H
    rate = jnp.maximum(logits, 0.0) + jnp.log1p(jnp.exp(-jnp.abs(logits)))
    rate = jnp.where(head, rate, 0.0)
    keep = 1.0 / (1.0 + rate)
    write = rate * keep
    total = nn(tri, -jnp.log1p(rate), HIGH)
    wide = nn(jnp.concatenate([split3(total), split3(write)], axis=0), spread)
    total_t, write_t = wide[:T], wide[T:]
    total_s = jnp.sum(jnp.where(diag, total_t, 0.0), axis=0, keepdims=True)
    write_s = jnp.sum(jnp.where(diag, write_t, 0.0), axis=0, keepdims=True)
    decay = jnp.where(causal, jnp.exp(jnp.where(causal, total_t - total_s, 0.0)), 0.0)
    k = key_query[:, :C]
    q = key_query[:, C:]
    inv = lax.rsqrt(jnp.sum(k * k, axis=1, keepdims=True) + 1e-06)
    unit = k * inv
    unit4 = jnp.concatenate([unit] * 4, axis=0)
    scores = nt(q, unit4, HIGH)
    return rate, keep, write_s, decay, k, q, inv, unit4, scores


def stack_heads(a, g):
    return jnp.concatenate([a[:, C * (4 * g + j) : C * (4 * g + j + 1)] for j in range(4)], axis=0)


def unstack_heads(parts):
    return jnp.concatenate([p[T * j : T * (j + 1)] for p in parts for j in range(4)], axis=1)


def block_diag(mixing, g, block):
    one = mixing[:, C * g : C * (g + 1)]
    return jnp.where(block, jnp.concatenate([one] * 4, axis=0), 0.0).astype(BF16)


def assemble_rows(z_ref):
    out = []
    lane = iota((T, C), 1)
    for m in range(8):
        p = []
        for i in range(4):
            z = z_ref[4 * m + i].astype(F32)
            p.append(jnp.concatenate([z[:, :C], z[:, C:]], axis=0))
        p1 = pltpu.roll(p[1], 96, 1)
        p2 = pltpu.roll(p[2], 64, 1)
        p3 = pltpu.roll(p[3], 32, 1)
        out.append(jnp.where(lane < 96, p[0], p1))
        out.append(jnp.where(lane < 64, p1, p2))
        out.append(jnp.where(lane < 32, p2, p3))
    return jnp.concatenate(out, axis=1)


def forward_kernel(pos_ref, *refs):
    pieces = refs[:10]
    stream_ref = refs[10]
    next_ref, xs_ref, ns_ref, mixed_ref, proj_ref, keys_ref, rows_ref = refs[11:18]
    k_scr, z_scr, sems = refs[18:]
    y, c = pos_ref[0], pos_ref[1]
    copies = []
    for layer in range(CHUNK):
        now = []
        for kc in range(2):
            cc = (c + kc) % 2
            for n, (ky, lo, hi) in enumerate([(0, 0, 4), (1, 0, 4), (3, 0, 4), (2, 0, 2), (2, 2, 4)]):
                yy = (y + 4 - ky) % 4
                src = pieces[kc * 5 + n]
                for where, scr, (a, b) in ((0, k_scr, (0, ROWS)), (1, z_scr, (ROWS, PIECE))):
                    copy = pltpu.make_async_copy(
                        src.at[:, layer, a:b, :],
                        scr.at[layer, lo:hi, yy, cc],
                        sems.at[layer, where, kc * 5 + n],
                    )
                    copy.start()
                    now.append(copy)
        copies.append(now)
    consts = masks()
    block = consts[3]
    stream = stream_ref[...]
    for layer in range(CHUNK):
        for copy in copies[layer]:
            copy.wait()
        rows = assemble_rows(z_scr.at[layer].reshape(32, 16, 256))
        rows_low = rows.astype(BF16)
        rows_ref[layer] = rows_low
        keys = k_scr[layer].reshape(D, 256)
        keys_ref[layer] = keys
        gain, scale, bias = rows[24:25], rows[25:26], rows[26:27, :T]
        xs_ref[layer] = stream
        x = stream.astype(F32)
        inv_rms = lax.rsqrt(jnp.sum(x * x, axis=1, keepdims=True) * (1.0 / D) + 1e-05)
        normed = (x * inv_rms * gain).astype(BF16)
        ns_ref[layer] = normed
        key_query = nn(normed, keys)
        logits = nt(normed, rows_low) + bias
        proj_ref[layer] = jnp.concatenate([key_query, logits, jnp.zeros((T, 96), F32)], axis=1)
        rate, keep, write_s, decay, k, q, inv, unit4, scores = mix_terms(key_query, logits, consts)
        mixing = decay * write_s * jnp.concatenate([scores] * GROUPS, axis=1)
        parts = [
            nn(block_diag(mixing, g, block), stack_heads(normed, g)) for g in range(GROUPS)
        ]
        mixed = unstack_heads(parts)
        mixed_ref[layer] = mixed.astype(BF16)
        stream = (x + scale * mixed).astype(BF16)
    next_ref[...] = stream


def backward_kernel(
    back_ref, xs_ref, ns_ref, mixed_ref, proj_ref, keys_ref, rows_ref, out_ref, pay_ref, k_scr, sems
):
    copies = []
    for layer in range(CHUNK):
        copy = pltpu.make_async_copy(keys_ref.at[layer], k_scr.at[layer], sems.at[layer])
        copy.start()
        copies.append(copy)
    consts = masks()
    causal, diag, spread, block, tri = consts
    back = back_ref[...]
    for layer in reversed(range(CHUNK)):
        x = xs_ref[layer].astype(F32)
        normed = ns_ref[layer]
        rows_low = rows_ref[layer]
        rows = rows_low[16:32].astype(F32)
        gain, scale = rows[8:9], rows[9:10]
        dy = back.astype(F32)
        key_query = proj_ref[layer][:, :256]
        logits = proj_ref[layer][:, 256 : 256 + T]
        rate, keep, write_s, decay, k, q, inv, unit4, scores = mix_terms(key_query, logits, consts)
        scores6 = jnp.concatenate([scores] * GROUPS, axis=1)
        mixing = decay * write_s * scores6
        d_scale = jnp.sum(dy * mixed_ref[layer].astype(F32), axis=0, keepdims=True)
        d_out = (dy * scale).astype(BF16)
        d_mix = []
        d_values = []
        for g in range(GROUPS):
            grad = stack_heads(d_out, g)
            full = jnp.where(block, nt(grad, stack_heads(normed, g)), 0.0)
            d_mix.append(full[:T] + full[T : 2 * T] + full[2 * T : 3 * T] + full[3 * T :])
            d_values.append(tn(block_diag(mixing, g, block), grad))
        d_mix = jnp.concatenate(d_mix, axis=1)
        d_values = unstack_heads(d_values)
        near = d_mix * decay
        scored = near * scores6
        d_write_s = jnp.sum(scored, axis=0, keepdims=True)
        weighted = near * write_s
        d_scores = sum(weighted[:, C * g : C * (g + 1)] for g in range(GROUPS))
        d_total = scored * write_s - jnp.where(diag, d_write_s * write_s, 0.0)
        d_write = jnp.where(diag, d_write_s, 0.0)
        gathered = []
        for part in (d_total, d_write):
            hi = part.astype(BF16)
            gathered += [hi, (part - hi.astype(F32)).astype(BF16)]
        summed = nt(jnp.concatenate(gathered, axis=0), spread[:T])
        d_total = summed[:T] + summed[T : 2 * T]
        d_write = summed[2 * T : 3 * T] + summed[3 * T :]
        d_log = tn(tri, d_total, HIGH)
        d_rate = keep * (d_write * keep - d_log)
        d_logits = d_rate / (1.0 + jnp.exp(-logits))
        d_logits = jnp.where(iota((T, T), 1) < H, d_logits, 0.0)
        d_q = nn(d_scores, unit4, HIGH)
        d_unit = tn(d_scores, q, HIGH)
        d_unit = d_unit[:T] + d_unit[T : 2 * T] + d_unit[2 * T : 3 * T] + d_unit[3 * T :]
        d_k = inv * d_unit - k * (inv * inv * inv * jnp.sum(d_unit * k, axis=1, keepdims=True))
        d_keyq = jnp.concatenate([d_k, d_q], axis=1).astype(BF16)
        d_low = d_logits.astype(BF16)
        copies[layer].wait()
        d_normed = d_values + nt(d_keyq, k_scr[layer]) + nn(d_low, rows_low)
        inv_rms = lax.rsqrt(jnp.sum(x * x, axis=1, keepdims=True) * (1.0 / D) + 1e-05)
        x_hat = x * inv_rms
        d_gain = jnp.sum(d_normed * x_hat, axis=0, keepdims=True)
        d_hat = d_normed * gain
        mean = jnp.sum(d_hat * x_hat, axis=1, keepdims=True) * (1.0 / D)
        back = (dy + inv_rms * (d_hat - x_hat * mean)).astype(BF16)
        pay_ref[layer, :T, :256] = d_keyq
        pay_ref[layer, :T, 256:] = jnp.concatenate([d_low, jnp.zeros((T, 96), BF16)], axis=1)
        pay_ref[layer, T:] = jnp.concatenate(
            [d[:, BLOCK * i : BLOCK * (i + 1)] for d in (d_gain, d_scale) for i in range(8)], axis=0
        ).astype(BF16)
    out_ref[...] = back


def route_kernel(pos_ref, *refs):
    ins, outs, sem = refs[:CHUNKS], refs[CHUNKS : CHUNKS + LAYERS], refs[-1]
    section = pos_ref[0]
    for k in range(LAYERS):
        layer = (section + k) % LAYERS
        for i in range(CHUNKS):
            @pl.when(layer // CHUNK == i)
            def _(i=i, k=k, layer=layer):
                pltpu.make_async_copy(ins[i].at[layer % CHUNK], outs[k], sem.at[k]).start()
    for k in range(LAYERS):
        pltpu.make_async_copy(ins[0].at[0], outs[k], sem.at[k]).wait()


def spread_kernel(pos_ref, *refs):
    ins, outs, sem = refs[:LAYERS], refs[LAYERS : LAYERS + 8], refs[-1]
    y, c = pos_ref[0], pos_ref[1]
    for ky in range(4):
        for kc in range(2):
            peer = ((y + ky) % 4) * 2 + (c + kc) % 2
            for k in range(LAYERS):
                pltpu.make_async_copy(
                    ins[k].at[:, pl.ds(pl.multiple_of(peer * BLOCK, BLOCK), BLOCK)],
                    outs[ky * 2 + kc].at[pl.ds(T * k, T)],
                    sem.at[ky * 2 + kc],
                ).start()
    for i in range(8):
        pltpu.make_async_copy(outs[i], outs[i], sem.at[i]).wait()


def pack_kernel(*refs):
    ins, out_ref = refs[:LAYERS], refs[LAYERS]
    total = jnp.zeros((16, BLOCK), F32)
    for k in range(LAYERS):
        out_ref[T * k : T * (k + 1)] = ins[k][:T]
        total = total + ins[k][T:].astype(F32)
    out_ref[TOK:] = total.astype(BF16)


def weight_kernel(pos_ref, *refs):
    normed, pay = refs[:8], refs[8:16]
    outs, scr = refs[16:20], refs[20]
    index, zh = pos_ref[0] * 2 + pos_ref[1], pos_ref[2]
    total = jnp.zeros((BLOCK, BLOCK), F32)
    extra = jnp.zeros((16, BLOCK), F32)
    bias = jnp.zeros((1, C), F32)
    for i in range(8):
        tokens = pay[i][:TOK]
        total = total + tn(normed[i][...], tokens)
        extra = extra + pay[i][TOK:].astype(F32)
        bias = bias + jnp.sum(tokens[:, 256:].astype(F32), axis=0, keepdims=True)
    scr[...] = total.astype(BF16)
    row = iota((16, BLOCK), 0)
    gain = jnp.sum(jnp.where(row == index, extra, 0.0), axis=0, keepdims=True)
    scale = jnp.sum(jnp.where(row == index + 8, extra, 0.0), axis=0, keepdims=True)
    for k in range(4):
        i = (zh + k) % 4
        outs[k][:ROWS] = scr[pl.ds(pl.multiple_of(i * ROWS, ROWS), ROWS)]
        own = []
        for line in (gain, scale):
            wide = line[:, :C]
            for j in range(1, 4):
                moved = jnp.concatenate([line[:, ROWS * j : ROWS * (j + 1)], jnp.zeros((1, 32), F32)], axis=1)
                wide = jnp.where(i == j, moved, wide)
            own.append(jnp.concatenate([wide, jnp.zeros((1, 256), F32)], axis=1))
        own.append(jnp.concatenate([bias, jnp.zeros((1, 256), F32)], axis=1))
        own.append(jnp.zeros((13, BLOCK), F32))
        outs[k][ROWS:] = jnp.concatenate(own, axis=0).astype(BF16)


def final_kernel(a, b, c, d, scales_ref, keys_ref, rates_ref, bias_ref):
    total = a[...].astype(F32) + b[...].astype(F32) + c[...].astype(F32) + d[...].astype(F32)
    keys_ref[...] = total[:ROWS, :256]
    rates_ref[...] = total[:ROWS, 256 : 256 + H]
    scales_ref[...] = total[ROWS : ROWS + 2, :ROWS]
    bias_ref[...] = total[ROWS + 2 : ROWS + 3, :H]


ANY = pl.BlockSpec(memory_space=pl.ANY)
VMEM = pl.BlockSpec(memory_space=pltpu.VMEM)
SMEM = pl.BlockSpec(memory_space=pltpu.SMEM)
PARAMS = pltpu.CompilerParams(vmem_limit_bytes=48 * 1024 * 1024)


def shape(*dims, dtype=BF16):
    return jax.ShapeDtypeStruct(dims, dtype)


def call(kernel, outs, ins, scratch, out_spec=None, cost=None):
    flops, moved = cost
    return pl.pallas_call(
        kernel,
        out_shape=outs,
        in_specs=ins,
        out_specs=out_spec or [VMEM] * len(outs),
        scratch_shapes=scratch,
        compiler_params=PARAMS,
        cost_estimate=pl.CostEstimate(flops=flops, bytes_accessed=moved, transcendentals=0),
    )


def shift(array, axis, by):
    n = lax.axis_size(axis)
    return lax.ppermute(array, axis, [(i, (i + by) % n) for i in range(n)])


def per_device(entries, cotangents, scales, key_weight, rate_weight, rate_bias):
    x, zl, zh, y, c = (lax.axis_index(a) for a in ("x", "zl", "zh", "y", "c"))
    section = x * 2 + zl
    mine = jnp.minimum(section, SEQS - 1)
    stream = lax.dynamic_index_in_dim(entries.reshape(SEQS, T, D), mine, 0, keepdims=False)
    back = lax.dynamic_index_in_dim(cotangents.reshape(SEQS, T, D), mine, 0, keepdims=False)
    back = jnp.where(section < SEQS, back, jnp.zeros_like(back))

    wide = jnp.pad(rate_weight[0].T, ((0, 0), (0, C - ROWS)))
    small = jnp.pad(scales[0], ((0, 0), (0, C - ROWS)))
    line = jnp.pad(rate_bias, ((0, 0), (0, C - H)))
    right = jnp.concatenate([wide[16:], small, line, jnp.zeros((5, C), BF16)], axis=0)
    packed = jnp.concatenate(
        [key_weight[0], jnp.concatenate([wide[:16], right], axis=1)], axis=0
    )

    across = jnp.stack([packed] + [shift(packed, "x", k) for k in range(1, 4)])
    across = jnp.take(across, (x + 4 - jnp.arange(4)) % 4, axis=0)
    other = shift(across, "zl", 1)
    layers = jnp.where(
        zl == 0, jnp.stack([across, other], axis=1), jnp.stack([other, across], axis=1)
    ).reshape(CHUNKS, CHUNK, PIECE, 256)

    pos_yc = jnp.stack([y, c]).astype(jnp.int32)
    order = (zh + 4 - jnp.arange(4)) % 4
    saved = []
    for i in range(CHUNKS):
        own = layers[i]
        along = jnp.stack([own] + [shift(own, "zh", k) for k in range(1, 4)])
        along = jnp.take(along, order, axis=0)
        up = shift(along, "y", 1)
        down = shift(along, "y", -1)
        far_lo = shift(up[:2], "y", 1)
        far_hi = shift(down[2:], "y", -1)
        near = [along, up, down, far_lo, far_hi]
        pieces = near + [shift(p, "c", 1) for p in near]
        stream, *kept = call(
            forward_kernel,
            [
                shape(T, D),
                shape(CHUNK, T, D),
                shape(CHUNK, T, D),
                shape(CHUNK, T, D),
                shape(CHUNK, T, BLOCK, dtype=F32),
                shape(CHUNK, D, 256),
                shape(CHUNK, T, D),
            ],
            [SMEM] + [ANY] * 10 + [VMEM],
            [
                pltpu.VMEM((CHUNK, 4, 4, 2, ROWS, 256), BF16),
                pltpu.VMEM((CHUNK, 4, 4, 2, 16, 256), BF16),
                pltpu.SemaphoreType.DMA((CHUNK, 2, 10)),
            ],
            cost=(CHUNK * 300_000_000, CHUNK * 8_000_000),
        )(pos_yc, *pieces, stream)
        saved.append(kept)

    pos_section = section.astype(jnp.int32)[None]
    slots = call(
        route_kernel,
        [shape(T, D)] * LAYERS,
        [SMEM] + [ANY] * CHUNKS,
        [pltpu.SemaphoreType.DMA((LAYERS,))],
        [ANY] * LAYERS,
        cost=(0, 3_200_000),
    )(pos_section, *[kept[1] for kept in saved])

    def to_section(arrays):
        got = [arrays[0]]
        for k in range(1, LAYERS):
            pairs = [(s, (s + k) % LAYERS) for s in range(SEQS)]
            got.append(lax.ppermute(arrays[k], SECTION, pairs))
        return got

    slots = to_section(slots)
    cut = call(
        spread_kernel,
        [shape(TOK, BLOCK)] * 8,
        [SMEM] + [ANY] * LAYERS,
        [pltpu.SemaphoreType.DMA((8,))],
        [ANY] * 8,
        cost=(0, 3_200_000),
    )(pos_yc, *slots)
    normed = [cut[0]]
    for ky in range(4):
        for kc in range(2):
            if ky or kc:
                pairs = [
                    (i, ((i // 2 + ky) % 4) * 2 + (i + kc) % 2) for i in range(8)
                ]
                normed.append(lax.ppermute(cut[ky * 2 + kc], ("y", "c"), pairs))

    pays = [None] * CHUNKS
    for i in reversed(range(CHUNKS)):
        xs, ns, mixed, proj, keys, rows = saved[i]
        back, pays[i] = call(
            backward_kernel,
            [shape(T, D), shape(CHUNK, PAY, BLOCK)],
            [VMEM] * 5 + [ANY, VMEM],
            [pltpu.VMEM((CHUNK, D, 256), BF16), pltpu.SemaphoreType.DMA((CHUNK,))],
            cost=(CHUNK * 900_000_000, CHUNK * 16_000_000),
        )(back, xs, ns, mixed, proj, keys, rows)

    pay = call(
        route_kernel,
        [shape(PAY, BLOCK)] * LAYERS,
        [SMEM] + [ANY] * CHUNKS,
        [pltpu.SemaphoreType.DMA((LAYERS,))],
        [ANY] * LAYERS,
        cost=(0, 600_000),
    )(pos_section, *pays)
    pay = to_section(pay)
    pay = call(
        pack_kernel, [shape(TOK + 16, BLOCK)], [VMEM] * LAYERS, [], cost=(0, 600_000)
    )(*pay)[0]
    by_y = [pay] + [shift(pay, "y", k) for k in range(1, 4)]
    all_pay = []
    for p in by_y:
        all_pay += [p, shift(p, "c", 1)]
    pos = jnp.stack([y, c, zh]).astype(jnp.int32)
    shares = call(
        weight_kernel,
        [shape(PIECE, BLOCK)] * 4,
        [SMEM] + [VMEM] * 16,
        [pltpu.VMEM((BLOCK, BLOCK), BF16)],
        cost=(600_000_000, 4_000_000),
    )(pos, *normed, *all_pay)
    got = [None] * 4
    for k in range(4):
        pairs = [(z * 8 + b, 4 * b + (z + k) % 4) for z in range(4) for b in range(8)]
        got[k] = lax.ppermute(shares[k], DP, pairs)
    g_scales, g_keys, g_rates, g_bias = call(
        final_kernel,
        [
            shape(2, ROWS, dtype=F32),
            shape(ROWS, 256, dtype=F32),
            shape(ROWS, H, dtype=F32),
            shape(1, H, dtype=F32),
        ],
        [VMEM] * 4,
        [],
        cost=(0, 500_000),
    )(*got)
    return g_scales[None], g_keys[None], g_rates[None], g_bias


def solution(mesh):
    fine = Mesh(mesh.devices.reshape(4, 2, 4, 4, 2), ("x", "zl", "zh", "y", "c"))
    placed = (
        P(None, None, DP, None),
        P(None, None, DP, None),
        P(SECTION, None, DP),
        P(SECTION, DP, None),
        P(SECTION, DP, None),
        P(SECTION, None),
    )
    return jax.shard_map(
        per_device,
        mesh=fine,
        in_specs=placed,
        out_specs=(
            P(SECTION, None, DP),
            P(SECTION, DP, None),
            P(SECTION, DP, None),
            P(SECTION, None),
        ),
        check_vma=False,
    )
```

```python
import functools

import jax
import jax.numpy as jnp
from jax import lax
from jax.experimental import pallas as pl
from jax.experimental.pallas import tpu as pltpu
from jax.sharding import Mesh, PartitionSpec as P

F32 = jnp.float32
BF16 = jnp.bfloat16
SECTION = ("x", "zl")
DP = ("zh", "y", "c")

T = 32
D = 3072
C = 128
H = 24
GROUPS = H // 4
W = H * T
LAYERS = 8
SEQS = 6
ROWS = 96
PIECE = 112
TOK = LAYERS * T
BLOCK = 384
BLOCKS = D // BLOCK
SENT = BLOCKS * T + T + 16


def iota(shape, axis):
    return lax.broadcasted_iota(jnp.int32, shape, axis)


def nt(a, b):
    return lax.dot_general(
        a, b, (((1,), (1,)), ((), ())), preferred_element_type=F32
    )


def tn(a, b):
    return lax.dot_general(
        a, b, (((0,), (0,)), ((), ())), preferred_element_type=F32
    )


def nn(a, b):
    return jnp.dot(a, b, preferred_element_type=F32)


def split3(a):
    hi = a.astype(BF16)
    rest = a - hi.astype(F32)
    mid = rest.astype(BF16)
    low = (rest - mid.astype(F32)).astype(BF16)
    return jnp.concatenate([hi, mid, low, jnp.zeros_like(hi)], axis=1)


def masks():
    row = iota((T, W), 0)
    col = iota((T, W), 1) % T
    spread = (iota((C, W), 0) % T == iota((C, W), 1) // T) & (iota((C, W), 0) < 3 * T)
    spread = jnp.where(spread, 1.0, 0.0).astype(BF16)
    block = iota((C, C), 0) // T == iota((C, C), 1) // T
    tri = jnp.where(iota((T, T), 0) >= iota((T, T), 1), 1.0, 0.0).astype(BF16)
    return row >= col, row == col, spread, block, tri


def tile4(a):
    return jnp.concatenate([a] * 4, axis=0)


def stack_heads(a, g):
    return jnp.concatenate([a[:, C * (4 * g + j) : C * (4 * g + j + 1)] for j in range(4)], axis=0)


def unstack_heads(parts):
    return jnp.concatenate([p[T * j : T * (j + 1)] for p in parts for j in range(4)], axis=1)


def block_diag(mixing, g, block):
    return jnp.where(block, tile4(mixing[:, C * g : C * (g + 1)]), 0.0).astype(BF16)


def assemble_rows(piece):
    out = []
    lane = iota((T, C), 1)
    for m in range(8):
        p = []
        for i in range(4):
            z = piece(4 * m + i).astype(F32)
            p.append(jnp.concatenate([z[:, :C], z[:, C:]], axis=0))
        p1 = pltpu.roll(p[1], 96, 1)
        p2 = pltpu.roll(p[2], 64, 1)
        p3 = pltpu.roll(p[3], 32, 1)
        out.append(jnp.where(lane < 96, p[0], p1))
        out.append(jnp.where(lane < 64, p1, p2))
        out.append(jnp.where(lane < 32, p2, p3))
    return jnp.concatenate(out, axis=1)


def cut_rows(rows):
    lane = iota((T, C), 1)
    a, b, c = rows[:, :C], rows[:, C : 2 * C], rows[:, 2 * C :]
    one = jnp.where(lane < 32, pltpu.roll(a, 32, 1), pltpu.roll(b, 32, 1))
    two = jnp.where(lane < 64, pltpu.roll(b, 64, 1), pltpu.roll(c, 64, 1))
    parts = [a, one, two, pltpu.roll(c, 96, 1)]
    return [jnp.concatenate([p[:16], p[16:]], axis=1) for p in parts]


def gray(i):
    return jnp.where(i >= 2, 5 - i, i)


def partner(i, c, first):
    return jnp.where((c == 0) == first, i ^ 1, 3 - i)


def sequence_kernel(pos_ref, *refs):
    left, right = refs[:8], refs[8:16]
    entry_ref, cot_ref, sent_ref = refs[16:19]
    w_scr, rows_scr, xs, ns, mixed_scr, decay_scr, write_scr, small_scr, proj_scr, sem_a, sem_b = refs[19:]
    x, y, c, valid = pos_ref[0], pos_ref[1], pos_ref[2], pos_ref[3]

    def ring(i, core):
        one, two = partner(i, core, True), partner(i, core, False)
        return [i, one, two, partner(two, core, True)]

    copies = []
    for kc in range(2):
        cc = (c + kc) % 2
        ys, xx = ring(y, cc), ring(x, cc)
        for i in range(4):
            for j in range(4):
                at = pl.ds(2 * xx[j], 2)
                copy = pltpu.make_async_copy(
                    left[kc * 4 + i].at[j],
                    w_scr.at[at, :, ys[i], cc, :, :C],
                    sem_a.at[xx[j]],
                )
                copy.start()
                at = pl.ds(2 * xx[i], 2)
                copy = pltpu.make_async_copy(
                    right[kc * 4 + i].at[j],
                    w_scr.at[at, :, ys[j], cc, :, C:],
                    sem_b.at[xx[i]],
                )
                copy.start()

    def wait_layers(at):
        for sem, src in ((sem_a, left[0]), (sem_b, right[0])):
            for _ in range(8):
                pltpu.make_async_copy(
                    src.at[0], w_scr.at[0:2, :, 0, 0, :, :C], sem.at[at]
                ).wait()

    causal, diag, spread, block, tri = masks()

    def keys_of(layer, m):
        parts = [w_scr[layer, m // 2, (m % 2) * 2 + i // 2, i % 2, :ROWS] for i in range(4)]
        return jnp.concatenate(parts, axis=0)

    def forward(layer, stream):
        @pl.when(layer % 2 == 0)
        def _():
            wait_layers(layer // 2)

        rows = assemble_rows(lambda d: w_scr[layer, d // 8, d // 2 % 4, d % 2, ROWS:])
        rows_low = rows.astype(BF16)
        rows_scr[layer] = rows_low
        gain, scale, bias = rows[24:25], rows[25:26], rows[26:27, :T]
        xs[layer] = stream
        x_f = stream.astype(F32)
        inv_rms = lax.rsqrt(jnp.sum(x_f * x_f, axis=1, keepdims=True) * (1.0 / D) + 1e-05)
        normed = (x_f * inv_rms * gain).astype(BF16)
        ns[layer] = normed
        for m in range(BLOCKS):
            sent_ref[layer, T * m : T * (m + 1)] = normed[:, BLOCK * m : BLOCK * (m + 1)]
        logits = nt(normed, rows_low) + bias
        key_query = sum(
            nn(normed[:, BLOCK * m : BLOCK * (m + 1)], keys_of(layer, m)) for m in range(BLOCKS)
        )
        head = iota((T, T), 1) < H
        rate = jnp.maximum(logits, 0.0) + jnp.log1p(jnp.exp(-jnp.abs(logits)))
        rate = jnp.where(head, rate, 0.0)
        keep = 1.0 / (1.0 + rate)
        write = rate * keep
        total = nn(tri, split3(-jnp.log1p(rate)))
        total = total[:, :T] + total[:, T : 2 * T] + total[:, 2 * T : 3 * T]
        wide = nn(jnp.concatenate([split3(total), split3(write)], axis=0), spread)
        total_t, write_t = wide[:T], wide[T:]
        total_s = jnp.sum(jnp.where(diag, total_t, 0.0), axis=0, keepdims=True)
        write_s = jnp.sum(jnp.where(diag, write_t, 0.0), axis=0, keepdims=True)
        decay = jnp.where(causal, jnp.exp(jnp.where(causal, total_t - total_s, 0.0)), 0.0)
        k = key_query[:, :C]
        q = key_query[:, C:]
        inv = lax.rsqrt(jnp.sum(k * k, axis=1, keepdims=True) + 1e-06)
        scores = nt(q.astype(BF16), tile4((k * inv).astype(BF16)))
        decay_scr[layer] = decay
        write_scr[layer] = write_s
        proj_scr[layer] = key_query
        small_scr[layer] = jnp.concatenate([scores, logits, keep, jnp.zeros((T, 64), F32)], axis=1)
        mixing = decay * write_s * jnp.concatenate([scores] * GROUPS, axis=1)
        mixed = unstack_heads(
            [nn(block_diag(mixing, g, block), stack_heads(normed, g)) for g in range(GROUPS)]
        )
        mixed_scr[layer] = mixed.astype(BF16)
        return (x_f + scale * mixed).astype(BF16)

    lax.fori_loop(0, LAYERS, forward, entry_ref[...])

    def backward(step, back):
        layer = LAYERS - 1 - step
        x_f = xs[layer].astype(F32)
        normed = ns[layer]
        rows_low = rows_scr[layer]
        rows = rows_low[16:].astype(F32)
        gain, scale = rows[8:9], rows[9:10]
        dy = back.astype(F32)
        decay = decay_scr[layer]
        write_s = write_scr[layer]
        small = small_scr[layer]
        scores, logits, keep = small[:, :C], small[:, C : C + T], small[:, C + T : C + 2 * T]
        scores6 = jnp.concatenate([scores] * GROUPS, axis=1)
        mixing = decay * write_s * scores6
        d_scale = jnp.sum(dy * mixed_scr[layer].astype(F32), axis=0, keepdims=True)
        d_out = (dy * scale).astype(BF16)
        d_mix = []
        d_values = []
        for g in range(GROUPS):
            grad = stack_heads(d_out, g)
            full = jnp.where(block, nt(grad, stack_heads(normed, g)), 0.0)
            d_mix.append(full[:T] + full[T : 2 * T] + full[2 * T : 3 * T] + full[3 * T :])
            d_values.append(tn(block_diag(mixing, g, block), grad))
        d_mix = jnp.concatenate(d_mix, axis=1)
        d_values = unstack_heads(d_values)
        near = d_mix * decay
        scored = near * scores6
        d_write_s = jnp.sum(scored, axis=0, keepdims=True)
        weighted = near * write_s
        d_scores = sum(weighted[:, C * g : C * (g + 1)] for g in range(GROUPS)).astype(BF16)
        d_total = scored * write_s - jnp.where(diag, d_write_s * write_s, 0.0)
        gathered = []
        for part in (d_total, jnp.where(diag, d_write_s, 0.0)):
            hi = part.astype(BF16)
            gathered += [hi, (part - hi.astype(F32)).astype(BF16)]
        summed = nt(jnp.concatenate(gathered, axis=0), spread[:T])
        d_total = summed[:T] + summed[T : 2 * T]
        d_write = summed[2 * T : 3 * T] + summed[3 * T :]
        d_log = tn(tri, split3(d_total))
        d_log = d_log[:, :T] + d_log[:, T : 2 * T] + d_log[:, 2 * T : 3 * T]
        d_rate = keep * (d_write * keep - d_log)
        d_logits = d_rate / (1.0 + jnp.exp(-logits))
        d_low = jnp.where(iota((T, T), 1) < H, d_logits, 0.0).astype(BF16)
        k = proj_scr[layer][:, :C]
        q = proj_scr[layer][:, C:]
        inv = lax.rsqrt(jnp.sum(k * k, axis=1, keepdims=True) + 1e-06)
        d_q = nn(d_scores, tile4((k * inv).astype(BF16)))
        d_unit = tn(d_scores, q.astype(BF16))
        d_unit = d_unit[:T] + d_unit[T : 2 * T] + d_unit[2 * T : 3 * T] + d_unit[3 * T :]
        d_k = inv * d_unit - k * (inv * inv * inv * jnp.sum(d_unit * k, axis=1, keepdims=True))
        d_keyq = jnp.concatenate([d_k, d_q], axis=1).astype(BF16)
        through = jnp.concatenate([nt(d_keyq, keys_of(layer, m)) for m in range(BLOCKS)], axis=1)
        d_normed = d_values + through + nn(d_low, rows_low)
        inv_rms = lax.rsqrt(jnp.sum(x_f * x_f, axis=1, keepdims=True) * (1.0 / D) + 1e-05)
        x_hat = x_f * inv_rms
        d_gain = jnp.sum(d_normed * x_hat, axis=0, keepdims=True)
        d_hat = d_normed * gain
        mean = jnp.sum(d_hat * x_hat, axis=1, keepdims=True) * (1.0 / D)
        sent_ref[layer, TOK : TOK + T, :256] = d_keyq
        sent_ref[layer, TOK : TOK + T, 256:] = jnp.concatenate(
            [d_low, jnp.zeros((T, 96), BF16)], axis=1
        )
        sent_ref[layer, TOK + T :] = jnp.concatenate(
            [d[:, BLOCK * i : BLOCK * (i + 1)] for d in (d_gain, d_scale) for i in range(8)], axis=0
        ).astype(BF16)
        return (dy + inv_rms * (d_hat - x_hat * mean)).astype(BF16)

    cot = jnp.where(valid > 0, cot_ref[...].astype(F32), 0.0).astype(BF16)
    lax.fori_loop(0, LAYERS, backward, cot)


def weight_kernel(pos_ref, got_ref, keep_ref, send_ref, scr, sem):
    zh, y, c = pos_ref[0], pos_ref[1], pos_ref[2]

    def slot(there, here, core):
        bits = gray(jnp.int32(there)) ^ gray(here)
        return bits if core else (bits & 1) * 2 + (bits >> 1)

    tokens = jnp.concatenate([got_ref[s, TOK : TOK + T] for s in range(LAYERS)], axis=0)
    extra = sum(got_ref[s, TOK + T :].astype(F32) for s in range(LAYERS))
    bias = jnp.sum(tokens[:, 256:].astype(F32), axis=0, keepdims=True)
    bias = jnp.concatenate([bias[:, :ROWS]] * 4, axis=1)
    for m in range(BLOCKS):
        normed = jnp.concatenate([got_ref[s, T * m : T * (m + 1)] for s in range(LAYERS)], axis=0)
        keys = tn(normed, tokens[:, :256])
        rates = tn(tokens[:, 256:], normed)[:H]
        rows = jnp.concatenate(
            [rates, extra[m : m + 1], extra[m + 8 : m + 9], bias, jnp.zeros((5, BLOCK), F32)],
            axis=0,
        )
        low = cut_rows(rows)
        for i in range(4):
            d = 4 * m + i
            z_at, y_at = slot(d // 8, zh, d % 2), slot(d // 2 % 4, y, d % 2)
            c_at = (d + c) % 2
            scr[c_at, z_at, y_at, :ROWS] = keys[ROWS * i : ROWS * (i + 1)].astype(BF16)
            scr[c_at, z_at, y_at, ROWS:] = low[i].astype(BF16)
    for i, ref in enumerate((keep_ref, send_ref)):
        pltpu.make_async_copy(scr.at[i], ref, sem.at[i]).start()
    for i, ref in enumerate((keep_ref, send_ref)):
        pltpu.make_async_copy(scr.at[i], ref, sem.at[i]).wait()


def add_kernel(axis, a_ref, b_ref, keep_ref, send_ref):
    total = (a_ref[...].astype(F32) + b_ref[...].astype(F32)).astype(BF16)
    if axis == 1:
        half = total.shape[1] // 2
        keep_ref[...] = total[:, :half]
        send_ref[...] = total[:, half:]
    else:
        half = total.shape[0] // 2
        keep_ref[...] = total[:half]
        send_ref[...] = total[half:]


def final_kernel(a_ref, b_ref, scales_ref, keys_ref, rates_ref, bias_ref):
    total = a_ref[0].astype(F32) + b_ref[0].astype(F32)
    keys_ref[...] = total[:ROWS]
    rates = jnp.concatenate([total[ROWS:, :C], total[ROWS:, C:]], axis=0)
    wide = jnp.concatenate([rates, jnp.zeros((C - T, C), F32)], axis=0)
    rates_ref[...] = wide.T[:ROWS, :H]
    scales_ref[...] = rates[24:26, :ROWS]
    bias_ref[...] = rates[26:27, :H]


ANY = pl.BlockSpec(memory_space=pl.ANY)
VMEM = pl.BlockSpec(memory_space=pltpu.VMEM)
SMEM = pl.BlockSpec(memory_space=pltpu.SMEM)
PARAMS = pltpu.CompilerParams(vmem_limit_bytes=56 * 1024 * 1024)


def shape(*dims, dtype=BF16):
    return jax.ShapeDtypeStruct(dims, dtype)


def call(kernel, outs, ins, scratch, out_spec=None, cost=None):
    flops, moved = cost
    return pl.pallas_call(
        kernel,
        out_shape=outs,
        in_specs=ins,
        out_specs=out_spec or [VMEM] * len(outs),
        scratch_shapes=scratch,
        compiler_params=PARAMS,
        cost_estimate=pl.CostEstimate(flops=flops, bytes_accessed=moved, transcendentals=0),
    )


def ring_pairs(first):
    pairs = []
    for i in range(4):
        for c in range(2):
            to = i ^ 1 if (c == 0) == first else 3 - i
            pairs.append((i * 2 + c, to * 2 + c))
    return pairs


def swap(array, axis, first):
    return lax.ppermute(array, (axis, "c"), ring_pairs(first))


def other_core(array):
    return lax.ppermute(array, "c", [(0, 1), (1, 0)])


def gather_ring(array, axis):
    one = swap(array, axis, True)
    two = swap(array, axis, False)
    return [array, one, two, swap(one, axis, False)]


def per_device(entries, cotangents, scales, key_weight, rate_weight, rate_bias):
    x, zl, zh, y, c = (lax.axis_index(a) for a in ("x", "zl", "zh", "y", "c"))
    section = x * 2 + zl
    mine = jnp.minimum(section, SEQS - 1)
    stream = lax.dynamic_index_in_dim(entries.reshape(SEQS, T, D), mine, 0, keepdims=False)
    back = lax.dynamic_index_in_dim(cotangents.reshape(SEQS, T, D), mine, 0, keepdims=False)

    wide = jnp.pad(rate_weight[0].T, ((0, 0), (0, C - ROWS)))
    small = jnp.pad(scales[0], ((0, 0), (0, C - ROWS)))
    line = jnp.pad(rate_bias, ((0, 0), (0, C - H)))
    right = jnp.concatenate([wide[16:], small, line, jnp.zeros((5, C), BF16)], axis=0)
    packed = jnp.concatenate(
        [key_weight[0], jnp.concatenate([wide[:16], right], axis=1)], axis=0
    )

    along = jnp.stack(gather_ring(packed, "zh"))
    first, second = partner(zh, c, True), partner(zh, c, False)
    across = partner(second, c, True)
    order = [jnp.where(j == first, 1, jnp.where(j == second, 2, jnp.where(j == across, 3, 0))) for j in range(4)]
    along = jnp.take(along, jnp.stack(order), axis=0)
    pairs = []
    for z in range(8):
        for core in range(2):
            to = z ^ 1 if core == 0 else (z + 1 if z % 2 else z - 1) % 8
            pairs.append(tuple(((i % 2) * 4 + i // 2) * 2 + core for i in (z, to)))
    other = lax.ppermute(along, ("zl", "zh", "c"), pairs)
    both = jnp.where(zl == 0, jnp.stack([along, other]), jnp.stack([other, along]))

    left = jnp.stack(gather_ring(both[..., :C], "x"))
    right = jnp.stack(gather_ring(both[..., C:], "y"))
    left = gather_ring(left, "y")
    right = gather_ring(right, "x")
    left = left + [other_core(a) for a in left]
    right = right + [other_core(a) for a in right]

    pos = jnp.stack([x, y, c, jnp.where(section < SEQS, 1, 0)]).astype(jnp.int32)
    sent = call(
        sequence_kernel,
        [shape(LAYERS, SENT, BLOCK)],
        [SMEM] + [ANY] * 16 + [VMEM] * 2,
        [
            pltpu.VMEM((LAYERS, 4, 4, 2, PIECE, 256), BF16),
            pltpu.VMEM((LAYERS, T, D), BF16),
            pltpu.VMEM((LAYERS, T, D), BF16),
            pltpu.VMEM((LAYERS, T, D), BF16),
            pltpu.VMEM((LAYERS, T, D), BF16),
            pltpu.VMEM((LAYERS, T, W), F32),
            pltpu.VMEM((LAYERS, 1, W), F32),
            pltpu.VMEM((LAYERS, T, 256), F32),
            pltpu.VMEM((LAYERS, T, 256), F32),
            pltpu.SemaphoreType.DMA((4,)),
            pltpu.SemaphoreType.DMA((4,)),
        ],
        cost=(8_000_000_000, 30_000_000),
    )(pos, *left, *right, stream, back)[0]

    got = lax.all_to_all(sent, SECTION, 0, 0, tiled=True)
    pos = jnp.stack([zh, y, c]).astype(jnp.int32)
    half = shape(4, 4, PIECE, 256)
    keep, send = call(
        weight_kernel,
        [half, half],
        [SMEM, VMEM],
        [pltpu.VMEM((2, 4, 4, PIECE, 256), BF16), pltpu.SemaphoreType.DMA((2,))],
        [ANY] * 2,
        cost=(600_000_000, 4_000_000),
    )(pos, got)
    got = other_core(send)
    for axis, first, out in (
        (1, True, (4, 2, PIECE, 256)),
        (1, False, (4, 1, PIECE, 256)),
        (0, True, (2, 1, PIECE, 256)),
        (0, False, (1, 1, PIECE, 256)),
    ):
        keep, send = call(
            functools.partial(add_kernel, axis),
            [shape(*out), shape(*out)],
            [VMEM] * 2,
            [],
            cost=(1_000_000, 4_000_000),
        )(keep, got)
        got = swap(send, "y" if axis == 1 else "zh", first)
    g_scales, g_keys, g_rates, g_bias = call(
        final_kernel,
        [
            shape(2, ROWS, dtype=F32),
            shape(ROWS, 256, dtype=F32),
            shape(ROWS, H, dtype=F32),
            shape(1, H, dtype=F32),
        ],
        [VMEM] * 2,
        [],
        cost=(0, 500_000),
    )(keep[0], got[0])
    return g_scales[None], g_keys[None], g_rates[None], g_bias


def solution(mesh):
    fine = Mesh(mesh.devices.reshape(4, 2, 4, 4, 2), ("x", "zl", "zh", "y", "c"))
    placed = (
        P(None, None, DP, None),
        P(None, None, DP, None),
        P(SECTION, None, DP),
        P(SECTION, DP, None),
        P(SECTION, DP, None),
        P(SECTION, None),
    )
    return jax.shard_map(
        per_device,
        mesh=fine,
        in_specs=placed,
        out_specs=(
            P(SECTION, None, DP),
            P(SECTION, DP, None),
            P(SECTION, DP, None),
            P(SECTION, None),
        ),
        check_vma=False,
    )
```

```python
import jax
import jax.numpy as jnp
from jax import lax
from jax.experimental import pallas as pl
from jax.experimental.pallas import tpu as pltpu
from jax.sharding import Mesh, PartitionSpec as P

F32 = jnp.float32
BF16 = jnp.bfloat16
SECTION = ("x", "zl")
DP = ("zh", "y", "c")

T = 32
D = 3072
C = 128
H = 24
GROUPS = H // 4
W = H * T
LAYERS = 8
SEQS = 6
ROWS = 96
PIECE = 112
TOK = LAYERS * T
BLOCK = 384
BLOCKS = D // BLOCK
SENT = BLOCKS * T + T + 16


def iota(shape, axis):
    return lax.broadcasted_iota(jnp.int32, shape, axis)


def nt(a, b):
    return lax.dot_general(
        a, b, (((1,), (1,)), ((), ())), preferred_element_type=F32
    )


def tn(a, b):
    return lax.dot_general(
        a, b, (((0,), (0,)), ((), ())), preferred_element_type=F32
    )


def nn(a, b):
    return jnp.dot(a, b, preferred_element_type=F32)


def split3(a):
    hi = a.astype(BF16)
    rest = a - hi.astype(F32)
    mid = rest.astype(BF16)
    low = (rest - mid.astype(F32)).astype(BF16)
    return jnp.concatenate([hi, mid, low, jnp.zeros_like(hi)], axis=1)


def masks():
    row = iota((T, W), 0)
    col = iota((T, W), 1) % T
    spread = (iota((C, W), 0) % T == iota((C, W), 1) // T) & (iota((C, W), 0) < 3 * T)
    spread = jnp.where(spread, 1.0, 0.0).astype(BF16)
    block = iota((C, C), 0) // T == iota((C, C), 1) // T
    tri = jnp.where(iota((T, T), 0) >= iota((T, T), 1), 1.0, 0.0).astype(BF16)
    return row >= col, row == col, spread, block, tri


def tile4(a):
    return jnp.concatenate([a] * 4, axis=0)


def stack_heads(a, g):
    return jnp.concatenate([a[:, C * (4 * g + j) : C * (4 * g + j + 1)] for j in range(4)], axis=0)


def unstack_heads(parts):
    return jnp.concatenate([p[T * j : T * (j + 1)] for p in parts for j in range(4)], axis=1)


def block_diag(mixing, g, block):
    return jnp.where(block, tile4(mixing[:, C * g : C * (g + 1)]), 0.0).astype(BF16)


def assemble_rows(piece):
    out = []
    lane = iota((T, C), 1)
    for m in range(8):
        p = []
        for i in range(4):
            z = piece(4 * m + i).astype(F32)
            p.append(jnp.concatenate([z[:, :C], z[:, C:]], axis=0))
        p1 = pltpu.roll(p[1], 96, 1)
        p2 = pltpu.roll(p[2], 64, 1)
        p3 = pltpu.roll(p[3], 32, 1)
        out.append(jnp.where(lane < 96, p[0], p1))
        out.append(jnp.where(lane < 64, p1, p2))
        out.append(jnp.where(lane < 32, p2, p3))
    return jnp.concatenate(out, axis=1)


def cut_rows(rows):
    lane = iota((T, C), 1)
    a, b, c = rows[:, :C], rows[:, C : 2 * C], rows[:, 2 * C :]
    one = jnp.where(lane < 32, pltpu.roll(a, 32, 1), pltpu.roll(b, 32, 1))
    two = jnp.where(lane < 64, pltpu.roll(b, 64, 1), pltpu.roll(c, 64, 1))
    parts = [a, one, two, pltpu.roll(c, 96, 1)]
    return [jnp.concatenate([p[:16], p[16:]], axis=1) for p in parts]


def gray(i):
    return jnp.where(i >= 2, 5 - i, i)


def partner(i, c, first):
    return jnp.where((c == 0) == first, i ^ 1, 3 - i)


def sequence_kernel(pos_ref, *refs):
    left, right = refs[:8], refs[8:16]
    entry_ref, cot_ref, sent_ref = refs[16:19]
    w_scr, rows_scr, xs, ns, mixed_scr, decay_scr, write_scr, small_scr, proj_scr = refs[19:28]
    first_scr, sem_a, sem_b, sem_c = refs[28:]
    x, y, c, zh, section = (pos_ref[i] for i in range(5))
    mine = jnp.minimum(section, SEQS - 1)
    loads = []
    for i, ref in enumerate((entry_ref, cot_ref)):
        copy = pltpu.make_async_copy(
            ref.at[mine // 3, mine % 3], first_scr.at[i], sem_c.at[i]
        )
        copy.start()
        loads.append(copy)

    def ring(i, core):
        one, two = partner(i, core, True), partner(i, core, False)
        return [i, one, two, partner(two, core, True)]

    copies = []
    for kc in range(2):
        cc = (c + kc) % 2
        ys, xx = ring(y, cc), ring(x, cc)
        for i in range(4):
            for j in range(4):
                at = pl.ds(2 * xx[j], 2)
                copy = pltpu.make_async_copy(
                    left[kc * 4 + i].at[j],
                    w_scr.at[at, :, ys[i], cc, :, :C],
                    sem_a.at[xx[j]],
                )
                copy.start()
                at = pl.ds(2 * xx[i], 2)
                copy = pltpu.make_async_copy(
                    right[kc * 4 + i].at[j],
                    w_scr.at[at, :, ys[j], cc, :, C:],
                    sem_b.at[xx[i]],
                )
                copy.start()

    def wait_layers(at):
        for sem, src in ((sem_a, left[0]), (sem_b, right[0])):
            for _ in range(8):
                pltpu.make_async_copy(
                    src.at[0], w_scr.at[0:2, :, 0, 0, :, :C], sem.at[at]
                ).wait()

    causal, diag, spread, block, tri = masks()

    def keys_of(layer, m):
        parts = [w_scr[layer, m // 2, (m % 2) * 2 + i // 2, i % 2, :ROWS] for i in range(4)]
        return jnp.concatenate(parts, axis=0)

    def forward(layer, stream):
        @pl.when(layer % 2 == 0)
        def _():
            wait_layers(layer // 2)

        rows = assemble_rows(lambda d: w_scr[layer, d // 8, d // 2 % 4, d % 2, ROWS:])
        rows_low = rows.astype(BF16)
        rows_scr[layer] = rows_low
        gain, scale, bias = rows[24:25], rows[25:26], rows[26:27, :T]
        xs[layer] = stream
        x_f = stream.astype(F32)
        inv_rms = lax.rsqrt(jnp.sum(x_f * x_f, axis=1, keepdims=True) * (1.0 / D) + 1e-05)
        normed = (x_f * inv_rms * gain).astype(BF16)
        ns[layer] = normed
        for m in range(BLOCKS):
            sent_ref[layer, T * m : T * (m + 1)] = normed[:, BLOCK * m : BLOCK * (m + 1)]
        logits = nt(normed, rows_low) + bias
        key_query = sum(
            nn(normed[:, BLOCK * m : BLOCK * (m + 1)], keys_of(layer, m)) for m in range(BLOCKS)
        )
        head = iota((T, T), 1) < H
        rate = jnp.maximum(logits, 0.0) + jnp.log1p(jnp.exp(-jnp.abs(logits)))
        rate = jnp.where(head, rate, 0.0)
        keep = 1.0 / (1.0 + rate)
        write = rate * keep
        total = nn(tri, split3(-jnp.log1p(rate)))
        total = total[:, :T] + total[:, T : 2 * T] + total[:, 2 * T : 3 * T]
        wide = nn(jnp.concatenate([split3(total), split3(write)], axis=0), spread)
        total_t, write_t = wide[:T], wide[T:]
        total_s = jnp.sum(jnp.where(diag, total_t, 0.0), axis=0, keepdims=True)
        write_s = jnp.sum(jnp.where(diag, write_t, 0.0), axis=0, keepdims=True)
        decay = jnp.where(causal, jnp.exp(jnp.where(causal, total_t - total_s, 0.0)), 0.0)
        k = key_query[:, :C]
        q = key_query[:, C:]
        inv = lax.rsqrt(jnp.sum(k * k, axis=1, keepdims=True) + 1e-06)
        scores = nt(q.astype(BF16), tile4((k * inv).astype(BF16)))
        decay_scr[layer] = decay
        write_scr[layer] = write_s
        proj_scr[layer] = key_query
        small_scr[layer] = jnp.concatenate([scores, logits, keep, jnp.zeros((T, 64), F32)], axis=1)
        mixing = decay * write_s * jnp.concatenate([scores] * GROUPS, axis=1)
        mixed = unstack_heads(
            [nn(block_diag(mixing, g, block), stack_heads(normed, g)) for g in range(GROUPS)]
        )
        mixed_scr[layer] = mixed.astype(BF16)
        return (x_f + scale * mixed).astype(BF16)

    loads[0].wait()
    loads[1].wait()
    lax.fori_loop(0, LAYERS, forward, first_scr[0])

    def backward(step, back):
        layer = LAYERS - 1 - step
        x_f = xs[layer].astype(F32)
        normed = ns[layer]
        rows_low = rows_scr[layer]
        rows = rows_low[16:].astype(F32)
        gain, scale = rows[8:9], rows[9:10]
        dy = back.astype(F32)
        decay = decay_scr[layer]
        write_s = write_scr[layer]
        small = small_scr[layer]
        scores, logits, keep = small[:, :C], small[:, C : C + T], small[:, C + T : C + 2 * T]
        scores6 = jnp.concatenate([scores] * GROUPS, axis=1)
        mixing = decay * write_s * scores6
        d_scale = jnp.sum(dy * mixed_scr[layer].astype(F32), axis=0, keepdims=True)
        d_out = (dy * scale).astype(BF16)
        d_mix = []
        d_values = []
        for g in range(GROUPS):
            grad = stack_heads(d_out, g)
            full = jnp.where(block, nt(grad, stack_heads(normed, g)), 0.0)
            d_mix.append(full[:T] + full[T : 2 * T] + full[2 * T : 3 * T] + full[3 * T :])
            d_values.append(tn(block_diag(mixing, g, block), grad))
        d_mix = jnp.concatenate(d_mix, axis=1)
        d_values = unstack_heads(d_values)
        near = d_mix * decay
        scored = near * scores6
        d_write_s = jnp.sum(scored, axis=0, keepdims=True)
        weighted = near * write_s
        d_scores = sum(weighted[:, C * g : C * (g + 1)] for g in range(GROUPS)).astype(BF16)
        d_total = scored * write_s - jnp.where(diag, d_write_s * write_s, 0.0)
        gathered = []
        for part in (d_total, jnp.where(diag, d_write_s, 0.0)):
            hi = part.astype(BF16)
            gathered += [hi, (part - hi.astype(F32)).astype(BF16)]
        summed = nt(jnp.concatenate(gathered, axis=0), spread[:T])
        d_total = summed[:T] + summed[T : 2 * T]
        d_write = summed[2 * T : 3 * T] + summed[3 * T :]
        d_log = tn(tri, split3(d_total))
        d_log = d_log[:, :T] + d_log[:, T : 2 * T] + d_log[:, 2 * T : 3 * T]
        d_rate = keep * (d_write * keep - d_log)
        d_logits = d_rate / (1.0 + jnp.exp(-logits))
        d_low = jnp.where(iota((T, T), 1) < H, d_logits, 0.0).astype(BF16)
        k = proj_scr[layer][:, :C]
        q = proj_scr[layer][:, C:]
        inv = lax.rsqrt(jnp.sum(k * k, axis=1, keepdims=True) + 1e-06)
        d_q = nn(d_scores, tile4((k * inv).astype(BF16)))
        d_unit = tn(d_scores, q.astype(BF16))
        d_unit = d_unit[:T] + d_unit[T : 2 * T] + d_unit[2 * T : 3 * T] + d_unit[3 * T :]
        d_k = inv * d_unit - k * (inv * inv * inv * jnp.sum(d_unit * k, axis=1, keepdims=True))
        d_keyq = jnp.concatenate([d_k, d_q], axis=1).astype(BF16)
        through = jnp.concatenate([nt(d_keyq, keys_of(layer, m)) for m in range(BLOCKS)], axis=1)
        d_normed = d_values + through + nn(d_low, rows_low)
        inv_rms = lax.rsqrt(jnp.sum(x_f * x_f, axis=1, keepdims=True) * (1.0 / D) + 1e-05)
        x_hat = x_f * inv_rms
        d_gain = jnp.sum(d_normed * x_hat, axis=0, keepdims=True)
        d_hat = d_normed * gain
        mean = jnp.sum(d_hat * x_hat, axis=1, keepdims=True) * (1.0 / D)
        sent_ref[layer, TOK : TOK + T, :256] = d_keyq
        sent_ref[layer, TOK : TOK + T, 256:] = jnp.concatenate(
            [d_low, jnp.zeros((T, 96), BF16)], axis=1
        )
        sent_ref[layer, TOK + T :] = jnp.concatenate(
            [d[:, BLOCK * i : BLOCK * (i + 1)] for d in (d_gain, d_scale) for i in range(8)], axis=0
        ).astype(BF16)
        return (dy + inv_rms * (d_hat - x_hat * mean)).astype(BF16)

    cot = jnp.where(section < SEQS, first_scr[1].astype(F32), 0.0).astype(BF16)
    lax.fori_loop(0, LAYERS, backward, cot)


def weight_kernel(pos_ref, got_ref, keep_ref, send_ref, got, scr, sem_in, sem):
    y, c, zh = pos_ref[1], pos_ref[2], pos_ref[3]
    loads = []
    for m in list(range(BLOCKS)) + [BLOCKS]:
        at = pl.ds(T * m, T if m < BLOCKS else T + 16)
        loads.append(pltpu.make_async_copy(got_ref.at[:, at], got.at[:, at], sem_in.at[m]))
    loads[-1].start()
    for copy in loads[:-1]:
        copy.start()

    def slot(there, here, core):
        bits = gray(jnp.int32(there)) ^ gray(here)
        return bits if core else (bits & 1) * 2 + (bits >> 1)

    loads[-1].wait()
    tokens = jnp.concatenate([got[s, TOK : TOK + T] for s in range(LAYERS)], axis=0)
    extra = sum(got[s, TOK + T :].astype(F32) for s in range(LAYERS))
    bias = jnp.sum(tokens[:, 256:].astype(F32), axis=0, keepdims=True)
    bias = jnp.concatenate([bias[:, :ROWS]] * 4, axis=1)
    for m in range(BLOCKS):
        loads[m].wait()
        normed = jnp.concatenate([got[s, T * m : T * (m + 1)] for s in range(LAYERS)], axis=0)
        keys = tn(normed, tokens[:, :256])
        rates = tn(tokens[:, 256:], normed)[:H]
        rows = jnp.concatenate(
            [rates, extra[m : m + 1], extra[m + 8 : m + 9], bias, jnp.zeros((5, BLOCK), F32)],
            axis=0,
        )
        low = cut_rows(rows)
        for i in range(4):
            d = 4 * m + i
            y_at, z_at = slot(d // 2 % 4, y, d % 2), slot(d // 8, zh, d % 2)
            c_at = (d + c) % 2
            scr[c_at, y_at, z_at, :ROWS] = keys[ROWS * i : ROWS * (i + 1)].astype(BF16)
            scr[c_at, y_at, z_at, ROWS:] = low[i].astype(BF16)
    for i, ref in enumerate((keep_ref, send_ref)):
        pltpu.make_async_copy(scr.at[i], ref, sem.at[i]).start()
    for i, ref in enumerate((keep_ref, send_ref)):
        pltpu.make_async_copy(scr.at[i], ref, sem.at[i]).wait()


def final_kernel(a_ref, b_ref, c_ref, d_ref, scales_ref, keys_ref, rates_ref, bias_ref):
    total = a_ref[...].astype(F32) + b_ref[...].astype(F32)
    total = total + c_ref[...].astype(F32) + d_ref[...].astype(F32)
    keys_ref[...] = total[:ROWS]
    rates = jnp.concatenate([total[ROWS:, :C], total[ROWS:, C:]], axis=0)
    rates_ref[...] = rates[:H, :ROWS]
    scales_ref[...] = rates[24:26, :ROWS]
    bias_ref[...] = rates[26:27, :H]


ANY = pl.BlockSpec(memory_space=pl.ANY)
VMEM = pl.BlockSpec(memory_space=pltpu.VMEM)
SMEM = pl.BlockSpec(memory_space=pltpu.SMEM)
PARAMS = pltpu.CompilerParams(vmem_limit_bytes=56 * 1024 * 1024)


def shape(*dims, dtype=BF16):
    return jax.ShapeDtypeStruct(dims, dtype)


def call(kernel, outs, ins, scratch, out_spec=None, cost=None):
    flops, moved = cost
    return pl.pallas_call(
        kernel,
        out_shape=outs,
        in_specs=ins,
        out_specs=out_spec or [VMEM] * len(outs),
        scratch_shapes=scratch,
        compiler_params=PARAMS,
        cost_estimate=pl.CostEstimate(flops=flops, bytes_accessed=moved, transcendentals=0),
    )


def ring_pairs(first):
    pairs = []
    for i in range(4):
        for c in range(2):
            to = i ^ 1 if (c == 0) == first else 3 - i
            pairs.append((i * 2 + c, to * 2 + c))
    return pairs


def swap(array, axis, first):
    return lax.ppermute(array, (axis, "c"), ring_pairs(first))


def other_core(array):
    return lax.ppermute(array, "c", [(0, 1), (1, 0)])


def opposite(array, axis):
    return lax.ppermute(array, axis, [(i, i ^ 2) for i in range(4)])


def gather_ring(array, axis, direct=False):
    one = swap(array, axis, True)
    two = swap(array, axis, False)
    return [array, one, two, opposite(array, axis) if direct else swap(one, axis, False)]


def add(a, b):
    return (a.astype(F32) + b.astype(F32)).astype(BF16)


def per_device(entries, cotangents, scales, key_weight, rate_weight, rate_bias):
    x, zl, zh, y, c = (lax.axis_index(a) for a in ("x", "zl", "zh", "y", "c"))
    section = x * 2 + zl
    pos = jnp.stack([x, y, c, zh, section]).astype(jnp.int32)

    wide = jnp.pad(rate_weight[0].T, ((0, 0), (0, C - ROWS)))
    small = jnp.pad(scales[0], ((0, 0), (0, C - ROWS)))
    line = jnp.pad(rate_bias, ((0, 0), (0, C - H)))
    right = jnp.concatenate([wide[16:], small, line, jnp.zeros((5, C), BF16)], axis=0)
    packed = jnp.concatenate(
        [key_weight[0], jnp.concatenate([wide[:16], right], axis=1)], axis=0
    )

    along = jnp.stack(gather_ring(packed, "zh", direct=True))
    first, second = partner(zh, c, True), partner(zh, c, False)
    across = partner(second, c, True)
    order = [jnp.where(j == first, 1, jnp.where(j == second, 2, jnp.where(j == across, 3, 0))) for j in range(4)]
    along = jnp.take(along, jnp.stack(order), axis=0)
    pairs = []
    for z in range(8):
        for core in range(2):
            to = z ^ 1 if core == 0 else (z + 1 if z % 2 else z - 1) % 8
            pairs.append(tuple(((i % 2) * 4 + i // 2) * 2 + core for i in (z, to)))
    other = lax.ppermute(along, ("zl", "zh", "c"), pairs)
    both = jnp.where(zl == 0, jnp.stack([along, other]), jnp.stack([other, along]))

    left = jnp.stack(gather_ring(both[..., :C], "x"))
    right = jnp.stack(gather_ring(both[..., C:], "y"))
    left = gather_ring(left, "y")
    right = gather_ring(right, "x")
    left = left + [other_core(a) for a in left]
    right = right + [other_core(a) for a in right]

    sent = call(
        sequence_kernel,
        [shape(LAYERS, SENT, BLOCK)],
        [SMEM] + [ANY] * 18,
        [
            pltpu.VMEM((LAYERS, 4, 4, 2, PIECE, 256), BF16),
            pltpu.VMEM((LAYERS, T, D), BF16),
            pltpu.VMEM((LAYERS, T, D), BF16),
            pltpu.VMEM((LAYERS, T, D), BF16),
            pltpu.VMEM((LAYERS, T, D), BF16),
            pltpu.VMEM((LAYERS, T, W), F32),
            pltpu.VMEM((LAYERS, 1, W), F32),
            pltpu.VMEM((LAYERS, T, 256), F32),
            pltpu.VMEM((LAYERS, T, 256), F32),
            pltpu.VMEM((2, T, D), BF16),
            pltpu.SemaphoreType.DMA((4,)),
            pltpu.SemaphoreType.DMA((4,)),
            pltpu.SemaphoreType.DMA((2,)),
        ],
        cost=(8_000_000_000, 30_000_000),
    )(pos, *left, *right, entries, cotangents)[0]

    got = lax.all_to_all(sent, SECTION, 0, 0, tiled=True)
    half = shape(4, 4, PIECE, 256)
    keep, send = call(
        weight_kernel,
        [half, half],
        [SMEM, ANY],
        [
            pltpu.VMEM((LAYERS, SENT, BLOCK), BF16),
            pltpu.VMEM((2, 4, 4, PIECE, 256), BF16),
            pltpu.SemaphoreType.DMA((BLOCKS + 1,)),
            pltpu.SemaphoreType.DMA((2,)),
        ],
        [ANY] * 2,
        cost=(600_000_000, 4_000_000),
    )(pos, got)
    got = other_core(send)
    got = swap(add(keep[2:], got[2:]), "y", True), keep[:2], got[:2]
    keep = add(got[1], got[2])
    got = got[0]
    got, keep = swap(add(keep[1], got[1]), "y", False), add(keep[0], got[0])
    got = add(keep, got)
    parts = [
        got[0],
        swap(got[2], "zh", True),
        swap(got[1], "zh", False),
        opposite(got[3], "zh"),
    ]
    g_scales, g_keys, g_rates, g_bias = call(
        final_kernel,
        [
            shape(2, ROWS, dtype=F32),
            shape(ROWS, 256, dtype=F32),
            shape(H, ROWS, dtype=F32),
            shape(1, H, dtype=F32),
        ],
        [VMEM] * 4,
        [],
        cost=(0, 500_000),
    )(*parts)
    return g_scales[None], g_keys[None], g_rates.T[None], g_bias


def solution(mesh):
    fine = Mesh(mesh.devices.reshape(4, 2, 4, 4, 2), ("x", "zl", "zh", "y", "c"))
    placed = (
        P(None, None, DP, None),
        P(None, None, DP, None),
        P(SECTION, None, DP),
        P(SECTION, DP, None),
        P(SECTION, DP, None),
        P(SECTION, None),
    )
    return jax.shard_map(
        per_device,
        mesh=fine,
        in_specs=placed,
        out_specs=(
            P(SECTION, None, DP),
            P(SECTION, DP, None),
            P(SECTION, DP, None),
            P(SECTION, None),
        ),
        check_vma=False,
    )
```

```python
import jax
import jax.numpy as jnp
from jax import lax
from jax.experimental import pallas as pl
from jax.experimental.pallas import tpu as pltpu
from jax.sharding import Mesh, PartitionSpec as P

F32 = jnp.float32
BF16 = jnp.bfloat16
SECTION = ("x", "zl")
DP = ("zh", "y", "c")

T = 32
D = 3072
C = 128
H = 24
GROUPS = H // 4
W = H * T
LAYERS = 8
SEQS = 6
ROWS = 96
PIECE = 112
TOK = LAYERS * T
BLOCK = 384
BLOCKS = D // BLOCK
PAY = T + 16


def iota(shape, axis):
    return lax.broadcasted_iota(jnp.int32, shape, axis)


def nt(a, b):
    return lax.dot_general(
        a, b, (((1,), (1,)), ((), ())), preferred_element_type=F32
    )


def tn(a, b):
    return lax.dot_general(
        a, b, (((0,), (0,)), ((), ())), preferred_element_type=F32
    )


def nn(a, b):
    return jnp.dot(a, b, preferred_element_type=F32)


def split3(a):
    hi = a.astype(BF16)
    rest = a - hi.astype(F32)
    mid = rest.astype(BF16)
    low = (rest - mid.astype(F32)).astype(BF16)
    return jnp.concatenate([hi, mid, low, jnp.zeros_like(hi)], axis=1)


def masks():
    row = iota((T, W), 0)
    col = iota((T, W), 1) % T
    spread = (iota((C, W), 0) % T == iota((C, W), 1) // T) & (iota((C, W), 0) < 3 * T)
    spread = jnp.where(spread, 1.0, 0.0).astype(BF16)
    block = iota((C, C), 0) // T == iota((C, C), 1) // T
    tri = jnp.where(iota((T, T), 0) >= iota((T, T), 1), 1.0, 0.0).astype(BF16)
    return row >= col, row == col, spread, block, tri


def tile4(a):
    return jnp.concatenate([a] * 4, axis=0)


def stack_heads(a, g):
    return jnp.concatenate([a[:, C * (4 * g + j) : C * (4 * g + j + 1)] for j in range(4)], axis=0)


def unstack_heads(parts):
    return jnp.concatenate([p[T * j : T * (j + 1)] for p in parts for j in range(4)], axis=1)


def block_diag(mixing, g, block):
    return jnp.where(block, tile4(mixing[:, C * g : C * (g + 1)]), 0.0).astype(BF16)


def assemble_rows(piece):
    out = []
    lane = iota((T, C), 1)
    for m in range(8):
        p = []
        for i in range(4):
            z = piece(4 * m + i).astype(F32)
            p.append(jnp.concatenate([z[:, :C], z[:, C:]], axis=0))
        p1 = pltpu.roll(p[1], 96, 1)
        p2 = pltpu.roll(p[2], 64, 1)
        p3 = pltpu.roll(p[3], 32, 1)
        out.append(jnp.where(lane < 96, p[0], p1))
        out.append(jnp.where(lane < 64, p1, p2))
        out.append(jnp.where(lane < 32, p2, p3))
    return jnp.concatenate(out, axis=1)


def cut_rows(rows):
    lane = iota((T, C), 1)
    a, b, c = rows[:, :C], rows[:, C : 2 * C], rows[:, 2 * C :]
    one = jnp.where(lane < 32, pltpu.roll(a, 32, 1), pltpu.roll(b, 32, 1))
    two = jnp.where(lane < 64, pltpu.roll(b, 64, 1), pltpu.roll(c, 64, 1))
    parts = [a, one, two, pltpu.roll(c, 96, 1)]
    return [jnp.concatenate([p[:16], p[16:]], axis=1) for p in parts]


def gray(i):
    return jnp.where(i >= 2, 5 - i, i)


def partner(i, c, first):
    return jnp.where((c == 0) == first, i ^ 1, 3 - i)


def load_weights(pos_ref, left, right, w_scr, sem_a, sem_b):
    x, y, c = pos_ref[0], pos_ref[1], pos_ref[2]

    def ring(i, core):
        one, two = partner(i, core, True), partner(i, core, False)
        return [i, one, two, partner(two, core, True)]

    for kc in range(2):
        cc = (c + kc) % 2
        ys, xx = ring(y, cc), ring(x, cc)
        for i in range(4):
            for j in range(4):
                at = pl.ds(2 * xx[j], 2)
                copy = pltpu.make_async_copy(
                    left[kc * 4 + i].at[j],
                    w_scr.at[at, :, ys[i], cc, :, :C],
                    sem_a.at[xx[j]],
                )
                copy.start()
                at = pl.ds(2 * xx[i], 2)
                copy = pltpu.make_async_copy(
                    right[kc * 4 + i].at[j],
                    w_scr.at[at, :, ys[j], cc, :, C:],
                    sem_b.at[xx[i]],
                )
                copy.start()

    def wait_layers(at):
        for sem, src in ((sem_a, left[0]), (sem_b, right[0])):
            for _ in range(8):
                pltpu.make_async_copy(
                    src.at[0], w_scr.at[0:2, :, 0, 0, :, :C], sem.at[at]
                ).wait()

    return wait_layers


def keys_of(w_scr, layer, m):
    parts = [w_scr[layer, m // 2, (m % 2) * 2 + i // 2, i % 2, :ROWS] for i in range(4)]
    return jnp.concatenate(parts, axis=0)


def forward_kernel(pos_ref, *refs):
    left, right, entry_ref, sent_ref, kept = refs[:8], refs[8:16], refs[16], refs[17], refs[18:22]
    w_scr, first_scr = refs[22:24]
    scrs, (sem_a, sem_b, sem_c, sem_k) = refs[24:28], refs[28:]
    rows_scr, xs, mixed_scr, wide_scr = scrs
    mine = jnp.minimum(pos_ref[4], SEQS - 1)
    first = pltpu.make_async_copy(entry_ref.at[mine // 3, mine % 3], first_scr, sem_c)
    first.start()
    wait_layers = load_weights(pos_ref, left, right, w_scr, sem_a, sem_b)
    causal, diag, spread, block, tri = masks()

    def forward(layer, stream):
        @pl.when(layer % 2 == 0)
        def _():
            wait_layers(layer // 2)

        rows = assemble_rows(lambda d: w_scr[layer, d // 8, d // 2 % 4, d % 2, ROWS:])
        rows_low = rows.astype(BF16)
        rows_scr[layer] = rows_low
        gain, scale, bias = rows[24:25], rows[25:26], rows[26:27, :T]
        xs[layer] = stream
        x_f = stream.astype(F32)
        inv_rms = lax.rsqrt(jnp.sum(x_f * x_f, axis=1, keepdims=True) * (1.0 / D) + 1e-05)
        normed = (x_f * inv_rms * gain).astype(BF16)
        for m in range(BLOCKS):
            sent_ref[layer, T * m : T * (m + 1)] = normed[:, BLOCK * m : BLOCK * (m + 1)]
        logits = nt(normed, rows_low) + bias
        key_query = sum(
            nn(normed[:, BLOCK * m : BLOCK * (m + 1)], keys_of(w_scr, layer, m)) for m in range(BLOCKS)
        )
        head = iota((T, T), 1) < H
        rate = jnp.maximum(logits, 0.0) + jnp.log1p(jnp.exp(-jnp.abs(logits)))
        rate = jnp.where(head, rate, 0.0)
        keep = 1.0 / (1.0 + rate)
        write = rate * keep
        total = nn(tri, split3(-jnp.log1p(rate)))
        total = total[:, :T] + total[:, T : 2 * T] + total[:, 2 * T : 3 * T]
        wide = nn(jnp.concatenate([split3(total), split3(write)], axis=0), spread)
        total_t, write_t = wide[:T], wide[T:]
        total_s = jnp.sum(jnp.where(diag, total_t, 0.0), axis=0, keepdims=True)
        write_s = jnp.sum(jnp.where(diag, write_t, 0.0), axis=0, keepdims=True)
        decay = jnp.where(causal, jnp.exp(jnp.where(causal, total_t - total_s, 0.0)), 0.0)
        k = key_query[:, :C]
        q = key_query[:, C:]
        inv = lax.rsqrt(jnp.sum(k * k, axis=1, keepdims=True) + 1e-06)
        scores = nt(q.astype(BF16), tile4((k * inv).astype(BF16)))
        wide_scr[layer, :T, :W] = decay
        wide_scr[layer, T:, :W] = jnp.broadcast_to(write_s, (8, W))
        wide_scr[layer, :T, W : W + 256] = key_query
        wide_scr[layer, :T, W + 256 :] = jnp.concatenate(
            [scores, logits, keep, jnp.zeros((T, 64), F32)], axis=1
        )
        mixing = decay * write_s * jnp.concatenate([scores] * GROUPS, axis=1)
        mixed = unstack_heads(
            [nn(block_diag(mixing, g, block), stack_heads(normed, g)) for g in range(GROUPS)]
        )
        mixed_scr[layer] = mixed.astype(BF16)
        for i in range(4):
            pltpu.make_async_copy(scrs[i].at[layer], kept[i].at[layer], sem_k.at[i]).start()
        return (x_f + scale * mixed).astype(BF16)

    first.wait()
    lax.fori_loop(0, LAYERS, forward, first_scr[...])
    for i in range(4):
        pltpu.make_async_copy(scrs[i], kept[i], sem_k.at[i]).wait()


def backward_kernel(pos_ref, *refs):
    left, right, cot_ref, kept, sent_ref = refs[:8], refs[8:16], refs[16], refs[17:22], refs[22]
    w_scr, first_scr = refs[23:25]
    scrs, (sem_a, sem_b, sem_c, sem_k) = refs[25:30], refs[30:]
    rows_scr, xs, mixed_scr, wide_scr, n_scr = scrs
    mine = jnp.minimum(pos_ref[4], SEQS - 1)
    first = pltpu.make_async_copy(cot_ref.at[mine // 3, mine % 3], first_scr, sem_c)
    first.start()

    def load(layer, start):
        for i in range(5):
            copy = pltpu.make_async_copy(kept[i].at[layer], scrs[i].at[layer], sem_k.at[layer])
            if start:
                copy.start()
            else:
                copy.wait()

    load(LAYERS - 1, True)
    wait_layers = load_weights(pos_ref, left, right, w_scr, sem_a, sem_b)
    for layer in reversed(range(LAYERS - 1)):
        load(layer, True)
    causal, diag, spread, block, tri = masks()

    def backward(step, back):
        layer = LAYERS - 1 - step
        load(layer, False)
        x_f = xs[layer].astype(F32)
        normed = jnp.concatenate([n_scr[layer, T * m : T * (m + 1)] for m in range(BLOCKS)], axis=1)
        rows_low = rows_scr[layer]
        rows = rows_low[16:].astype(F32)
        gain, scale = rows[8:9], rows[9:10]
        dy = back.astype(F32)
        decay = wide_scr[layer, :T, :W]
        write_s = wide_scr[layer, T : T + 1, :W]
        small = wide_scr[layer, :T, W + 256 :]
        scores, logits, keep = small[:, :C], small[:, C : C + T], small[:, C + T : C + 2 * T]
        scores6 = jnp.concatenate([scores] * GROUPS, axis=1)
        mixing = decay * write_s * scores6
        d_scale = jnp.sum(dy * mixed_scr[layer].astype(F32), axis=0, keepdims=True)
        d_out = (dy * scale).astype(BF16)
        d_mix = []
        d_values = []
        for g in range(GROUPS):
            grad = stack_heads(d_out, g)
            full = jnp.where(block, nt(grad, stack_heads(normed, g)), 0.0)
            d_mix.append(full[:T] + full[T : 2 * T] + full[2 * T : 3 * T] + full[3 * T :])
            d_values.append(tn(block_diag(mixing, g, block), grad))
        d_mix = jnp.concatenate(d_mix, axis=1)
        d_values = unstack_heads(d_values)
        near = d_mix * decay
        scored = near * scores6
        d_write_s = jnp.sum(scored, axis=0, keepdims=True)
        weighted = near * write_s
        d_scores = sum(weighted[:, C * g : C * (g + 1)] for g in range(GROUPS)).astype(BF16)
        d_total = scored * write_s - jnp.where(diag, d_write_s * write_s, 0.0)
        gathered = []
        for part in (d_total, jnp.where(diag, d_write_s, 0.0)):
            hi = part.astype(BF16)
            gathered += [hi, (part - hi.astype(F32)).astype(BF16)]
        summed = nt(jnp.concatenate(gathered, axis=0), spread[:T])
        d_total = summed[:T] + summed[T : 2 * T]
        d_write = summed[2 * T : 3 * T] + summed[3 * T :]
        d_log = tn(tri, split3(d_total))
        d_log = d_log[:, :T] + d_log[:, T : 2 * T] + d_log[:, 2 * T : 3 * T]
        d_rate = keep * (d_write * keep - d_log)
        d_logits = d_rate / (1.0 + jnp.exp(-logits))
        d_low = jnp.where(iota((T, T), 1) < H, d_logits, 0.0).astype(BF16)
        k = wide_scr[layer, :T, W : W + C]
        q = wide_scr[layer, :T, W + C : W + 256]
        inv = lax.rsqrt(jnp.sum(k * k, axis=1, keepdims=True) + 1e-06)
        d_q = nn(d_scores, tile4((k * inv).astype(BF16)))
        d_unit = tn(d_scores, q.astype(BF16))
        d_unit = d_unit[:T] + d_unit[T : 2 * T] + d_unit[2 * T : 3 * T] + d_unit[3 * T :]
        d_k = inv * d_unit - k * (inv * inv * inv * jnp.sum(d_unit * k, axis=1, keepdims=True))
        d_keyq = jnp.concatenate([d_k, d_q], axis=1).astype(BF16)

        @pl.when(layer % 2 == 1)
        def _():
            wait_layers(layer // 2)

        through = jnp.concatenate([nt(d_keyq, keys_of(w_scr, layer, m)) for m in range(BLOCKS)], axis=1)
        d_normed = d_values + through + nn(d_low, rows_low)
        inv_rms = lax.rsqrt(jnp.sum(x_f * x_f, axis=1, keepdims=True) * (1.0 / D) + 1e-05)
        x_hat = x_f * inv_rms
        d_gain = jnp.sum(d_normed * x_hat, axis=0, keepdims=True)
        d_hat = d_normed * gain
        mean = jnp.sum(d_hat * x_hat, axis=1, keepdims=True) * (1.0 / D)
        sent_ref[layer, :T, :256] = d_keyq
        sent_ref[layer, :T, 256:] = jnp.concatenate(
            [d_low, jnp.zeros((T, 96), BF16)], axis=1
        )
        sent_ref[layer, T:] = jnp.concatenate(
            [d[:, BLOCK * i : BLOCK * (i + 1)] for d in (d_gain, d_scale) for i in range(8)], axis=0
        ).astype(BF16)
        return (dy + inv_rms * (d_hat - x_hat * mean)).astype(BF16)

    first.wait()
    cot = jnp.where(pos_ref[4] < SEQS, first_scr[...].astype(F32), 0.0).astype(BF16)
    lax.fori_loop(0, LAYERS, backward, cot)


def weight_kernel(pos_ref, got_ref, pay_ref, keep_ref, send_ref, got, pay, scr, sem_in, sem):
    y, c, zh = pos_ref[1], pos_ref[2], pos_ref[3]
    loads = []
    for m in range(BLOCKS):
        at = pl.ds(T * m, T)
        loads.append(pltpu.make_async_copy(got_ref.at[:, at], got.at[:, at], sem_in.at[m]))
    loads.append(pltpu.make_async_copy(pay_ref, pay, sem_in.at[BLOCKS]))
    loads[-1].start()
    for copy in loads[:-1]:
        copy.start()

    def slot(there, here, core):
        bits = gray(jnp.int32(there)) ^ gray(here)
        return bits if core else (bits & 1) * 2 + (bits >> 1)

    loads[-1].wait()
    tokens = jnp.concatenate([pay[s, :T] for s in range(LAYERS)], axis=0)
    extra = sum(pay[s, T:].astype(F32) for s in range(LAYERS))
    bias = jnp.sum(tokens[:, 256:].astype(F32), axis=0, keepdims=True)
    bias = jnp.concatenate([bias[:, :ROWS]] * 4, axis=1)
    for m in range(BLOCKS):
        loads[m].wait()
        normed = jnp.concatenate([got[s, T * m : T * (m + 1)] for s in range(LAYERS)], axis=0)
        keys = tn(normed, tokens[:, :256])
        rates = tn(tokens[:, 256:], normed)[:H]
        rows = jnp.concatenate(
            [rates, extra[m : m + 1], extra[m + 8 : m + 9], bias, jnp.zeros((5, BLOCK), F32)],
            axis=0,
        )
        low = cut_rows(rows)
        for i in range(4):
            d = 4 * m + i
            y_at, z_at = slot(d // 2 % 4, y, d % 2), slot(d // 8, zh, d % 2)
            c_at = (d + c) % 2
            scr[c_at, y_at, z_at, :ROWS] = keys[ROWS * i : ROWS * (i + 1)].astype(BF16)
            scr[c_at, y_at, z_at, ROWS:] = low[i].astype(BF16)
    for i, ref in enumerate((keep_ref, send_ref)):
        pltpu.make_async_copy(scr.at[i], ref, sem.at[i]).start()
    for i, ref in enumerate((keep_ref, send_ref)):
        pltpu.make_async_copy(scr.at[i], ref, sem.at[i]).wait()


def final_kernel(a_ref, b_ref, c_ref, d_ref, scales_ref, keys_ref, rates_ref, bias_ref):
    total = a_ref[...].astype(F32) + b_ref[...].astype(F32)
    total = total + c_ref[...].astype(F32) + d_ref[...].astype(F32)
    keys_ref[...] = total[:ROWS]
    rates = jnp.concatenate([total[ROWS:, :C], total[ROWS:, C:]], axis=0)
    rates_ref[...] = rates[:H, :ROWS]
    scales_ref[...] = rates[24:26, :ROWS]
    bias_ref[...] = rates[26:27, :H]


ANY = pl.BlockSpec(memory_space=pl.ANY)
VMEM = pl.BlockSpec(memory_space=pltpu.VMEM)
SMEM = pl.BlockSpec(memory_space=pltpu.SMEM)
PARAMS = pltpu.CompilerParams(vmem_limit_bytes=56 * 1024 * 1024)


def shape(*dims, dtype=BF16):
    return jax.ShapeDtypeStruct(dims, dtype)


def call(kernel, outs, ins, scratch, out_spec=None, cost=None):
    flops, moved = cost
    return pl.pallas_call(
        kernel,
        out_shape=outs,
        in_specs=ins,
        out_specs=out_spec or [VMEM] * len(outs),
        scratch_shapes=scratch,
        compiler_params=PARAMS,
        cost_estimate=pl.CostEstimate(flops=flops, bytes_accessed=moved, transcendentals=0),
    )


def ring_pairs(first):
    pairs = []
    for i in range(4):
        for c in range(2):
            to = i ^ 1 if (c == 0) == first else 3 - i
            pairs.append((i * 2 + c, to * 2 + c))
    return pairs


def swap(array, axis, first):
    return lax.ppermute(array, (axis, "c"), ring_pairs(first))


def other_core(array):
    return lax.ppermute(array, "c", [(0, 1), (1, 0)])


def opposite(array, axis):
    return lax.ppermute(array, axis, [(i, i ^ 2) for i in range(4)])


def gather_ring(array, axis, direct=False):
    one = swap(array, axis, True)
    two = swap(array, axis, False)
    return [array, one, two, opposite(array, axis) if direct else swap(one, axis, False)]


def add(a, b):
    return (a.astype(F32) + b.astype(F32)).astype(BF16)


def per_device(entries, cotangents, scales, key_weight, rate_weight, rate_bias):
    x, zl, zh, y, c = (lax.axis_index(a) for a in ("x", "zl", "zh", "y", "c"))
    section = x * 2 + zl
    pos = jnp.stack([x, y, c, zh, section]).astype(jnp.int32)

    wide = jnp.pad(rate_weight[0].T, ((0, 0), (0, C - ROWS)))
    small = jnp.pad(scales[0], ((0, 0), (0, C - ROWS)))
    line = jnp.pad(rate_bias, ((0, 0), (0, C - H)))
    right = jnp.concatenate([wide[16:], small, line, jnp.zeros((5, C), BF16)], axis=0)
    packed = jnp.concatenate(
        [key_weight[0], jnp.concatenate([wide[:16], right], axis=1)], axis=0
    )

    along = jnp.stack(gather_ring(packed, "zh", direct=True))
    first, second = partner(zh, c, True), partner(zh, c, False)
    across = partner(second, c, True)
    order = [jnp.where(j == first, 1, jnp.where(j == second, 2, jnp.where(j == across, 3, 0))) for j in range(4)]
    along = jnp.take(along, jnp.stack(order), axis=0)
    pairs = []
    for z in range(8):
        for core in range(2):
            to = z ^ 1 if core == 0 else (z + 1 if z % 2 else z - 1) % 8
            pairs.append(tuple(((i % 2) * 4 + i // 2) * 2 + core for i in (z, to)))
    other = lax.ppermute(along, ("zl", "zh", "c"), pairs)
    both = jnp.where(zl == 0, jnp.stack([along, other]), jnp.stack([other, along]))

    left = jnp.stack(gather_ring(both[..., :C], "x"))
    right = jnp.stack(gather_ring(both[..., C:], "y"))
    left = gather_ring(left, "y")
    right = gather_ring(right, "x")
    left = left + [other_core(a) for a in left]
    right = right + [other_core(a) for a in right]

    wide = shape(LAYERS, T + 8, W + 512, dtype=F32)
    stored = shape(LAYERS, T, D)
    normed = shape(LAYERS, TOK, BLOCK)
    held = [
        pltpu.VMEM((LAYERS, 4, 4, 2, PIECE, 256), BF16),
        pltpu.VMEM((T, D), BF16),
        pltpu.VMEM(stored.shape, BF16),
        pltpu.VMEM(stored.shape, BF16),
        pltpu.VMEM(stored.shape, BF16),
        pltpu.VMEM(wide.shape, F32),
    ]
    sems = [pltpu.SemaphoreType.DMA((4,)), pltpu.SemaphoreType.DMA((4,)), pltpu.SemaphoreType.DMA]
    normed, *kept = call(
        forward_kernel,
        [normed, stored, stored, stored, wide],
        [SMEM] + [ANY] * 17,
        held + sems + [pltpu.SemaphoreType.DMA((4,))],
        [VMEM] + [ANY] * 4,
        cost=(3_000_000_000, 30_000_000),
    )(pos, *left, *right, entries)
    got = lax.all_to_all(normed, SECTION, 0, 0, tiled=True)
    pay = call(
        backward_kernel,
        [shape(LAYERS, PAY, BLOCK)],
        [SMEM] + [ANY] * 22,
        held + [pltpu.VMEM((LAYERS, TOK, BLOCK), BF16)] + sems + [pltpu.SemaphoreType.DMA((LAYERS,))],
        cost=(8_000_000_000, 40_000_000),
    )(pos, *left, *right, cotangents, *kept, normed)[0]
    pay = lax.all_to_all(pay, SECTION, 0, 0, tiled=True)
    half = shape(4, 4, PIECE, 256)
    keep, send = call(
        weight_kernel,
        [half, half],
        [SMEM, ANY, ANY],
        [
            pltpu.VMEM((LAYERS, TOK, BLOCK), BF16),
            pltpu.VMEM((LAYERS, PAY, BLOCK), BF16),
            pltpu.VMEM((2, 4, 4, PIECE, 256), BF16),
            pltpu.SemaphoreType.DMA((BLOCKS + 1,)),
            pltpu.SemaphoreType.DMA((2,)),
        ],
        [ANY] * 2,
        cost=(600_000_000, 4_000_000),
    )(pos, got, pay)
    got = other_core(send)
    got = swap(add(keep[2:], got[2:]), "y", True), keep[:2], got[:2]
    keep = add(got[1], got[2])
    got = got[0]
    got, keep = swap(add(keep[1], got[1]), "y", False), add(keep[0], got[0])
    got = add(keep, got)
    parts = [
        got[0],
        swap(got[2], "zh", True),
        swap(got[1], "zh", False),
        opposite(got[3], "zh"),
    ]
    g_scales, g_keys, g_rates, g_bias = call(
        final_kernel,
        [
            shape(2, ROWS, dtype=F32),
            shape(ROWS, 256, dtype=F32),
            shape(H, ROWS, dtype=F32),
            shape(1, H, dtype=F32),
        ],
        [VMEM] * 4,
        [],
        cost=(0, 500_000),
    )(*parts)
    return g_scales[None], g_keys[None], g_rates.T[None], g_bias


def solution(mesh):
    fine = Mesh(mesh.devices.reshape(4, 2, 4, 4, 2), ("x", "zl", "zh", "y", "c"))
    placed = (
        P(None, None, DP, None),
        P(None, None, DP, None),
        P(SECTION, None, DP),
        P(SECTION, DP, None),
        P(SECTION, DP, None),
        P(SECTION, None),
    )
    return jax.shard_map(
        per_device,
        mesh=fine,
        in_specs=placed,
        out_specs=(
            P(SECTION, None, DP),
            P(SECTION, DP, None),
            P(SECTION, DP, None),
            P(SECTION, None),
        ),
        check_vma=False,
    )
```

```python
import jax
import jax.numpy as jnp
from jax import lax
from jax.experimental import pallas as pl
from jax.experimental.pallas import tpu as pltpu
from jax.sharding import Mesh, PartitionSpec as P

F32 = jnp.float32
BF16 = jnp.bfloat16
SECTION = ("x", "zl")
DP = ("zh", "y", "c")

T = 32
D = 3072
C = 128
H = 24
GROUPS = H // 4
W = H * T
LAYERS = 8
SEQS = 6
ROWS = 96
PIECE = 112
TOK = LAYERS * T
BLOCK = 384
BLOCKS = D // BLOCK
SENT = BLOCKS * T + T + 16


def iota(shape, axis):
    return lax.broadcasted_iota(jnp.int32, shape, axis)


def nt(a, b):
    return lax.dot_general(
        a, b, (((1,), (1,)), ((), ())), preferred_element_type=F32
    )


def tn(a, b):
    return lax.dot_general(
        a, b, (((0,), (0,)), ((), ())), preferred_element_type=F32
    )


def nn(a, b):
    return jnp.dot(a, b, preferred_element_type=F32)


def split3(a):
    hi = a.astype(BF16)
    rest = a - hi.astype(F32)
    mid = rest.astype(BF16)
    low = (rest - mid.astype(F32)).astype(BF16)
    return jnp.concatenate([hi, mid, low, jnp.zeros_like(hi)], axis=1)


def masks():
    row = iota((T, W), 0)
    col = iota((T, W), 1) % T
    spread = (iota((C, W), 0) % T == iota((C, W), 1) // T) & (iota((C, W), 0) < 3 * T)
    spread = jnp.where(spread, 1.0, 0.0).astype(BF16)
    block = iota((C, C), 0) // T == iota((C, C), 1) // T
    tri = jnp.where(iota((T, T), 0) >= iota((T, T), 1), 1.0, 0.0).astype(BF16)
    return row >= col, row == col, spread, block, tri


def tile4(a):
    return jnp.concatenate([a] * 4, axis=0)


def stack_heads(a, g):
    return jnp.concatenate([a[:, C * (4 * g + j) : C * (4 * g + j + 1)] for j in range(4)], axis=0)


def unstack_heads(parts):
    return jnp.concatenate([p[T * j : T * (j + 1)] for p in parts for j in range(4)], axis=1)


def block_diag(mixing, g, block):
    return jnp.where(block, tile4(mixing[:, C * g : C * (g + 1)]), 0.0).astype(BF16)


def assemble_rows(piece):
    out = []
    lane = iota((T, C), 1)
    for m in range(8):
        p = []
        for i in range(4):
            z = piece(4 * m + i).astype(F32)
            p.append(jnp.concatenate([z[:, :C], z[:, C:]], axis=0))
        p1 = pltpu.roll(p[1], 96, 1)
        p2 = pltpu.roll(p[2], 64, 1)
        p3 = pltpu.roll(p[3], 32, 1)
        out.append(jnp.where(lane < 96, p[0], p1))
        out.append(jnp.where(lane < 64, p1, p2))
        out.append(jnp.where(lane < 32, p2, p3))
    return jnp.concatenate(out, axis=1)


def cut_rows(rows):
    lane = iota((T, C), 1)
    a, b, c = rows[:, :C], rows[:, C : 2 * C], rows[:, 2 * C :]
    one = jnp.where(lane < 32, pltpu.roll(a, 32, 1), pltpu.roll(b, 32, 1))
    two = jnp.where(lane < 64, pltpu.roll(b, 64, 1), pltpu.roll(c, 64, 1))
    parts = [a, one, two, pltpu.roll(c, 96, 1)]
    return [jnp.concatenate([p[:16], p[16:]], axis=1) for p in parts]


def gray(i):
    return jnp.where(i >= 2, 5 - i, i)


def partner(i, c, first):
    return jnp.where((c == 0) == first, i ^ 1, 3 - i)


def sequence_kernel(pos_ref, *refs):
    left, right = refs[:16], refs[16:32]
    entry_ref, cot_ref, sent_ref = refs[32:35]
    w_scr, rows_scr, xs, ns, mixed_scr, decay_scr, write_scr, small_scr, proj_scr = refs[35:44]
    first_scr, sem_a, sem_b, sem_c = refs[44:]
    x, y, c, zh, section = (pos_ref[i] for i in range(5))
    mine = jnp.minimum(section, SEQS - 1)
    loads = []
    for i, ref in enumerate((entry_ref, cot_ref)):
        copy = pltpu.make_async_copy(
            ref.at[mine // 3, mine % 3], first_scr.at[i], sem_c.at[i]
        )
        copy.start()
        loads.append(copy)

    def ring(i, core):
        one, two = partner(i, core, True), partner(i, core, False)
        return [i, one, two, partner(two, core, True)]

    for part in range(2):
        for kc in range(2):
            cc = (c + kc) % 2
            ys, xx = ring(y, cc), ring(x, cc)
            for i in range(4):
                at = (kc * 2 + part) * 4 + i
                pltpu.make_async_copy(
                    left[at],
                    w_scr.at[4 * part : 4 * part + 4, :, ys[i], cc, :, :C],
                    sem_a.at[part],
                ).start()
                pltpu.make_async_copy(
                    right[at], w_scr.at[2 * xx[i] + part, :, :, cc, :, C:], sem_b.at[xx[i]]
                ).start()

    def wait_left(part):
        for _ in range(8):
            pltpu.make_async_copy(
                left[0], w_scr.at[0:4, :, 0, 0, :, :C], sem_a.at[part]
            ).wait()

    def wait_right(at):
        for _ in range(4):
            pltpu.make_async_copy(right[0], w_scr.at[0, :, :, 0, :, C:], sem_b.at[at]).wait()

    causal, diag, spread, block, tri = masks()

    def keys_of(layer, m):
        parts = [w_scr[layer, m // 2, (m % 2) * 2 + i // 2, i % 2, :ROWS] for i in range(4)]
        return jnp.concatenate(parts, axis=0)

    def forward(layer, stream):
        @pl.when(layer % 4 == 0)
        def _():
            wait_left(layer // 4)

        @pl.when(layer % 2 == 0)
        def _():
            wait_right(layer // 2)

        rows = assemble_rows(lambda d: w_scr[layer, d // 8, d // 2 % 4, d % 2, ROWS:])
        rows_low = rows.astype(BF16)
        rows_scr[layer] = rows_low
        gain, scale, bias = rows[24:25], rows[25:26], rows[26:27, :T]
        xs[layer] = stream
        x_f = stream.astype(F32)
        inv_rms = lax.rsqrt(jnp.sum(x_f * x_f, axis=1, keepdims=True) * (1.0 / D) + 1e-05)
        normed = (x_f * inv_rms * gain).astype(BF16)
        ns[layer] = normed
        for m in range(BLOCKS):
            sent_ref[layer, T * m : T * (m + 1)] = normed[:, BLOCK * m : BLOCK * (m + 1)]
        logits = nt(normed, rows_low) + bias
        key_query = sum(
            nn(normed[:, BLOCK * m : BLOCK * (m + 1)], keys_of(layer, m)) for m in range(BLOCKS)
        )
        head = iota((T, T), 1) < H
        rate = jnp.maximum(logits, 0.0) + jnp.log1p(jnp.exp(-jnp.abs(logits)))
        rate = jnp.where(head, rate, 0.0)
        keep = 1.0 / (1.0 + rate)
        write = rate * keep
        total = nn(tri, split3(-jnp.log1p(rate)))
        total = total[:, :T] + total[:, T : 2 * T] + total[:, 2 * T : 3 * T]
        wide = nn(jnp.concatenate([split3(total), split3(write)], axis=0), spread)
        total_t, write_t = wide[:T], wide[T:]
        total_s = jnp.sum(jnp.where(diag, total_t, 0.0), axis=0, keepdims=True)
        write_s = jnp.sum(jnp.where(diag, write_t, 0.0), axis=0, keepdims=True)
        decay = jnp.where(causal, jnp.exp(jnp.where(causal, total_t - total_s, 0.0)), 0.0)
        k = key_query[:, :C]
        q = key_query[:, C:]
        inv = lax.rsqrt(jnp.sum(k * k, axis=1, keepdims=True) + 1e-06)
        scores = nt(q.astype(BF16), tile4((k * inv).astype(BF16)))
        decay_scr[layer] = decay
        write_scr[layer] = write_s
        proj_scr[layer] = key_query
        small_scr[layer] = jnp.concatenate([scores, logits, keep, jnp.zeros((T, 64), F32)], axis=1)
        mixing = decay * write_s * jnp.concatenate([scores] * GROUPS, axis=1)
        mixed = unstack_heads(
            [nn(block_diag(mixing, g, block), stack_heads(normed, g)) for g in range(GROUPS)]
        )
        mixed_scr[layer] = mixed.astype(BF16)
        return (x_f + scale * mixed).astype(BF16)

    loads[0].wait()
    loads[1].wait()
    lax.fori_loop(0, LAYERS, forward, first_scr[0])

    def backward(step, back):
        layer = LAYERS - 1 - step
        x_f = xs[layer].astype(F32)
        normed = ns[layer]
        rows_low = rows_scr[layer]
        rows = rows_low[16:].astype(F32)
        gain, scale = rows[8:9], rows[9:10]
        dy = back.astype(F32)
        decay = decay_scr[layer]
        write_s = write_scr[layer]
        small = small_scr[layer]
        scores, logits, keep = small[:, :C], small[:, C : C + T], small[:, C + T : C + 2 * T]
        scores6 = jnp.concatenate([scores] * GROUPS, axis=1)
        mixing = decay * write_s * scores6
        d_scale = jnp.sum(dy * mixed_scr[layer].astype(F32), axis=0, keepdims=True)
        d_out = (dy * scale).astype(BF16)
        d_mix = []
        d_values = []
        for g in range(GROUPS):
            grad = stack_heads(d_out, g)
            full = jnp.where(block, nt(grad, stack_heads(normed, g)), 0.0)
            d_mix.append(full[:T] + full[T : 2 * T] + full[2 * T : 3 * T] + full[3 * T :])
            d_values.append(tn(block_diag(mixing, g, block), grad))
        d_mix = jnp.concatenate(d_mix, axis=1)
        d_values = unstack_heads(d_values)
        near = d_mix * decay
        scored = near * scores6
        d_write_s = jnp.sum(scored, axis=0, keepdims=True)
        weighted = near * write_s
        d_scores = sum(weighted[:, C * g : C * (g + 1)] for g in range(GROUPS)).astype(BF16)
        d_total = scored * write_s - jnp.where(diag, d_write_s * write_s, 0.0)
        gathered = []
        for part in (d_total, jnp.where(diag, d_write_s, 0.0)):
            hi = part.astype(BF16)
            gathered += [hi, (part - hi.astype(F32)).astype(BF16)]
        summed = nt(jnp.concatenate(gathered, axis=0), spread[:T])
        d_total = summed[:T] + summed[T : 2 * T]
        d_write = summed[2 * T : 3 * T] + summed[3 * T :]
        d_log = tn(tri, split3(d_total))
        d_log = d_log[:, :T] + d_log[:, T : 2 * T] + d_log[:, 2 * T : 3 * T]
        d_rate = keep * (d_write * keep - d_log)
        d_logits = d_rate / (1.0 + jnp.exp(-logits))
        d_low = jnp.where(iota((T, T), 1) < H, d_logits, 0.0).astype(BF16)
        k = proj_scr[layer][:, :C]
        q = proj_scr[layer][:, C:]
        inv = lax.rsqrt(jnp.sum(k * k, axis=1, keepdims=True) + 1e-06)
        d_q = nn(d_scores, tile4((k * inv).astype(BF16)))
        d_unit = tn(d_scores, q.astype(BF16))
        d_unit = d_unit[:T] + d_unit[T : 2 * T] + d_unit[2 * T : 3 * T] + d_unit[3 * T :]
        d_k = inv * d_unit - k * (inv * inv * inv * jnp.sum(d_unit * k, axis=1, keepdims=True))
        d_keyq = jnp.concatenate([d_k, d_q], axis=1).astype(BF16)
        through = jnp.concatenate([nt(d_keyq, keys_of(layer, m)) for m in range(BLOCKS)], axis=1)
        d_normed = d_values + through + nn(d_low, rows_low)
        inv_rms = lax.rsqrt(jnp.sum(x_f * x_f, axis=1, keepdims=True) * (1.0 / D) + 1e-05)
        x_hat = x_f * inv_rms
        d_gain = jnp.sum(d_normed * x_hat, axis=0, keepdims=True)
        d_hat = d_normed * gain
        mean = jnp.sum(d_hat * x_hat, axis=1, keepdims=True) * (1.0 / D)
        sent_ref[layer, TOK : TOK + T, :256] = d_keyq
        sent_ref[layer, TOK : TOK + T, 256:] = jnp.concatenate(
            [d_low, jnp.zeros((T, 96), BF16)], axis=1
        )
        sent_ref[layer, TOK + T :] = jnp.concatenate(
            [d[:, BLOCK * i : BLOCK * (i + 1)] for d in (d_gain, d_scale) for i in range(8)], axis=0
        ).astype(BF16)
        return (dy + inv_rms * (d_hat - x_hat * mean)).astype(BF16)

    cot = jnp.where(section < SEQS, first_scr[1].astype(F32), 0.0).astype(BF16)
    lax.fori_loop(0, LAYERS, backward, cot)


def weight_kernel(pos_ref, got_ref, keep_ref, send_ref, got, scr, sem_in, sem):
    y, c, zh = pos_ref[1], pos_ref[2], pos_ref[3]
    loads = []
    for m in list(range(BLOCKS)) + [BLOCKS]:
        at = pl.ds(T * m, T if m < BLOCKS else T + 16)
        loads.append(pltpu.make_async_copy(got_ref.at[:, at], got.at[:, at], sem_in.at[m]))
    loads[-1].start()
    for copy in loads[:-1]:
        copy.start()

    def slot(there, here, core):
        bits = gray(jnp.int32(there)) ^ gray(here)
        return bits if core else (bits & 1) * 2 + (bits >> 1)

    loads[-1].wait()
    tokens = jnp.concatenate([got[s, TOK : TOK + T] for s in range(LAYERS)], axis=0)
    extra = sum(got[s, TOK + T :].astype(F32) for s in range(LAYERS))
    bias = jnp.sum(tokens[:, 256:].astype(F32), axis=0, keepdims=True)
    bias = jnp.concatenate([bias[:, :ROWS]] * 4, axis=1)
    for m in range(BLOCKS):
        loads[m].wait()
        normed = jnp.concatenate([got[s, T * m : T * (m + 1)] for s in range(LAYERS)], axis=0)
        keys = tn(normed, tokens[:, :256])
        rates = tn(tokens[:, 256:], normed)[:H]
        rows = jnp.concatenate(
            [rates, extra[m : m + 1], extra[m + 8 : m + 9], bias, jnp.zeros((5, BLOCK), F32)],
            axis=0,
        )
        low = cut_rows(rows)
        for i in range(4):
            d = 4 * m + i
            y_at, z_at = slot(d // 2 % 4, y, d % 2), slot(d // 8, zh, d % 2)
            c_at = (d + c) % 2
            scr[c_at, y_at, z_at, :ROWS] = keys[ROWS * i : ROWS * (i + 1)].astype(BF16)
            scr[c_at, y_at, z_at, ROWS:] = low[i].astype(BF16)
    for i, ref in enumerate((keep_ref, send_ref)):
        pltpu.make_async_copy(scr.at[i], ref, sem.at[i]).start()
    for i, ref in enumerate((keep_ref, send_ref)):
        pltpu.make_async_copy(scr.at[i], ref, sem.at[i]).wait()


def final_kernel(a_ref, b_ref, c_ref, d_ref, scales_ref, keys_ref, rates_ref, bias_ref):
    total = a_ref[...].astype(F32) + b_ref[...].astype(F32)
    total = total + c_ref[...].astype(F32) + d_ref[...].astype(F32)
    keys_ref[...] = total[:ROWS]
    rates = jnp.concatenate([total[ROWS:, :C], total[ROWS:, C:]], axis=0)
    rates_ref[...] = rates[:H, :ROWS]
    scales_ref[...] = rates[24:26, :ROWS]
    bias_ref[...] = rates[26:27, :H]


ANY = pl.BlockSpec(memory_space=pl.ANY)
VMEM = pl.BlockSpec(memory_space=pltpu.VMEM)
SMEM = pl.BlockSpec(memory_space=pltpu.SMEM)
PARAMS = pltpu.CompilerParams(vmem_limit_bytes=56 * 1024 * 1024)


def shape(*dims, dtype=BF16):
    return jax.ShapeDtypeStruct(dims, dtype)


def call(kernel, outs, ins, scratch, out_spec=None, cost=None):
    flops, moved = cost
    return pl.pallas_call(
        kernel,
        out_shape=outs,
        in_specs=ins,
        out_specs=out_spec or [VMEM] * len(outs),
        scratch_shapes=scratch,
        compiler_params=PARAMS,
        cost_estimate=pl.CostEstimate(flops=flops, bytes_accessed=moved, transcendentals=0),
    )


def ring_pairs(first):
    pairs = []
    for i in range(4):
        for c in range(2):
            to = i ^ 1 if (c == 0) == first else 3 - i
            pairs.append((i * 2 + c, to * 2 + c))
    return pairs


def swap(array, axis, first):
    return lax.ppermute(array, (axis, "c"), ring_pairs(first))


def other_core(array):
    return lax.ppermute(array, "c", [(0, 1), (1, 0)])


def opposite(array, axis):
    return lax.ppermute(array, axis, [(i, i ^ 2) for i in range(4)])


def gather_ring(array, axis):
    one = swap(array, axis, True)
    two = swap(array, axis, False)
    return [array, one, two, swap(one, axis, False)]


def add(*parts):
    return sum(a.astype(F32) for a in parts).astype(BF16)


def per_device(entries, cotangents, scales, key_weight, rate_weight, rate_bias):
    x, zl, zh, y, c = (lax.axis_index(a) for a in ("x", "zl", "zh", "y", "c"))
    section = x * 2 + zl
    pos = jnp.stack([x, y, c, zh, section]).astype(jnp.int32)

    wide = jnp.pad(rate_weight[0].T, ((0, 0), (0, C - ROWS)))
    small = jnp.pad(scales[0], ((0, 0), (0, C - ROWS)))
    line = jnp.pad(rate_bias, ((0, 0), (0, C - H)))
    right = jnp.concatenate([wide[16:], small, line, jnp.zeros((5, C), BF16)], axis=0)
    packed = jnp.concatenate(
        [key_weight[0], jnp.concatenate([wide[:16], right], axis=1)], axis=0
    )

    along = [packed] + [None] * 7
    for k in (4, 3, 5, 2, 6, 1, 7):
        pairs = []
        for z in range(8):
            for core in range(2):
                to = (z + k if core == 0 else z - k) % 8
                pairs.append(tuple(((i % 2) * 4 + i // 2) * 2 + core for i in (z, to)))
        along[k] = lax.ppermute(packed, ("zl", "zh", "c"), pairs)
    z = zh * 2 + zl
    there = jnp.arange(4)[None] * 2 + jnp.arange(2)[:, None]
    both = jnp.take(jnp.stack(along), jnp.where(c == 0, z - there, there - z) % 8, axis=0)

    def order(i):
        bits = gray(jnp.arange(4)) ^ gray(i)
        return jnp.where(c == 0, jnp.array([0, 1, 2, 3])[bits], jnp.array([0, 2, 1, 3])[bits])

    left = jnp.stack(gather_ring(both[..., :C], "x"))
    right = jnp.stack(gather_ring(both[..., C:], "y"), axis=2)
    x_order, y_order = order(x), order(y)
    lefts, rights = [], []
    for part in range(2):
        own = jnp.take(left, x_order[2 * part : 2 * part + 2], axis=0)
        lefts += gather_ring(own.reshape(4, 4, PIECE, C), "y")
        own = jnp.take(right[part], y_order, axis=1)
        rights += gather_ring(own, "x")
    left = lefts + [other_core(a) for a in lefts]
    right = rights + [other_core(a) for a in rights]

    sent = call(
        sequence_kernel,
        [shape(LAYERS, SENT, BLOCK)],
        [SMEM] + [ANY] * 34,
        [
            pltpu.VMEM((LAYERS, 4, 4, 2, PIECE, 256), BF16),
            pltpu.VMEM((LAYERS, T, D), BF16),
            pltpu.VMEM((LAYERS, T, D), BF16),
            pltpu.VMEM((LAYERS, T, D), BF16),
            pltpu.VMEM((LAYERS, T, D), BF16),
            pltpu.VMEM((LAYERS, T, W), F32),
            pltpu.VMEM((LAYERS, 1, W), F32),
            pltpu.VMEM((LAYERS, T, 256), F32),
            pltpu.VMEM((LAYERS, T, 256), F32),
            pltpu.VMEM((2, T, D), BF16),
            pltpu.SemaphoreType.DMA((2,)),
            pltpu.SemaphoreType.DMA((4,)),
            pltpu.SemaphoreType.DMA((2,)),
        ],
        cost=(8_000_000_000, 30_000_000),
    )(pos, *left, *right, entries, cotangents)[0]

    got = lax.all_to_all(sent, SECTION, 0, 0, tiled=True)
    half = shape(4, 4, PIECE, 256)
    keep, send = call(
        weight_kernel,
        [half, half],
        [SMEM, ANY],
        [
            pltpu.VMEM((LAYERS, SENT, BLOCK), BF16),
            pltpu.VMEM((2, 4, 4, PIECE, 256), BF16),
            pltpu.SemaphoreType.DMA((BLOCKS + 1,)),
            pltpu.SemaphoreType.DMA((2,)),
        ],
        [ANY] * 2,
        cost=(600_000_000, 4_000_000),
    )(pos, got)
    got = other_core(send)
    total = [add(keep[i], got[i]) for i in range(4)]
    got = add(
        total[0], swap(total[2], "y", True), swap(total[1], "y", False), opposite(total[3], "y")
    )
    parts = [
        got[0],
        swap(got[2], "zh", True),
        swap(got[1], "zh", False),
        opposite(got[3], "zh"),
    ]
    g_scales, g_keys, g_rates, g_bias = call(
        final_kernel,
        [
            shape(2, ROWS, dtype=F32),
            shape(ROWS, 256, dtype=F32),
            shape(H, ROWS, dtype=F32),
            shape(1, H, dtype=F32),
        ],
        [VMEM] * 4,
        [],
        cost=(0, 500_000),
    )(*parts)
    return g_scales[None], g_keys[None], g_rates.T[None], g_bias


def solution(mesh):
    fine = Mesh(mesh.devices.reshape(4, 2, 4, 4, 2), ("x", "zl", "zh", "y", "c"))
    placed = (
        P(None, None, DP, None),
        P(None, None, DP, None),
        P(SECTION, None, DP),
        P(SECTION, DP, None),
        P(SECTION, DP, None),
        P(SECTION, None),
    )
    return jax.shard_map(
        per_device,
        mesh=fine,
        in_specs=placed,
        out_specs=(
            P(SECTION, None, DP),
            P(SECTION, DP, None),
            P(SECTION, DP, None),
            P(SECTION, None),
        ),
        check_vma=False,
    )
```

```python
import jax
import jax.numpy as jnp
from jax import lax
from jax.experimental import pallas as pl
from jax.experimental.pallas import tpu as pltpu
from jax.sharding import Mesh, PartitionSpec as P

F32 = jnp.float32
BF16 = jnp.bfloat16
SECTION = ("x", "zl")
DP = ("zh", "y", "c")

T = 32
D = 3072
C = 128
H = 24
GROUPS = H // 4
W = H * T
LAYERS = 8
SEQS = 6
ROWS = 96
PIECE = 112
TOK = LAYERS * T
BLOCK = 384
BLOCKS = D // BLOCK
SENT = BLOCKS * T + T + 16


def iota(shape, axis):
    return lax.broadcasted_iota(jnp.int32, shape, axis)


def nt(a, b):
    return lax.dot_general(
        a, b, (((1,), (1,)), ((), ())), preferred_element_type=F32
    )


def tn(a, b):
    return lax.dot_general(
        a, b, (((0,), (0,)), ((), ())), preferred_element_type=F32
    )


def nn(a, b):
    return jnp.dot(a, b, preferred_element_type=F32)


def split3(a):
    hi = a.astype(BF16)
    rest = a - hi.astype(F32)
    mid = rest.astype(BF16)
    low = (rest - mid.astype(F32)).astype(BF16)
    return jnp.concatenate([hi, mid, low, jnp.zeros_like(hi)], axis=1)


def masks():
    row = iota((T, W), 0)
    col = iota((T, W), 1) % T
    spread = (iota((C, W), 0) % T == iota((C, W), 1) // T) & (iota((C, W), 0) < 3 * T)
    spread = jnp.where(spread, 1.0, 0.0).astype(BF16)
    block = iota((C, C), 0) // T == iota((C, C), 1) // T
    tri = jnp.where(iota((T, T), 0) >= iota((T, T), 1), 1.0, 0.0).astype(BF16)
    return row >= col, row == col, spread, block, tri


def tile4(a):
    return jnp.concatenate([a] * 4, axis=0)


def stack_heads(a, g):
    return jnp.concatenate([a[:, C * (4 * g + j) : C * (4 * g + j + 1)] for j in range(4)], axis=0)


def unstack_heads(parts):
    return jnp.concatenate([p[T * j : T * (j + 1)] for p in parts for j in range(4)], axis=1)


def block_diag(mixing, g, block):
    return jnp.where(block, tile4(mixing[:, C * g : C * (g + 1)]), 0.0).astype(BF16)


def assemble_rows(piece):
    out = []
    lane = iota((T, C), 1)
    for m in range(8):
        p = []
        for i in range(4):
            z = piece(4 * m + i).astype(F32)
            p.append(jnp.concatenate([z[:, :C], z[:, C:]], axis=0))
        p1 = pltpu.roll(p[1], 96, 1)
        p2 = pltpu.roll(p[2], 64, 1)
        p3 = pltpu.roll(p[3], 32, 1)
        out.append(jnp.where(lane < 96, p[0], p1))
        out.append(jnp.where(lane < 64, p1, p2))
        out.append(jnp.where(lane < 32, p2, p3))
    return jnp.concatenate(out, axis=1)


def cut_rows(rows):
    lane = iota((T, C), 1)
    a, b, c = rows[:, :C], rows[:, C : 2 * C], rows[:, 2 * C :]
    one = jnp.where(lane < 32, pltpu.roll(a, 32, 1), pltpu.roll(b, 32, 1))
    two = jnp.where(lane < 64, pltpu.roll(b, 64, 1), pltpu.roll(c, 64, 1))
    parts = [a, one, two, pltpu.roll(c, 96, 1)]
    return [jnp.concatenate([p[:16], p[16:]], axis=1) for p in parts]


def gray(i):
    return jnp.where(i >= 2, 5 - i, i)


def partner(i, c, first):
    return jnp.where((c == 0) == first, i ^ 1, 3 - i)


def sequence_kernel(pos_ref, *refs):
    left, right = refs[:8], refs[8:16]
    entry_ref, cot_ref, sent_ref = refs[16:19]
    w_scr, rows_scr, xs, ns, mixed_scr, decay_scr, write_scr, small_scr, proj_scr = refs[19:28]
    first_scr, sem_a, sem_b, sem_c = refs[28:]
    x, y, c, zh, section = (pos_ref[i] for i in range(5))
    mine = jnp.minimum(section, SEQS - 1)
    loads = []
    for i, ref in enumerate((entry_ref, cot_ref)):
        copy = pltpu.make_async_copy(
            ref.at[mine // 3, mine % 3], first_scr.at[i], sem_c.at[i]
        )
        copy.start()
        loads.append(copy)

    def ring(i, core):
        one, two = partner(i, core, True), partner(i, core, False)
        return [i, one, two, partner(two, core, True)]

    for target in range(4):
        for kc in range(2):
            cc = (c + kc) % 2
            ys, xx = ring(y, cc), ring(x, cc)
            slot = sum(jnp.where(xx[j] == target, j, 0) for j in range(4))
            for i in range(4):
                pltpu.make_async_copy(
                    left[kc * 4 + i].at[slot],
                    w_scr.at[2 * target : 2 * target + 2, :, ys[i], cc, :, :C],
                    sem_a.at[target],
                ).start()

                @pl.when(xx[i] == target)
                def _(i=i, kc=kc, cc=cc, ys=ys, target=target):
                    for j in range(4):
                        pltpu.make_async_copy(
                            right[kc * 4 + i].at[j],
                            w_scr.at[2 * target : 2 * target + 2, :, ys[j], cc, :, C:],
                            sem_b.at[target],
                        ).start()

    def wait_layers(at):
        for sem, src in ((sem_a, left[0]), (sem_b, right[0])):
            for _ in range(8):
                pltpu.make_async_copy(
                    src.at[0], w_scr.at[0:2, :, 0, 0, :, :C], sem.at[at]
                ).wait()

    causal, diag, spread, block, tri = masks()

    def keys_of(layer, m):
        parts = [w_scr[layer, m // 2, (m % 2) * 2 + i // 2, i % 2, :ROWS] for i in range(4)]
        return jnp.concatenate(parts, axis=0)

    def forward(layer, stream):
        @pl.when(layer % 2 == 0)
        def _():
            wait_layers(layer // 2)

        rows = assemble_rows(lambda d: w_scr[layer, d // 8, d // 2 % 4, d % 2, ROWS:])
        rows_low = rows.astype(BF16)
        rows_scr[layer] = rows_low
        gain, scale, bias = rows[24:25], rows[25:26], rows[26:27, :T]
        xs[layer] = stream
        x_f = stream.astype(F32)
        inv_rms = lax.rsqrt(jnp.sum(x_f * x_f, axis=1, keepdims=True) * (1.0 / D) + 1e-05)
        normed = (x_f * inv_rms * gain).astype(BF16)
        ns[layer] = normed
        for m in range(BLOCKS):
            sent_ref[layer, T * m : T * (m + 1)] = normed[:, BLOCK * m : BLOCK * (m + 1)]
        logits = nt(normed, rows_low) + bias
        key_query = sum(
            nn(normed[:, BLOCK * m : BLOCK * (m + 1)], keys_of(layer, m)) for m in range(BLOCKS)
        )
        head = iota((T, T), 1) < H
        rate = jnp.maximum(logits, 0.0) + jnp.log1p(jnp.exp(-jnp.abs(logits)))
        rate = jnp.where(head, rate, 0.0)
        keep = 1.0 / (1.0 + rate)
        write = rate * keep
        total = nn(tri, split3(-jnp.log1p(rate)))
        total = total[:, :T] + total[:, T : 2 * T] + total[:, 2 * T : 3 * T]
        wide = nn(jnp.concatenate([split3(total), split3(write)], axis=0), spread)
        total_t, write_t = wide[:T], wide[T:]
        total_s = jnp.sum(jnp.where(diag, total_t, 0.0), axis=0, keepdims=True)
        write_s = jnp.sum(jnp.where(diag, write_t, 0.0), axis=0, keepdims=True)
        decay = jnp.where(causal, jnp.exp(jnp.where(causal, total_t - total_s, 0.0)), 0.0)
        k = key_query[:, :C]
        q = key_query[:, C:]
        inv = lax.rsqrt(jnp.sum(k * k, axis=1, keepdims=True) + 1e-06)
        scores = nt(q.astype(BF16), tile4((k * inv).astype(BF16)))
        decay_scr[layer] = decay
        write_scr[layer] = write_s
        proj_scr[layer] = key_query
        small_scr[layer] = jnp.concatenate([scores, logits, keep, jnp.zeros((T, 64), F32)], axis=1)
        mixing = decay * write_s * jnp.concatenate([scores] * GROUPS, axis=1)
        mixed = unstack_heads(
            [nn(block_diag(mixing, g, block), stack_heads(normed, g)) for g in range(GROUPS)]
        )
        mixed_scr[layer] = mixed.astype(BF16)
        return (x_f + scale * mixed).astype(BF16)

    loads[0].wait()
    loads[1].wait()
    lax.fori_loop(0, LAYERS, forward, first_scr[0], unroll=2)

    def backward(step, back):
        layer = LAYERS - 1 - step
        x_f = xs[layer].astype(F32)
        normed = ns[layer]
        rows_low = rows_scr[layer]
        rows = rows_low[16:].astype(F32)
        gain, scale = rows[8:9], rows[9:10]
        dy = back.astype(F32)
        decay = decay_scr[layer]
        write_s = write_scr[layer]
        small = small_scr[layer]
        scores, logits, keep = small[:, :C], small[:, C : C + T], small[:, C + T : C + 2 * T]
        scores6 = jnp.concatenate([scores] * GROUPS, axis=1)
        mixing = decay * write_s * scores6
        d_scale = jnp.sum(dy * mixed_scr[layer].astype(F32), axis=0, keepdims=True)
        d_out = (dy * scale).astype(BF16)
        d_mix = []
        d_values = []
        for g in range(GROUPS):
            grad = stack_heads(d_out, g)
            full = jnp.where(block, nt(grad, stack_heads(normed, g)), 0.0)
            d_mix.append(full[:T] + full[T : 2 * T] + full[2 * T : 3 * T] + full[3 * T :])
            d_values.append(tn(block_diag(mixing, g, block), grad))
        d_mix = jnp.concatenate(d_mix, axis=1)
        d_values = unstack_heads(d_values)
        near = d_mix * decay
        scored = near * scores6
        d_write_s = jnp.sum(scored, axis=0, keepdims=True)
        weighted = near * write_s
        d_scores = sum(weighted[:, C * g : C * (g + 1)] for g in range(GROUPS)).astype(BF16)
        d_total = scored * write_s - jnp.where(diag, d_write_s * write_s, 0.0)
        gathered = []
        for part in (d_total, jnp.where(diag, d_write_s, 0.0)):
            hi = part.astype(BF16)
            gathered += [hi, (part - hi.astype(F32)).astype(BF16)]
        summed = nt(jnp.concatenate(gathered, axis=0), spread[:T])
        d_total = summed[:T] + summed[T : 2 * T]
        d_write = summed[2 * T : 3 * T] + summed[3 * T :]
        d_log = tn(tri, split3(d_total))
        d_log = d_log[:, :T] + d_log[:, T : 2 * T] + d_log[:, 2 * T : 3 * T]
        d_rate = keep * (d_write * keep - d_log)
        d_logits = d_rate / (1.0 + jnp.exp(-logits))
        d_low = jnp.where(iota((T, T), 1) < H, d_logits, 0.0).astype(BF16)
        k = proj_scr[layer][:, :C]
        q = proj_scr[layer][:, C:]
        inv = lax.rsqrt(jnp.sum(k * k, axis=1, keepdims=True) + 1e-06)
        d_q = nn(d_scores, tile4((k * inv).astype(BF16)))
        d_unit = tn(d_scores, q.astype(BF16))
        d_unit = d_unit[:T] + d_unit[T : 2 * T] + d_unit[2 * T : 3 * T] + d_unit[3 * T :]
        d_k = inv * d_unit - k * (inv * inv * inv * jnp.sum(d_unit * k, axis=1, keepdims=True))
        d_keyq = jnp.concatenate([d_k, d_q], axis=1).astype(BF16)
        through = jnp.concatenate([nt(d_keyq, keys_of(layer, m)) for m in range(BLOCKS)], axis=1)
        d_normed = d_values + through + nn(d_low, rows_low)
        inv_rms = lax.rsqrt(jnp.sum(x_f * x_f, axis=1, keepdims=True) * (1.0 / D) + 1e-05)
        x_hat = x_f * inv_rms
        d_gain = jnp.sum(d_normed * x_hat, axis=0, keepdims=True)
        d_hat = d_normed * gain
        mean = jnp.sum(d_hat * x_hat, axis=1, keepdims=True) * (1.0 / D)
        sent_ref[layer, TOK : TOK + T, :256] = d_keyq
        sent_ref[layer, TOK : TOK + T, 256:] = jnp.concatenate(
            [d_low, jnp.zeros((T, 96), BF16)], axis=1
        )
        sent_ref[layer, TOK + T :] = jnp.concatenate(
            [d[:, BLOCK * i : BLOCK * (i + 1)] for d in (d_gain, d_scale) for i in range(8)], axis=0
        ).astype(BF16)
        return (dy + inv_rms * (d_hat - x_hat * mean)).astype(BF16)

    cot = jnp.where(section < SEQS, first_scr[1].astype(F32), 0.0).astype(BF16)
    lax.fori_loop(0, LAYERS, backward, cot, unroll=2)


def weight_kernel(pos_ref, got_ref, keep_ref, send_ref, got, scr, sem_in, sem):
    y, c, zh = pos_ref[1], pos_ref[2], pos_ref[3]
    loads = []
    for m in list(range(BLOCKS)) + [BLOCKS]:
        at = pl.ds(T * m, T if m < BLOCKS else T + 16)
        loads.append(pltpu.make_async_copy(got_ref.at[:, at], got.at[:, at], sem_in.at[m]))
    loads[-1].start()
    for copy in loads[:-1]:
        copy.start()

    def slot(there, here, core):
        bits = gray(jnp.int32(there)) ^ gray(here)
        return bits if core else (bits & 1) * 2 + (bits >> 1)

    loads[-1].wait()
    tokens = jnp.concatenate([got[s, TOK : TOK + T] for s in range(LAYERS)], axis=0)
    extra = sum(got[s, TOK + T :].astype(F32) for s in range(LAYERS))
    bias = jnp.sum(tokens[:, 256:].astype(F32), axis=0, keepdims=True)
    bias = jnp.concatenate([bias[:, :ROWS]] * 4, axis=1)
    for m in range(BLOCKS):
        loads[m].wait()
        normed = jnp.concatenate([got[s, T * m : T * (m + 1)] for s in range(LAYERS)], axis=0)
        keys = tn(normed, tokens[:, :256])
        rates = tn(tokens[:, 256:], normed)[:H]
        rows = jnp.concatenate(
            [rates, extra[m : m + 1], extra[m + 8 : m + 9], bias, jnp.zeros((5, BLOCK), F32)],
            axis=0,
        )
        low = cut_rows(rows)
        for i in range(4):
            d = 4 * m + i
            y_at, z_at = slot(d // 2 % 4, y, d % 2), slot(d // 8, zh, d % 2)
            c_at = (d + c) % 2
            scr[c_at, y_at, z_at, :ROWS] = keys[ROWS * i : ROWS * (i + 1)].astype(BF16)
            scr[c_at, y_at, z_at, ROWS:] = low[i].astype(BF16)
        if m % 2:
            for core in range(2):
                z_at = slot(m // 2, zh, core)
                for i, ref in enumerate((keep_ref, send_ref)):

                    @pl.when((core + c) % 2 == i)
                    def _(i=i, ref=ref, z_at=z_at):
                        pltpu.make_async_copy(scr.at[i, :, z_at], ref.at[:, z_at], sem.at[i]).start()

    for i, ref in enumerate((keep_ref, send_ref)):
        pltpu.make_async_copy(scr.at[i], ref, sem.at[i]).wait()


def final_kernel(a_ref, b_ref, c_ref, d_ref, scales_ref, keys_ref, rates_ref, bias_ref):
    total = a_ref[...].astype(F32) + b_ref[...].astype(F32)
    total = total + c_ref[...].astype(F32) + d_ref[...].astype(F32)
    keys_ref[...] = total[:ROWS]
    rates = jnp.concatenate([total[ROWS:, :C], total[ROWS:, C:]], axis=0)
    rates_ref[...] = rates[:H, :ROWS]
    scales_ref[...] = rates[24:26, :ROWS]
    bias_ref[...] = rates[26:27, :H]


ANY = pl.BlockSpec(memory_space=pl.ANY)
VMEM = pl.BlockSpec(memory_space=pltpu.VMEM)
SMEM = pl.BlockSpec(memory_space=pltpu.SMEM)
PARAMS = pltpu.CompilerParams(vmem_limit_bytes=56 * 1024 * 1024)


def shape(*dims, dtype=BF16):
    return jax.ShapeDtypeStruct(dims, dtype)


def call(kernel, outs, ins, scratch, out_spec=None, cost=None):
    flops, moved = cost
    return pl.pallas_call(
        kernel,
        out_shape=outs,
        in_specs=ins,
        out_specs=out_spec or [VMEM] * len(outs),
        scratch_shapes=scratch,
        compiler_params=PARAMS,
        cost_estimate=pl.CostEstimate(flops=flops, bytes_accessed=moved, transcendentals=0),
    )


def ring_pairs(first):
    pairs = []
    for i in range(4):
        for c in range(2):
            to = i ^ 1 if (c == 0) == first else 3 - i
            pairs.append((i * 2 + c, to * 2 + c))
    return pairs


def swap(array, axis, first):
    return lax.ppermute(array, (axis, "c"), ring_pairs(first))


def other_core(array):
    return lax.ppermute(array, "c", [(0, 1), (1, 0)])


def opposite(array, axis):
    return lax.ppermute(array, axis, [(i, i ^ 2) for i in range(4)])


def gather_ring(array, axis, direct=False):
    one = swap(array, axis, True)
    two = swap(array, axis, False)
    return [array, one, two, opposite(array, axis) if direct else swap(one, axis, False)]


def add(a, b):
    return (a.astype(F32) + b.astype(F32)).astype(BF16)


def per_device(entries, cotangents, scales, key_weight, rate_weight, rate_bias):
    x, zl, zh, y, c = (lax.axis_index(a) for a in ("x", "zl", "zh", "y", "c"))
    section = x * 2 + zl
    pos = jnp.stack([x, y, c, zh, section]).astype(jnp.int32)

    wide = jnp.pad(rate_weight[0].T, ((0, 0), (0, C - ROWS)))
    small = jnp.pad(scales[0], ((0, 0), (0, C - ROWS)))
    line = jnp.pad(rate_bias, ((0, 0), (0, C - H)))
    right = jnp.concatenate([wide[16:], small, line, jnp.zeros((5, C), BF16)], axis=0)
    packed = jnp.concatenate(
        [key_weight[0], jnp.concatenate([wide[:16], right], axis=1)], axis=0
    )

    along = jnp.stack(gather_ring(packed, "zh", direct=True))
    first, second = partner(zh, c, True), partner(zh, c, False)
    across = partner(second, c, True)
    order = [jnp.where(j == first, 1, jnp.where(j == second, 2, jnp.where(j == across, 3, 0))) for j in range(4)]
    along = jnp.take(along, jnp.stack(order), axis=0)
    pairs = []
    for z in range(8):
        for core in range(2):
            to = z ^ 1 if core == 0 else (z + 1 if z % 2 else z - 1) % 8
            pairs.append(tuple(((i % 2) * 4 + i // 2) * 2 + core for i in (z, to)))
    other = lax.ppermute(along, ("zl", "zh", "c"), pairs)
    both = jnp.where(zl == 0, jnp.stack([along, other]), jnp.stack([other, along]))

    left = jnp.stack(gather_ring(both[..., :C], "x"))
    right = jnp.stack(gather_ring(both[..., C:], "y"))
    left = gather_ring(left, "y")
    right = gather_ring(right, "x")
    left = left + [other_core(a) for a in left]
    right = right + [other_core(a) for a in right]

    sent = call(
        sequence_kernel,
        [shape(LAYERS, SENT, BLOCK)],
        [SMEM] + [ANY] * 18,
        [
            pltpu.VMEM((LAYERS, 4, 4, 2, PIECE, 256), BF16),
            pltpu.VMEM((LAYERS, T, D), BF16),
            pltpu.VMEM((LAYERS, T, D), BF16),
            pltpu.VMEM((LAYERS, T, D), BF16),
            pltpu.VMEM((LAYERS, T, D), BF16),
            pltpu.VMEM((LAYERS, T, W), F32),
            pltpu.VMEM((LAYERS, 1, W), F32),
            pltpu.VMEM((LAYERS, T, 256), F32),
            pltpu.VMEM((LAYERS, T, 256), F32),
            pltpu.VMEM((2, T, D), BF16),
            pltpu.SemaphoreType.DMA((4,)),
            pltpu.SemaphoreType.DMA((4,)),
            pltpu.SemaphoreType.DMA((2,)),
        ],
        cost=(8_000_000_000, 30_000_000),
    )(pos, *left, *right, entries, cotangents)[0]

    groups = [
        [
            (((i * 4) + (z - i % 2 * core) % 4) * 4 + row) * 2 + core
            for i in range(LAYERS)
        ]
        for z in range(4)
        for row in range(4)
        for core in range(2)
    ]
    got = lax.all_to_all(
        sent, ("x", "zl", "zh", "y", "c"), 0, 0, axis_index_groups=groups, tiled=True
    )
    half = shape(4, 4, PIECE, 256)
    keep, send = call(
        weight_kernel,
        [half, half],
        [SMEM, ANY],
        [
            pltpu.VMEM((LAYERS, SENT, BLOCK), BF16),
            pltpu.VMEM((2, 4, 4, PIECE, 256), BF16),
            pltpu.SemaphoreType.DMA((BLOCKS + 1,)),
            pltpu.SemaphoreType.DMA((2,)),
        ],
        [ANY] * 2,
        cost=(600_000_000, 4_000_000),
    )(pos, got)
    got = other_core(send)
    got = swap(add(keep[2:], got[2:]), "y", True), keep[:2], got[:2]
    keep = add(got[1], got[2])
    got = got[0]
    got, keep = swap(add(keep[1], got[1]), "y", False), add(keep[0], got[0])
    got = add(keep, got)
    parts = [
        got[0],
        swap(got[2], "zh", True),
        swap(got[1], "zh", False),
        opposite(got[3], "zh"),
    ]
    g_scales, g_keys, g_rates, g_bias = call(
        final_kernel,
        [
            shape(2, ROWS, dtype=F32),
            shape(ROWS, 256, dtype=F32),
            shape(H, ROWS, dtype=F32),
            shape(1, H, dtype=F32),
        ],
        [VMEM] * 4,
        [],
        cost=(0, 500_000),
    )(*parts)
    return g_scales[None], g_keys[None], g_rates.T[None], g_bias


def solution(mesh):
    fine = Mesh(mesh.devices.reshape(4, 2, 4, 4, 2), ("x", "zl", "zh", "y", "c"))
    placed = (
        P(None, None, DP, None),
        P(None, None, DP, None),
        P(SECTION, None, DP),
        P(SECTION, DP, None),
        P(SECTION, DP, None),
        P(SECTION, None),
    )
    return jax.shard_map(
        per_device,
        mesh=fine,
        in_specs=placed,
        out_specs=(
            P(SECTION, None, DP),
            P(SECTION, DP, None),
            P(SECTION, DP, None),
            P(SECTION, None),
        ),
        check_vma=False,
    )
```

```python
import jax
import jax.numpy as jnp
from jax import lax
from jax.experimental import pallas as pl
from jax.experimental.pallas import tpu as pltpu
from jax.sharding import Mesh, PartitionSpec as P

F32 = jnp.float32
BF16 = jnp.bfloat16
SECTION = ("x", "zl")
DP = ("zh", "y", "c")

T = 32
D = 3072
C = 128
H = 24
GROUPS = H // 4
W = H * T
LAYERS = 8
SEQS = 6
ROWS = 96
PIECE = 112
TOK = LAYERS * T
BLOCK = 384
BLOCKS = D // BLOCK
SENT = BLOCKS * T + T + 16


def iota(shape, axis):
    return lax.broadcasted_iota(jnp.int32, shape, axis)


def nt(a, b):
    return lax.dot_general(
        a, b, (((1,), (1,)), ((), ())), preferred_element_type=F32
    )


def tn(a, b):
    return lax.dot_general(
        a, b, (((0,), (0,)), ((), ())), preferred_element_type=F32
    )


def nn(a, b):
    return jnp.dot(a, b, preferred_element_type=F32)


def split3(a):
    hi = a.astype(BF16)
    rest = a - hi.astype(F32)
    mid = rest.astype(BF16)
    low = (rest - mid.astype(F32)).astype(BF16)
    return jnp.concatenate([hi, mid, low, jnp.zeros_like(hi)], axis=1)


def masks():
    row = iota((T, W), 0)
    col = iota((T, W), 1) % T
    spread = (iota((C, W), 0) % T == iota((C, W), 1) // T) & (iota((C, W), 0) < 3 * T)
    spread = jnp.where(spread, 1.0, 0.0).astype(BF16)
    block = iota((C, C), 0) // T == iota((C, C), 1) // T
    tri = jnp.where(iota((T, T), 0) >= iota((T, T), 1), 1.0, 0.0).astype(BF16)
    return row >= col, row == col, spread, block, tri


def tile4(a):
    return jnp.concatenate([a] * 4, axis=0)


def stack_heads(a, g):
    return jnp.concatenate([a[:, C * (4 * g + j) : C * (4 * g + j + 1)] for j in range(4)], axis=0)


def unstack_heads(parts):
    return jnp.concatenate([p[T * j : T * (j + 1)] for p in parts for j in range(4)], axis=1)


def block_diag(mixing, g, block):
    return jnp.where(block, tile4(mixing[:, C * g : C * (g + 1)]), 0.0).astype(BF16)


def assemble_rows(piece):
    out = []
    lane = iota((T, C), 1)
    for m in range(8):
        p = []
        for i in range(4):
            z = piece(4 * m + i).astype(F32)
            p.append(jnp.concatenate([z[:, :C], z[:, C:]], axis=0))
        p1 = pltpu.roll(p[1], 96, 1)
        p2 = pltpu.roll(p[2], 64, 1)
        p3 = pltpu.roll(p[3], 32, 1)
        out.append(jnp.where(lane < 96, p[0], p1))
        out.append(jnp.where(lane < 64, p1, p2))
        out.append(jnp.where(lane < 32, p2, p3))
    return jnp.concatenate(out, axis=1)


def cut_rows(rows):
    lane = iota((T, C), 1)
    a, b, c = rows[:, :C], rows[:, C : 2 * C], rows[:, 2 * C :]
    one = jnp.where(lane < 32, pltpu.roll(a, 32, 1), pltpu.roll(b, 32, 1))
    two = jnp.where(lane < 64, pltpu.roll(b, 64, 1), pltpu.roll(c, 64, 1))
    parts = [a, one, two, pltpu.roll(c, 96, 1)]
    return [jnp.concatenate([p[:16], p[16:]], axis=1) for p in parts]


def gray(i):
    return jnp.where(i >= 2, 5 - i, i)


def ring(i):
    return [i, i ^ 1, 3 - i, (3 - i) ^ 1]


def sequence_kernel(pos_ref, *refs):
    sets = refs[:5], refs[5:10]
    entry_ref, cot_ref, sent_ref = refs[10:13]
    w_scr, rows_scr, xs, ns, mixed_scr, decay_scr, write_scr, small_scr, proj_scr = refs[13:22]
    first_scr, sem_w, sem_c = refs[22:]
    x, y, c, zh, section = (pos_ref[i] for i in range(5))
    mine = jnp.minimum(section, SEQS - 1)
    loads = []
    for i, ref in enumerate((entry_ref, cot_ref)):
        copy = pltpu.make_async_copy(
            ref.at[mine // 3, mine % 3], first_scr.at[i], sem_c.at[i]
        )
        copy.start()
        loads.append(copy)

    def place(at):
        side = (c + at) % 2
        ys, xs_ = ring(y), ring(x)
        for i in range(4):
            for j in range(4):
                src = sets[at][i].at[j] if i < 3 else sets[at][3 + j // 2].at[j % 2]
                yy = jnp.where(side == 0, ys[i], ys[j])
                xx = jnp.where(side == 0, xs_[j], xs_[i])
                lanes = pl.ds(pl.multiple_of(side * C, C), C)
                yield src, w_scr.at[pl.ds(2 * xx, 2), :, yy, :, :, lanes], xx

    for low, high in ((0, 0), (1, 1), (2, 3)):
        for at in range(2):
            for src, dst, xx in place(at):

                @pl.when((xx >= low) & (xx <= high))
                def _(src=src, dst=dst, xx=xx):
                    pltpu.make_async_copy(src, dst, sem_w.at[xx]).start()

    def wait_layers(at):
        for _ in range(8):
            pltpu.make_async_copy(
                sets[0][0].at[0], w_scr.at[0:2, :, 0, :, :, :C], sem_w.at[at]
            ).wait()

    causal, diag, spread, block, tri = masks()

    def keys_of(layer, m):
        parts = [w_scr[layer, m // 2, (m % 2) * 2 + i // 2, i % 2, :ROWS] for i in range(4)]
        return jnp.concatenate(parts, axis=0)

    def forward(layer, stream):
        @pl.when(layer % 2 == 0)
        def _():
            wait_layers(layer // 2)

        rows = assemble_rows(lambda d: w_scr[layer, d // 8, d // 2 % 4, d % 2, ROWS:])
        rows_low = rows.astype(BF16)
        rows_scr[layer] = rows_low
        gain, scale, bias = rows[24:25], rows[25:26], rows[26:27, :T]
        xs[layer] = stream
        x_f = stream.astype(F32)
        inv_rms = lax.rsqrt(jnp.sum(x_f * x_f, axis=1, keepdims=True) * (1.0 / D) + 1e-05)
        normed = (x_f * inv_rms * gain).astype(BF16)
        ns[layer] = normed
        for m in range(BLOCKS):
            sent_ref[layer, T * m : T * (m + 1)] = normed[:, BLOCK * m : BLOCK * (m + 1)]
        logits = nt(normed, rows_low) + bias
        key_query = sum(
            nn(normed[:, BLOCK * m : BLOCK * (m + 1)], keys_of(layer, m)) for m in range(BLOCKS)
        )
        head = iota((T, T), 1) < H
        rate = jnp.maximum(logits, 0.0) + jnp.log1p(jnp.exp(-jnp.abs(logits)))
        rate = jnp.where(head, rate, 0.0)
        keep = 1.0 / (1.0 + rate)
        write = rate * keep
        total = nn(tri, split3(-jnp.log1p(rate)))
        total = total[:, :T] + total[:, T : 2 * T] + total[:, 2 * T : 3 * T]
        wide = nn(jnp.concatenate([split3(total), split3(write)], axis=0), spread)
        total_t, write_t = wide[:T], wide[T:]
        total_s = jnp.sum(jnp.where(diag, total_t, 0.0), axis=0, keepdims=True)
        write_s = jnp.sum(jnp.where(diag, write_t, 0.0), axis=0, keepdims=True)
        decay = jnp.where(causal, jnp.exp(jnp.where(causal, total_t - total_s, 0.0)), 0.0)
        k = key_query[:, :C]
        q = key_query[:, C:]
        inv = lax.rsqrt(jnp.sum(k * k, axis=1, keepdims=True) + 1e-06)
        scores = nt(q.astype(BF16), tile4((k * inv).astype(BF16)))
        decay_scr[layer] = decay
        write_scr[layer] = write_s
        proj_scr[layer] = key_query
        small_scr[layer] = jnp.concatenate([scores, logits, keep, jnp.zeros((T, 64), F32)], axis=1)
        mixing = decay * write_s * jnp.concatenate([scores] * GROUPS, axis=1)
        mixed = unstack_heads(
            [nn(block_diag(mixing, g, block), stack_heads(normed, g)) for g in range(GROUPS)]
        )
        mixed_scr[layer] = mixed.astype(BF16)
        return (x_f + scale * mixed).astype(BF16)

    loads[0].wait()
    loads[1].wait()
    lax.fori_loop(0, LAYERS, forward, first_scr[0], unroll=2)

    def backward(step, back):
        layer = LAYERS - 1 - step
        x_f = xs[layer].astype(F32)
        normed = ns[layer]
        rows_low = rows_scr[layer]
        rows = rows_low[16:].astype(F32)
        gain, scale = rows[8:9], rows[9:10]
        dy = back.astype(F32)
        decay = decay_scr[layer]
        write_s = write_scr[layer]
        small = small_scr[layer]
        scores, logits, keep = small[:, :C], small[:, C : C + T], small[:, C + T : C + 2 * T]
        scores6 = jnp.concatenate([scores] * GROUPS, axis=1)
        mixing = decay * write_s * scores6
        d_scale = jnp.sum(dy * mixed_scr[layer].astype(F32), axis=0, keepdims=True)
        d_out = (dy * scale).astype(BF16)
        d_mix = []
        d_values = []
        for g in range(GROUPS):
            grad = stack_heads(d_out, g)
            full = jnp.where(block, nt(grad, stack_heads(normed, g)), 0.0)
            d_mix.append(full[:T] + full[T : 2 * T] + full[2 * T : 3 * T] + full[3 * T :])
            d_values.append(tn(block_diag(mixing, g, block), grad))
        d_mix = jnp.concatenate(d_mix, axis=1)
        d_values = unstack_heads(d_values)
        near = d_mix * decay
        scored = near * scores6
        d_write_s = jnp.sum(scored, axis=0, keepdims=True)
        weighted = near * write_s
        d_scores = sum(weighted[:, C * g : C * (g + 1)] for g in range(GROUPS)).astype(BF16)
        d_total = scored * write_s - jnp.where(diag, d_write_s * write_s, 0.0)
        gathered = []
        for part in (d_total, jnp.where(diag, d_write_s, 0.0)):
            hi = part.astype(BF16)
            gathered += [hi, (part - hi.astype(F32)).astype(BF16)]
        summed = nt(jnp.concatenate(gathered, axis=0), spread[:T])
        d_total = summed[:T] + summed[T : 2 * T]
        d_write = summed[2 * T : 3 * T] + summed[3 * T :]
        d_log = tn(tri, split3(d_total))
        d_log = d_log[:, :T] + d_log[:, T : 2 * T] + d_log[:, 2 * T : 3 * T]
        d_rate = keep * (d_write * keep - d_log)
        d_logits = d_rate / (1.0 + jnp.exp(-logits))
        d_low = jnp.where(iota((T, T), 1) < H, d_logits, 0.0).astype(BF16)
        k = proj_scr[layer][:, :C]
        q = proj_scr[layer][:, C:]
        inv = lax.rsqrt(jnp.sum(k * k, axis=1, keepdims=True) + 1e-06)
        d_q = nn(d_scores, tile4((k * inv).astype(BF16)))
        d_unit = tn(d_scores, q.astype(BF16))
        d_unit = d_unit[:T] + d_unit[T : 2 * T] + d_unit[2 * T : 3 * T] + d_unit[3 * T :]
        d_k = inv * d_unit - k * (inv * inv * inv * jnp.sum(d_unit * k, axis=1, keepdims=True))
        d_keyq = jnp.concatenate([d_k, d_q], axis=1).astype(BF16)
        through = jnp.concatenate([nt(d_keyq, keys_of(layer, m)) for m in range(BLOCKS)], axis=1)
        d_normed = d_values + through + nn(d_low, rows_low)
        inv_rms = lax.rsqrt(jnp.sum(x_f * x_f, axis=1, keepdims=True) * (1.0 / D) + 1e-05)
        x_hat = x_f * inv_rms
        d_gain = jnp.sum(d_normed * x_hat, axis=0, keepdims=True)
        d_hat = d_normed * gain
        mean = jnp.sum(d_hat * x_hat, axis=1, keepdims=True) * (1.0 / D)
        sent_ref[layer, TOK : TOK + T, :256] = d_keyq
        sent_ref[layer, TOK : TOK + T, 256:] = jnp.concatenate(
            [d_low, jnp.zeros((T, 96), BF16)], axis=1
        )
        sent_ref[layer, TOK + T :] = jnp.concatenate(
            [d[:, BLOCK * i : BLOCK * (i + 1)] for d in (d_gain, d_scale) for i in range(8)], axis=0
        ).astype(BF16)
        return (dy + inv_rms * (d_hat - x_hat * mean)).astype(BF16)

    cot = jnp.where(section < SEQS, first_scr[1].astype(F32), 0.0).astype(BF16)
    lax.fori_loop(0, LAYERS, backward, cot, unroll=2)


def weight_kernel(pos_ref, got_ref, keep_ref, send_ref, got, scr, sem_in, sem):
    y, c, zh = pos_ref[1], pos_ref[2], pos_ref[3]
    loads = []
    for m in list(range(BLOCKS)) + [BLOCKS]:
        at = pl.ds(T * m, T if m < BLOCKS else T + 16)
        loads.append(pltpu.make_async_copy(got_ref.at[:, at], got.at[:, at], sem_in.at[m]))
    loads[-1].start()
    for copy in loads[:-1]:
        copy.start()

    def slot(there, here, core):
        bits = gray(jnp.int32(there)) ^ gray(here)
        return bits if core else (bits & 1) * 2 + (bits >> 1)

    loads[-1].wait()
    tokens = jnp.concatenate([got[s, TOK : TOK + T] for s in range(LAYERS)], axis=0)
    extra = sum(got[s, TOK + T :].astype(F32) for s in range(LAYERS))
    bias = jnp.sum(tokens[:, 256:].astype(F32), axis=0, keepdims=True)
    bias = jnp.concatenate([bias[:, :ROWS]] * 4, axis=1)
    for m in range(BLOCKS):
        loads[m].wait()
        normed = jnp.concatenate([got[s, T * m : T * (m + 1)] for s in range(LAYERS)], axis=0)
        keys = tn(normed, tokens[:, :256])
        rates = tn(tokens[:, 256:], normed)[:H]
        rows = jnp.concatenate(
            [rates, extra[m : m + 1], extra[m + 8 : m + 9], bias, jnp.zeros((5, BLOCK), F32)],
            axis=0,
        )
        low = cut_rows(rows)
        for i in range(4):
            d = 4 * m + i
            y_at, z_at = slot(d // 2 % 4, y, d % 2), slot(d // 8, zh, d % 2)
            c_at = (d + c) % 2
            scr[c_at, y_at, z_at, :ROWS] = keys[ROWS * i : ROWS * (i + 1)].astype(BF16)
            scr[c_at, y_at, z_at, ROWS:] = low[i].astype(BF16)
        if m % 2:
            for core in range(2):
                z_at = slot(m // 2, zh, core)
                for i, ref in enumerate((keep_ref, send_ref)):

                    @pl.when((core + c) % 2 == i)
                    def _(i=i, ref=ref, z_at=z_at):
                        pltpu.make_async_copy(scr.at[i, :, z_at], ref.at[:, z_at], sem.at[i]).start()

    for i, ref in enumerate((keep_ref, send_ref)):
        pltpu.make_async_copy(scr.at[i], ref, sem.at[i]).wait()


def final_kernel(a_ref, b_ref, c_ref, d_ref, scales_ref, keys_ref, rates_ref, bias_ref):
    total = a_ref[...].astype(F32) + b_ref[...].astype(F32)
    total = total + c_ref[...].astype(F32) + d_ref[...].astype(F32)
    keys_ref[...] = total[:ROWS]
    rates = jnp.concatenate([total[ROWS:, :C], total[ROWS:, C:]], axis=0)
    rates_ref[...] = rates[:H, :ROWS]
    scales_ref[...] = rates[24:26, :ROWS]
    bias_ref[...] = rates[26:27, :H]


ANY = pl.BlockSpec(memory_space=pl.ANY)
VMEM = pl.BlockSpec(memory_space=pltpu.VMEM)
SMEM = pl.BlockSpec(memory_space=pltpu.SMEM)
PARAMS = pltpu.CompilerParams(vmem_limit_bytes=56 * 1024 * 1024)


def shape(*dims, dtype=BF16):
    return jax.ShapeDtypeStruct(dims, dtype)


def call(kernel, outs, ins, scratch, out_spec=None, cost=None):
    flops, moved = cost
    return pl.pallas_call(
        kernel,
        out_shape=outs,
        in_specs=ins,
        out_specs=out_spec or [VMEM] * len(outs),
        scratch_shapes=scratch,
        compiler_params=PARAMS,
        cost_estimate=pl.CostEstimate(flops=flops, bytes_accessed=moved, transcendentals=0),
    )


def ring_pairs(first):
    pairs = []
    for i in range(4):
        for c in range(2):
            to = i ^ 1 if (c == 0) == first else 3 - i
            pairs.append((i * 2 + c, to * 2 + c))
    return pairs


def swap(array, axis, first):
    return lax.ppermute(array, (axis, "c"), ring_pairs(first))


def other_core(array):
    return lax.ppermute(array, "c", [(0, 1), (1, 0)])


def opposite(array, axis):
    return lax.ppermute(array, axis, [(i, i ^ 2) for i in range(4)])


def cross(array, of_core, first):
    pairs = []
    for x in range(4):
        for y in range(4):
            for c in range(2):
                to = [x, y]
                axis = of_core[c]
                to[axis] = to[axis] ^ 1 if first else 3 - to[axis]
                pairs.append(((x * 4 + y) * 2 + c, (to[0] * 4 + to[1]) * 2 + c))
    return lax.ppermute(array, ("x", "y", "c"), pairs)


def gather_cross(array, of_core):
    one = cross(array, of_core, True)
    two = cross(array, of_core, False)
    half = array.shape[0] // 2
    return [array, one, two, cross(one[:half], of_core, False), cross(two[half:], of_core, True)]


def add(a, b):
    return (a.astype(F32) + b.astype(F32)).astype(BF16)


def per_device(entries, cotangents, scales, key_weight, rate_weight, rate_bias):
    x, zl, zh, y, c = (lax.axis_index(a) for a in ("x", "zl", "zh", "y", "c"))
    section = x * 2 + zl
    pos = jnp.stack([x, y, c, zh, section]).astype(jnp.int32)

    wide = jnp.pad(rate_weight[0].T, ((0, 0), (0, C - ROWS)))
    small = jnp.pad(scales[0], ((0, 0), (0, C - ROWS)))
    line = jnp.pad(rate_bias, ((0, 0), (0, C - H)))
    right = jnp.concatenate([wide[16:], small, line, jnp.zeros((5, C), BF16)], axis=0)
    packed = jnp.concatenate(
        [key_weight[0], jnp.concatenate([wide[:16], right], axis=1)], axis=0
    )

    left, right = packed[:, :C], packed[:, C:]
    mine = jnp.where(c == 0, left, right)
    theirs = other_core(jnp.where(c == 0, right, left))
    half = jnp.where(c == 0, jnp.stack([mine, theirs]), jnp.stack([theirs, mine]))

    along = [half, swap(half, "zh", True), swap(half, "zh", False), opposite(half, "zh")]
    bits = gray(jnp.arange(4)) ^ gray(zh)
    order = jnp.where(c == 0, bits, jnp.array([0, 2, 1, 3])[bits])
    along = jnp.take(jnp.stack(along), order, axis=0)
    pairs = []
    for z in range(8):
        for core in range(2):
            to = z ^ 1 if core == 0 else (z + 1 if z % 2 else z - 1) % 8
            pairs.append(tuple(((i % 2) * 4 + i // 2) * 2 + core for i in (z, to)))
    other = lax.ppermute(along, ("zl", "zh", "c"), pairs)
    both = jnp.where(zl == 0, jnp.stack([along, other]), jnp.stack([other, along]))

    *three, low, high = gather_cross(both, (0, 1))
    sets = gather_cross(jnp.stack(three + [jnp.concatenate([low, high])]), (1, 0))
    sets = sets + [other_core(a) for a in sets]

    sent = call(
        sequence_kernel,
        [shape(LAYERS, SENT, BLOCK)],
        [SMEM] + [ANY] * 12,
        [
            pltpu.VMEM((LAYERS, 4, 4, 2, PIECE, 256), BF16),
            pltpu.VMEM((LAYERS, T, D), BF16),
            pltpu.VMEM((LAYERS, T, D), BF16),
            pltpu.VMEM((LAYERS, T, D), BF16),
            pltpu.VMEM((LAYERS, T, D), BF16),
            pltpu.VMEM((LAYERS, T, W), F32),
            pltpu.VMEM((LAYERS, 1, W), F32),
            pltpu.VMEM((LAYERS, T, 256), F32),
            pltpu.VMEM((LAYERS, T, 256), F32),
            pltpu.VMEM((2, T, D), BF16),
            pltpu.SemaphoreType.DMA((4,)),
            pltpu.SemaphoreType.DMA((2,)),
        ],
        cost=(8_000_000_000, 30_000_000),
    )(pos, *sets, entries, cotangents)[0]

    groups = [
        [
            (((i * 4) + (z - i % 2 * core) % 4) * 4 + row) * 2 + core
            for i in range(LAYERS)
        ]
        for z in range(4)
        for row in range(4)
        for core in range(2)
    ]
    got = lax.all_to_all(
        sent, ("x", "zl", "zh", "y", "c"), 0, 0, axis_index_groups=groups, tiled=True
    )
    half = shape(4, 4, PIECE, 256)
    keep, send = call(
        weight_kernel,
        [half, half],
        [SMEM, ANY],
        [
            pltpu.VMEM((LAYERS, SENT, BLOCK), BF16),
            pltpu.VMEM((2, 4, 4, PIECE, 256), BF16),
            pltpu.SemaphoreType.DMA((BLOCKS + 1,)),
            pltpu.SemaphoreType.DMA((2,)),
        ],
        [ANY] * 2,
        cost=(600_000_000, 4_000_000),
    )(pos, got)
    got = other_core(send)
    got = swap(add(keep[2:], got[2:]), "y", True), keep[:2], got[:2]
    keep = add(got[1], got[2])
    got = got[0]
    got, keep = swap(add(keep[1], got[1]), "y", False), add(keep[0], got[0])
    got = add(keep, got)
    parts = [
        got[0],
        swap(got[2], "zh", True),
        swap(got[1], "zh", False),
        opposite(got[3], "zh"),
    ]
    g_scales, g_keys, g_rates, g_bias = call(
        final_kernel,
        [
            shape(2, ROWS, dtype=F32),
            shape(ROWS, 256, dtype=F32),
            shape(H, ROWS, dtype=F32),
            shape(1, H, dtype=F32),
        ],
        [VMEM] * 4,
        [],
        cost=(0, 500_000),
    )(*parts)
    return g_scales[None], g_keys[None], g_rates.T[None], g_bias


def solution(mesh):
    fine = Mesh(mesh.devices.reshape(4, 2, 4, 4, 2), ("x", "zl", "zh", "y", "c"))
    placed = (
        P(None, None, DP, None),
        P(None, None, DP, None),
        P(SECTION, None, DP),
        P(SECTION, DP, None),
        P(SECTION, DP, None),
        P(SECTION, None),
    )
    return jax.shard_map(
        per_device,
        mesh=fine,
        in_specs=placed,
        out_specs=(
            P(SECTION, None, DP),
            P(SECTION, DP, None),
            P(SECTION, DP, None),
            P(SECTION, None),
        ),
        check_vma=False,
    )
```

```python
import jax
import jax.numpy as jnp
from jax import lax
from jax.experimental import pallas as pl
from jax.experimental.pallas import tpu as pltpu
from jax.sharding import Mesh, PartitionSpec as P

F32 = jnp.float32
BF16 = jnp.bfloat16
SECTION = ("x", "zl")
DP = ("zh", "y", "c")

T = 32
D = 3072
C = 128
H = 24
GROUPS = H // 4
W = H * T
LAYERS = 8
SEQS = 6
ROWS = 96
PIECE = 112
TOK = LAYERS * T
BLOCK = 384
BLOCKS = D // BLOCK
SENT = BLOCKS * T + T + 16


def iota(shape, axis):
    return lax.broadcasted_iota(jnp.int32, shape, axis)


def nt(a, b):
    return lax.dot_general(
        a, b, (((1,), (1,)), ((), ())), preferred_element_type=F32
    )


def tn(a, b):
    return lax.dot_general(
        a, b, (((0,), (0,)), ((), ())), preferred_element_type=F32
    )


def nn(a, b):
    return jnp.dot(a, b, preferred_element_type=F32)


def split3(a):
    hi = a.astype(BF16)
    rest = a - hi.astype(F32)
    mid = rest.astype(BF16)
    low = (rest - mid.astype(F32)).astype(BF16)
    return jnp.concatenate([hi, mid, low, jnp.zeros_like(hi)], axis=1)


def masks():
    row = iota((T, W), 0)
    col = iota((T, W), 1) % T
    spread = (iota((C, W), 0) % T == iota((C, W), 1) // T) & (iota((C, W), 0) < 3 * T)
    spread = jnp.where(spread, 1.0, 0.0).astype(BF16)
    block = iota((C, C), 0) // T == iota((C, C), 1) // T
    tri = jnp.where(iota((T, T), 0) >= iota((T, T), 1), 1.0, 0.0).astype(BF16)
    tri_back = jnp.where(iota((T, T), 0) <= iota((T, T), 1), 1.0, 0.0).astype(BF16)
    return row >= col, row == col, spread, block, tri, tri_back


def tile4(a):
    return jnp.concatenate([a] * 4, axis=0)


def stack_heads(a, g):
    return jnp.concatenate([a[:, C * (4 * g + j) : C * (4 * g + j + 1)] for j in range(4)], axis=0)


def unstack_heads(parts):
    return jnp.concatenate([p[T * j : T * (j + 1)] for p in parts for j in range(4)], axis=1)


def block_diag(mixing, g, block):
    return jnp.where(block, tile4(mixing[:, C * g : C * (g + 1)]), 0.0).astype(BF16)


def assemble_rows(piece):
    out = []
    lane = iota((T, C), 1)
    for m in range(8):
        p = []
        for i in range(4):
            z = piece(4 * m + i).astype(F32)
            p.append(jnp.concatenate([z[:, :C], z[:, C:]], axis=0))
        p1 = pltpu.roll(p[1], 96, 1)
        p2 = pltpu.roll(p[2], 64, 1)
        p3 = pltpu.roll(p[3], 32, 1)
        out.append(jnp.where(lane < 96, p[0], p1))
        out.append(jnp.where(lane < 64, p1, p2))
        out.append(jnp.where(lane < 32, p2, p3))
    return jnp.concatenate(out, axis=1)


def cut_rows(rows):
    lane = iota((T, C), 1)
    a, b, c = rows[:, :C], rows[:, C : 2 * C], rows[:, 2 * C :]
    one = jnp.where(lane < 32, pltpu.roll(a, 32, 1), pltpu.roll(b, 32, 1))
    two = jnp.where(lane < 64, pltpu.roll(b, 64, 1), pltpu.roll(c, 64, 1))
    parts = [a, one, two, pltpu.roll(c, 96, 1)]
    return [jnp.concatenate([p[:16], p[16:]], axis=1) for p in parts]


def gray(i):
    return jnp.where(i >= 2, 5 - i, i)


def partner(i, c, first):
    return jnp.where((c == 0) == first, i ^ 1, 3 - i)


def sequence_kernel(*refs):
    left, right = refs[:8], refs[8:16]
    entry_ref, cot_ref, out_ref = refs[16:19]
    w_scr, rows_scr, xs, ns, mixed_scr, decay_scr, write_scr, small_scr, proj_scr = refs[19:28]
    first_scr, sent_ref, sem_a, sem_b, sem_c, sem_out = refs[28:]

    def send(layer, rows):
        pltpu.make_async_copy(sent_ref.at[layer, rows], out_ref.at[layer, rows], sem_out).start()

    x, y, c = (lax.axis_index(a) for a in ("x", "y", "c"))
    section = x * 2 + lax.axis_index("zl")
    mine = jnp.minimum(section, SEQS - 1)
    loads = []
    for i, ref in enumerate((entry_ref, cot_ref)):
        copy = pltpu.make_async_copy(
            ref.at[mine // 3, mine % 3], first_scr.at[i], sem_c.at[i]
        )
        copy.start()
        loads.append(copy)

    def ring(i, core):
        one, two = partner(i, core, True), partner(i, core, False)
        return [i, one, two, partner(two, core, True)]

    for target in range(4):
        for kc in range(2):
            cc = (c + kc) % 2
            ys, xx = ring(y, cc), ring(x, cc)
            slot = sum(jnp.where(xx[j] == target, j, 0) for j in range(4))
            for i in range(4):
                pltpu.make_async_copy(
                    left[kc * 4 + i].at[slot],
                    w_scr.at[2 * target : 2 * target + 2, :, ys[i], cc, :, :C],
                    sem_a.at[target],
                ).start()

                @pl.when(xx[i] == target)
                def _(i=i, kc=kc, cc=cc, ys=ys, target=target):
                    for j in range(4):
                        pltpu.make_async_copy(
                            right[kc * 4 + i].at[j],
                            w_scr.at[2 * target : 2 * target + 2, :, ys[j], cc, :, C:],
                            sem_b.at[target],
                        ).start()

    def wait_layers(at):
        for sem, src in ((sem_a, left[0]), (sem_b, right[0])):
            for _ in range(8):
                pltpu.make_async_copy(
                    src.at[0], w_scr.at[0:2, :, 0, 0, :, :C], sem.at[at]
                ).wait()

    causal, diag, spread, block, tri, tri_back = masks()

    def keys_of(layer, m):
        parts = [w_scr[layer, m // 2, (m % 2) * 2 + i // 2, i % 2, :ROWS] for i in range(4)]
        return jnp.concatenate(parts, axis=0)

    def forward(layer, stream):
        @pl.when(layer % 2 == 0)
        def _():
            wait_layers(layer // 2)

        rows = assemble_rows(lambda d: w_scr[layer, d // 8, d // 2 % 4, d % 2, ROWS:])
        rows_low = rows.astype(BF16)
        rows_scr[layer] = rows_low
        gain, scale, bias = rows[24:25], rows[25:26], rows[26:27, :T]
        xs[layer] = stream
        x_f = stream.astype(F32)
        inv_rms = lax.rsqrt(jnp.sum(x_f * x_f, axis=1, keepdims=True) * (1.0 / D) + 1e-05)
        normed = (x_f * inv_rms * gain).astype(BF16)
        ns[layer] = normed
        for m in range(BLOCKS):
            sent_ref[layer, T * m : T * (m + 1)] = normed[:, BLOCK * m : BLOCK * (m + 1)]
        send(layer, pl.ds(0, TOK))
        logits = nt(normed, rows_low) + bias
        key_query = sum(
            nn(normed[:, BLOCK * m : BLOCK * (m + 1)], keys_of(layer, m)) for m in range(BLOCKS)
        )
        head = iota((T, T), 1) < H
        rate = jnp.maximum(logits, 0.0) + jnp.log1p(jnp.exp(-jnp.abs(logits)))
        rate = jnp.where(head, rate, 0.0)
        keep = 1.0 / (1.0 + rate)
        write = rate * keep
        total = nn(tri, split3(-jnp.log1p(rate)))
        total = total[:, :T] + total[:, T : 2 * T] + total[:, 2 * T : 3 * T]
        wide = nn(jnp.concatenate([split3(total), split3(write)], axis=0), spread)
        total_t, write_t = wide[:T], wide[T:]
        total_s = jnp.sum(jnp.where(diag, total_t, 0.0), axis=0, keepdims=True)
        write_s = jnp.sum(jnp.where(diag, write_t, 0.0), axis=0, keepdims=True)
        decay = jnp.where(causal, jnp.exp(jnp.where(causal, total_t - total_s, 0.0)), 0.0)
        k = key_query[:, :C]
        q = key_query[:, C:]
        inv = lax.rsqrt(jnp.sum(k * k, axis=1, keepdims=True) + 1e-06)
        scores = nt(q.astype(BF16), tile4((k * inv).astype(BF16)))
        decay_scr[layer] = decay
        write_scr[layer] = write_s
        proj_scr[layer] = key_query
        small_scr[layer] = jnp.concatenate([scores, logits, keep, jnp.zeros((T, 64), F32)], axis=1)
        mixing = decay * write_s * jnp.concatenate([scores] * GROUPS, axis=1)
        mixed = unstack_heads(
            [nn(block_diag(mixing, g, block), stack_heads(normed, g)) for g in range(GROUPS)]
        )
        mixed_scr[layer] = mixed.astype(BF16)
        return (x_f + scale * mixed).astype(BF16)

    loads[0].wait()
    loads[1].wait()
    lax.fori_loop(0, LAYERS, forward, first_scr[0], unroll=2)

    def backward(step, back):
        layer = LAYERS - 1 - step
        x_f = xs[layer].astype(F32)
        normed = ns[layer]
        rows_low = rows_scr[layer]
        rows = rows_low[16:].astype(F32)
        gain, scale = rows[8:9], rows[9:10]
        dy = back.astype(F32)
        decay = decay_scr[layer]
        write_s = write_scr[layer]
        small = small_scr[layer]
        scores, logits, keep = small[:, :C], small[:, C : C + T], small[:, C + T : C + 2 * T]
        scores6 = jnp.concatenate([scores] * GROUPS, axis=1)
        mixing = decay * write_s * scores6
        d_scale = jnp.sum(dy * mixed_scr[layer].astype(F32), axis=0, keepdims=True)
        d_out = (dy * scale).astype(BF16)
        d_mix = []
        d_values = []
        for g in range(GROUPS):
            grad = stack_heads(d_out, g)
            full = jnp.where(block, nt(grad, stack_heads(normed, g)), 0.0)
            d_mix.append(full[:T] + full[T : 2 * T] + full[2 * T : 3 * T] + full[3 * T :])
            d_values.append(tn(block_diag(mixing, g, block), grad))
        d_mix = jnp.concatenate(d_mix, axis=1)
        d_values = unstack_heads(d_values)
        near = d_mix * decay
        scored = near * scores6
        d_write_s = jnp.sum(scored, axis=0, keepdims=True)
        weighted = near * write_s
        d_scores = sum(weighted[:, C * g : C * (g + 1)] for g in range(GROUPS)).astype(BF16)
        later = jnp.where(causal & ~diag, nn(tri_back, (scored * write_s).astype(BF16)), 0.0)
        own = jnp.where(diag, d_write_s, 0.0)
        summed = nt(jnp.concatenate([later.astype(BF16), own.astype(BF16)], axis=0), spread[:T])
        d_log, d_write = summed[:T], summed[T:]
        d_rate = keep * (d_write * keep - d_log)
        d_logits = d_rate / (1.0 + jnp.exp(-logits))
        d_low = jnp.where(iota((T, T), 1) < H, d_logits, 0.0).astype(BF16)
        k = proj_scr[layer][:, :C]
        q = proj_scr[layer][:, C:]
        inv = lax.rsqrt(jnp.sum(k * k, axis=1, keepdims=True) + 1e-06)
        d_q = nn(d_scores, tile4((k * inv).astype(BF16)))
        d_unit = tn(d_scores, q.astype(BF16))
        d_unit = d_unit[:T] + d_unit[T : 2 * T] + d_unit[2 * T : 3 * T] + d_unit[3 * T :]
        d_k = inv * d_unit - k * (inv * inv * inv * jnp.sum(d_unit * k, axis=1, keepdims=True))
        d_keyq = jnp.concatenate([d_k, d_q], axis=1).astype(BF16)
        through = jnp.concatenate([nt(d_keyq, keys_of(layer, m)) for m in range(BLOCKS)], axis=1)
        d_normed = d_values + through + nn(d_low, rows_low)
        inv_rms = lax.rsqrt(jnp.sum(x_f * x_f, axis=1, keepdims=True) * (1.0 / D) + 1e-05)
        x_hat = x_f * inv_rms
        d_gain = jnp.sum(d_normed * x_hat, axis=0, keepdims=True)
        d_hat = d_normed * gain
        mean = jnp.sum(d_hat * x_hat, axis=1, keepdims=True) * (1.0 / D)
        sent_ref[layer, TOK : TOK + T, :256] = d_keyq
        sent_ref[layer, TOK : TOK + T, 256:] = jnp.concatenate(
            [d_low, jnp.zeros((T, 96), BF16)], axis=1
        )
        sent_ref[layer, TOK + T :] = jnp.concatenate(
            [d[:, BLOCK * i : BLOCK * (i + 1)] for d in (d_gain, d_scale) for i in range(8)], axis=0
        ).astype(BF16)
        send(layer, pl.ds(TOK, T + 16))
        return (dy + inv_rms * (d_hat - x_hat * mean)).astype(BF16)

    cot = jnp.where(section < SEQS, first_scr[1].astype(F32), 0.0).astype(BF16)
    lax.fori_loop(0, LAYERS, backward, cot, unroll=2)
    pltpu.make_async_copy(sent_ref, out_ref, sem_out).wait()


def weight_kernel(got_ref, keep_ref, send_ref, got, scr, sem_in, sem):
    y, c, zh = (lax.axis_index(a) for a in ("y", "c", "zh"))
    loads = []
    for m in list(range(BLOCKS)) + [BLOCKS]:
        at = pl.ds(T * m, T if m < BLOCKS else T + 16)
        loads.append(pltpu.make_async_copy(got_ref.at[:, at], got.at[:, at], sem_in.at[m]))
    loads[-1].start()
    for copy in loads[:-1]:
        copy.start()

    def slot(there, here, core):
        bits = gray(jnp.int32(there)) ^ gray(here)
        return bits if core else (bits & 1) * 2 + (bits >> 1)

    loads[-1].wait()
    tokens = jnp.concatenate([got[s, TOK : TOK + T] for s in range(LAYERS)], axis=0)
    extra = sum(got[s, TOK + T :].astype(F32) for s in range(LAYERS))
    bias = jnp.sum(tokens[:, 256:].astype(F32), axis=0, keepdims=True)
    bias = jnp.concatenate([bias[:, :ROWS]] * 4, axis=1)
    for m in range(BLOCKS):
        loads[m].wait()
        normed = jnp.concatenate([got[s, T * m : T * (m + 1)] for s in range(LAYERS)], axis=0)
        keys = tn(normed, tokens[:, :256])
        rates = tn(tokens[:, 256:], normed)[:H]
        rows = jnp.concatenate(
            [rates, extra[m : m + 1], extra[m + 8 : m + 9], bias, jnp.zeros((5, BLOCK), F32)],
            axis=0,
        )
        low = cut_rows(rows)
        for i in range(4):
            d = 4 * m + i
            y_at, z_at = slot(d // 2 % 4, y, d % 2), slot(d // 8, zh, d % 2)
            c_at = (d + c) % 2
            scr[c_at, y_at, z_at, :ROWS] = keys[ROWS * i : ROWS * (i + 1)].astype(BF16)
            scr[c_at, y_at, z_at, ROWS:] = low[i].astype(BF16)
        if m % 2:
            for core in range(2):
                z_at = slot(m // 2, zh, core)
                for i, ref in enumerate((keep_ref, send_ref)):

                    @pl.when((core + c) % 2 == i)
                    def _(i=i, ref=ref, z_at=z_at):
                        pltpu.make_async_copy(scr.at[i, :, z_at], ref.at[:, z_at], sem.at[i]).start()

    for i, ref in enumerate((keep_ref, send_ref)):
        pltpu.make_async_copy(scr.at[i], ref, sem.at[i]).wait()


def final_kernel(a_ref, b_ref, c_ref, d_ref, scales_ref, keys_ref, rates_ref, bias_ref):
    total = a_ref[...].astype(F32) + b_ref[...].astype(F32)
    total = total + c_ref[...].astype(F32) + d_ref[...].astype(F32)
    keys_ref[...] = total[:ROWS]
    rates = jnp.concatenate([total[ROWS:, :C], total[ROWS:, C:]], axis=0)
    rates_ref[...] = rates[:H, :ROWS]
    scales_ref[...] = rates[24:26, :ROWS]
    bias_ref[...] = rates[26:27, :H]


ANY = pl.BlockSpec(memory_space=pl.ANY)
VMEM = pl.BlockSpec(memory_space=pltpu.VMEM)
PARAMS = pltpu.CompilerParams(vmem_limit_bytes=56 * 1024 * 1024)


def shape(*dims, dtype=BF16):
    return jax.ShapeDtypeStruct(dims, dtype)


def call(kernel, outs, ins, scratch, out_spec=None, cost=None):
    flops, moved = cost
    return pl.pallas_call(
        kernel,
        out_shape=outs,
        in_specs=ins,
        out_specs=out_spec or [VMEM] * len(outs),
        scratch_shapes=scratch,
        compiler_params=PARAMS,
        cost_estimate=pl.CostEstimate(flops=flops, bytes_accessed=moved, transcendentals=0),
    )


def ring_pairs(first):
    pairs = []
    for i in range(4):
        for c in range(2):
            to = i ^ 1 if (c == 0) == first else 3 - i
            pairs.append((i * 2 + c, to * 2 + c))
    return pairs


def swap(array, axis, first):
    return lax.ppermute(array, (axis, "c"), ring_pairs(first))


def other_core(array):
    return lax.ppermute(array, "c", [(0, 1), (1, 0)])


def opposite(array, axis):
    return lax.ppermute(array, axis, [(i, i ^ 2) for i in range(4)])


def gather_ring(array, axis, direct=False):
    one = swap(array, axis, True)
    two = swap(array, axis, False)
    return [array, one, two, opposite(array, axis) if direct else swap(one, axis, False)]


def add(a, b):
    return (a.astype(F32) + b.astype(F32)).astype(BF16)


def per_device(entries, cotangents, scales, key_weight, rate_weight, rate_bias):
    x, zl, zh, y, c = (lax.axis_index(a) for a in ("x", "zl", "zh", "y", "c"))
    rates = rate_weight[0].T
    packed = sum(
        jnp.pad(a, ((row, PIECE - row - a.shape[0]), (lane, 256 - lane - a.shape[1])))
        for a, row, lane in (
            (key_weight[0], 0, 0),
            (rates[:16], ROWS, 0),
            (rates[16:], ROWS, C),
            (scales[0], ROWS + 8, C),
            (rate_bias, ROWS + 10, C),
        )
    )

    along = jnp.stack(gather_ring(packed, "zh", direct=True))
    first, second = partner(zh, c, True), partner(zh, c, False)
    across = partner(second, c, True)
    order = [jnp.where(j == first, 1, jnp.where(j == second, 2, jnp.where(j == across, 3, 0))) for j in range(4)]
    along = jnp.take(along, jnp.stack(order), axis=0)
    pairs = []
    for z in range(8):
        for core in range(2):
            to = z ^ 1 if core == 0 else (z + 1 if z % 2 else z - 1) % 8
            pairs.append(tuple(((i % 2) * 4 + i // 2) * 2 + core for i in (z, to)))
    other = lax.ppermute(along, ("zl", "zh", "c"), pairs)
    both = jnp.where(zl == 0, jnp.stack([along, other]), jnp.stack([other, along]))

    left = jnp.stack(gather_ring(both[..., :C], "x"))
    right = jnp.stack(gather_ring(both[..., C:], "y"))
    left = gather_ring(left, "y")
    right = gather_ring(right, "x")
    left = left + [other_core(a) for a in left]
    right = right + [other_core(a) for a in right]

    sent = call(
        sequence_kernel,
        [shape(LAYERS, SENT, BLOCK)],
        [ANY] * 18,
        [
            pltpu.VMEM((LAYERS, 4, 4, 2, PIECE, 256), BF16),
            pltpu.VMEM((LAYERS, T, D), BF16),
            pltpu.VMEM((LAYERS, T, D), BF16),
            pltpu.VMEM((LAYERS, T, D), BF16),
            pltpu.VMEM((LAYERS, T, D), BF16),
            pltpu.VMEM((LAYERS, T, W), F32),
            pltpu.VMEM((LAYERS, 1, W), F32),
            pltpu.VMEM((LAYERS, T, 256), F32),
            pltpu.VMEM((LAYERS, T, 256), F32),
            pltpu.VMEM((2, T, D), BF16),
            pltpu.VMEM((LAYERS, SENT, BLOCK), BF16),
            pltpu.SemaphoreType.DMA((4,)),
            pltpu.SemaphoreType.DMA((4,)),
            pltpu.SemaphoreType.DMA((2,)),
            pltpu.SemaphoreType.DMA,
        ],
        [ANY],
        cost=(8_000_000_000, 30_000_000),
    )(*left, *right, entries, cotangents)[0]

    groups = [
        [
            (((i * 4) + (z - i % 2 * core) % 4) * 4 + row) * 2 + core
            for i in range(LAYERS)
        ]
        for z in range(4)
        for row in range(4)
        for core in range(2)
    ]
    got = lax.all_to_all(
        sent, ("x", "zl", "zh", "y", "c"), 0, 0, axis_index_groups=groups, tiled=True
    )
    half = shape(4, 4, PIECE, 256)
    keep, send = call(
        weight_kernel,
        [half, half],
        [ANY],
        [
            pltpu.VMEM((LAYERS, SENT, BLOCK), BF16),
            pltpu.VMEM((2, 4, 4, PIECE, 256), BF16),
            pltpu.SemaphoreType.DMA((BLOCKS + 1,)),
            pltpu.SemaphoreType.DMA((2,)),
        ],
        [ANY] * 2,
        cost=(600_000_000, 4_000_000),
    )(got)
    got = other_core(send)
    got = swap(add(keep[2:], got[2:]), "y", True), keep[:2], got[:2]
    keep = add(got[1], got[2])
    got = got[0]
    got, keep = swap(add(keep[1], got[1]), "y", False), add(keep[0], got[0])
    got = add(keep, got)
    parts = [
        got[0],
        swap(got[2], "zh", True),
        swap(got[1], "zh", False),
        opposite(got[3], "zh"),
    ]
    g_scales, g_keys, g_rates, g_bias = call(
        final_kernel,
        [
            shape(2, ROWS, dtype=F32),
            shape(ROWS, 256, dtype=F32),
            shape(H, ROWS, dtype=F32),
            shape(1, H, dtype=F32),
        ],
        [VMEM] * 4,
        [],
        cost=(0, 500_000),
    )(*parts)
    return g_scales[None], g_keys[None], g_rates.T[None], g_bias


def solution(mesh):
    fine = Mesh(mesh.devices.reshape(4, 2, 4, 4, 2), ("x", "zl", "zh", "y", "c"))
    placed = (
        P(None, None, DP, None),
        P(None, None, DP, None),
        P(SECTION, None, DP),
        P(SECTION, DP, None),
        P(SECTION, DP, None),
        P(SECTION, None),
    )
    return jax.shard_map(
        per_device,
        mesh=fine,
        in_specs=placed,
        out_specs=(
            P(SECTION, None, DP),
            P(SECTION, DP, None),
            P(SECTION, DP, None),
            P(SECTION, None),
        ),
        check_vma=False,
    )
```

```python
import jax
import jax.numpy as jnp
from jax import lax
from jax.experimental import pallas as pl
from jax.experimental.pallas import tpu as pltpu
from jax.sharding import Mesh, PartitionSpec as P

F32 = jnp.float32
BF16 = jnp.bfloat16
SECTION = ("x", "zl")
DP = ("zh", "y", "c")

T = 32
D = 3072
C = 128
H = 24
GROUPS = H // 4
W = H * T
LAYERS = 8
SEQS = 6
ROWS = 96
PIECE = 112
TOK = LAYERS * T
BLOCK = 384
BLOCKS = D // BLOCK
SENT = BLOCKS * T + T + 16


def iota(shape, axis):
    return lax.broadcasted_iota(jnp.int32, shape, axis)


def nt(a, b):
    return lax.dot_general(
        a, b, (((1,), (1,)), ((), ())), preferred_element_type=F32
    )


def tn(a, b):
    return lax.dot_general(
        a, b, (((0,), (0,)), ((), ())), preferred_element_type=F32
    )


def nn(a, b):
    return jnp.dot(a, b, preferred_element_type=F32)


def split3(a):
    hi = a.astype(BF16)
    rest = a - hi.astype(F32)
    mid = rest.astype(BF16)
    low = (rest - mid.astype(F32)).astype(BF16)
    return jnp.concatenate([hi, mid, low, jnp.zeros_like(hi)], axis=1)


def masks():
    row = iota((T, W), 0)
    col = iota((T, W), 1) % T
    spread = (iota((C, W), 0) % T == iota((C, W), 1) // T) & (iota((C, W), 0) < 3 * T)
    spread = jnp.where(spread, 1.0, 0.0).astype(BF16)
    block = iota((C, C), 0) // T == iota((C, C), 1) // T
    tri = jnp.where(iota((T, T), 0) >= iota((T, T), 1), 1.0, 0.0).astype(BF16)
    tri_back = jnp.where(iota((T, T), 0) <= iota((T, T), 1), 1.0, 0.0).astype(BF16)
    return row >= col, row == col, spread, block, tri, tri_back


def tile4(a):
    return jnp.concatenate([a] * 4, axis=0)


def stack_heads(a, g):
    return jnp.concatenate([a[:, C * (4 * g + j) : C * (4 * g + j + 1)] for j in range(4)], axis=0)


def unstack_heads(parts):
    return jnp.concatenate([p[T * j : T * (j + 1)] for p in parts for j in range(4)], axis=1)


def block_diag(mixing, g, block):
    return jnp.where(block, tile4(mixing[:, C * g : C * (g + 1)]), 0.0).astype(BF16)


def assemble_rows(piece):
    out = []
    lane = iota((T, C), 1)
    for m in range(8):
        p = []
        for i in range(4):
            z = piece(4 * m + i).astype(F32)
            p.append(jnp.concatenate([z[:, :C], z[:, C:]], axis=0))
        p1 = pltpu.roll(p[1], 96, 1)
        p2 = pltpu.roll(p[2], 64, 1)
        p3 = pltpu.roll(p[3], 32, 1)
        out.append(jnp.where(lane < 96, p[0], p1))
        out.append(jnp.where(lane < 64, p1, p2))
        out.append(jnp.where(lane < 32, p2, p3))
    return jnp.concatenate(out, axis=1)


def cut_rows(rows):
    lane = iota((T, C), 1)
    a, b, c = rows[:, :C], rows[:, C : 2 * C], rows[:, 2 * C :]
    one = jnp.where(lane < 32, pltpu.roll(a, 32, 1), pltpu.roll(b, 32, 1))
    two = jnp.where(lane < 64, pltpu.roll(b, 64, 1), pltpu.roll(c, 64, 1))
    parts = [a, one, two, pltpu.roll(c, 96, 1)]
    return [jnp.concatenate([p[:16], p[16:]], axis=1) for p in parts]


def gray(i):
    return jnp.where(i >= 2, 5 - i, i)


def partner(i, c, first):
    return jnp.where((c == 0) == first, i ^ 1, 3 - i)


def sequence_kernel(*refs):
    left, right = refs[:8], refs[8:16]
    entry_ref, cot_ref, out_ref = refs[16:19]
    w_scr, rows_scr, xs, ns, mixed_scr, decay_scr, write_scr, small_scr, proj_scr = refs[19:28]
    first_scr, sent_ref, sem_a, sem_b, sem_c, sem_out = refs[28:]

    def send(layer, rows):
        pltpu.make_async_copy(sent_ref.at[layer, rows], out_ref.at[layer, rows], sem_out).start()

    x, y, c = (lax.axis_index(a) for a in ("x", "y", "c"))
    section = x * 2 + lax.axis_index("zl")
    mine = jnp.minimum(section, SEQS - 1)
    loads = []
    for i, ref in enumerate((entry_ref, cot_ref)):
        copy = pltpu.make_async_copy(
            ref.at[mine // 3, mine % 3], first_scr.at[i], sem_c.at[i]
        )
        copy.start()
        loads.append(copy)

    def ring(i, core):
        one, two = partner(i, core, True), partner(i, core, False)
        return [i, one, two, partner(two, core, True)]

    for target in range(4):
        for kc in range(2):
            cc = (c + kc) % 2
            ys, xx = ring(y, cc), ring(x, cc)
            slot = sum(jnp.where(xx[j] == target, j, 0) for j in range(4))
            for i in range(4):
                pltpu.make_async_copy(
                    left[kc * 4 + i].at[slot],
                    w_scr.at[2 * target : 2 * target + 2, :, ys[i], cc, :, :C],
                    sem_a.at[target],
                ).start()

                @pl.when(xx[i] == target)
                def _(i=i, kc=kc, cc=cc, ys=ys, target=target):
                    for j in range(4):
                        pltpu.make_async_copy(
                            right[kc * 4 + i].at[j],
                            w_scr.at[2 * target : 2 * target + 2, :, ys[j], cc, :, C:],
                            sem_b.at[target],
                        ).start()

    def wait_layers(at):
        for sem, src in ((sem_a, left[0]), (sem_b, right[0])):
            for _ in range(8):
                pltpu.make_async_copy(
                    src.at[0], w_scr.at[0:2, :, 0, 0, :, :C], sem.at[at]
                ).wait()

    causal, diag, spread, block, tri, tri_back = masks()

    def keys_of(layer, m):
        parts = [w_scr[layer, m // 2, (m % 2) * 2 + i // 2, i % 2, :ROWS] for i in range(4)]
        return jnp.concatenate(parts, axis=0)

    def forward(layer, stream):
        @pl.when(layer % 2 == 0)
        def _():
            wait_layers(layer // 2)

        rows = assemble_rows(lambda d: w_scr[layer, d // 8, d // 2 % 4, d % 2, ROWS:])
        rows_low = rows.astype(BF16)
        rows_scr[layer] = rows_low
        gain, scale, bias = rows[24:25], rows[25:26], rows[26:27, :T]
        xs[layer] = stream
        x_f = stream.astype(F32)
        inv_rms = lax.rsqrt(jnp.sum(x_f * x_f, axis=1, keepdims=True) * (1.0 / D) + 1e-05)
        normed = (x_f * inv_rms * gain).astype(BF16)
        ns[layer] = normed
        for m in range(BLOCKS):
            sent_ref[layer, T * m : T * (m + 1)] = normed[:, BLOCK * m : BLOCK * (m + 1)]
        send(layer, pl.ds(0, TOK))
        logits = nt(normed, rows_low) + bias
        key_query = sum(
            nn(normed[:, BLOCK * m : BLOCK * (m + 1)], keys_of(layer, m)) for m in range(BLOCKS)
        )
        head = iota((T, T), 1) < H
        rate = jnp.maximum(logits, 0.0) + jnp.log1p(jnp.exp(-jnp.abs(logits)))
        rate = jnp.where(head, rate, 0.0)
        keep = 1.0 / (1.0 + rate)
        write = rate * keep
        total = nn(tri, split3(-jnp.log1p(rate)))
        total = total[:, :T] + total[:, T : 2 * T] + total[:, 2 * T : 3 * T]
        wide = nn(jnp.concatenate([split3(total), split3(write)], axis=0), spread)
        total_t, write_t = wide[:T], wide[T:]
        total_s = jnp.sum(jnp.where(diag, total_t, 0.0), axis=0, keepdims=True)
        write_s = jnp.sum(jnp.where(diag, write_t, 0.0), axis=0, keepdims=True)
        decay = jnp.where(causal, jnp.exp(jnp.where(causal, total_t - total_s, 0.0)), 0.0)
        k = key_query[:, :C]
        q = key_query[:, C:]
        inv = lax.rsqrt(jnp.sum(k * k, axis=1, keepdims=True) + 1e-06)
        scores = nt(q.astype(BF16), tile4((k * inv).astype(BF16)))
        decay_scr[layer] = decay
        write_scr[layer] = write_s
        proj_scr[layer] = key_query
        small_scr[layer] = jnp.concatenate([scores, logits, keep, jnp.zeros((T, 64), F32)], axis=1)
        mixing = decay * write_s * jnp.concatenate([scores] * GROUPS, axis=1)
        mixed = unstack_heads(
            [nn(block_diag(mixing, g, block), stack_heads(normed, g)) for g in range(GROUPS)]
        )
        mixed_scr[layer] = mixed.astype(BF16)
        return (x_f + scale * mixed).astype(BF16)

    loads[0].wait()
    loads[1].wait()
    lax.fori_loop(0, LAYERS, forward, first_scr[0], unroll=2)

    def backward(step, back):
        layer = LAYERS - 1 - step
        x_f = xs[layer].astype(F32)
        normed = ns[layer]
        rows_low = rows_scr[layer]
        rows = rows_low[16:].astype(F32)
        gain, scale = rows[8:9], rows[9:10]
        dy = back.astype(F32)
        decay = decay_scr[layer]
        write_s = write_scr[layer]
        small = small_scr[layer]
        scores, logits, keep = small[:, :C], small[:, C : C + T], small[:, C + T : C + 2 * T]
        scores6 = jnp.concatenate([scores] * GROUPS, axis=1)
        mixing = decay * write_s * scores6
        d_scale = jnp.sum(dy * mixed_scr[layer].astype(F32), axis=0, keepdims=True)
        d_out = (dy * scale).astype(BF16)
        d_mix = []
        d_values = []
        for g in range(GROUPS):
            grad = stack_heads(d_out, g)
            full = jnp.where(block, nt(grad, stack_heads(normed, g)), 0.0)
            d_mix.append(full[:T] + full[T : 2 * T] + full[2 * T : 3 * T] + full[3 * T :])
            d_values.append(tn(block_diag(mixing, g, block), grad))
        d_mix = jnp.concatenate(d_mix, axis=1)
        d_values = unstack_heads(d_values)
        near = d_mix * decay
        scored = near * scores6
        d_write_s = jnp.sum(scored, axis=0, keepdims=True)
        weighted = near * write_s
        d_scores = sum(weighted[:, C * g : C * (g + 1)] for g in range(GROUPS)).astype(BF16)
        later = jnp.where(causal & ~diag, nn(tri_back, (scored * write_s).astype(BF16)), 0.0)
        own = jnp.where(diag, d_write_s, 0.0)
        summed = nt(jnp.concatenate([later.astype(BF16), own.astype(BF16)], axis=0), spread[:T])
        d_log, d_write = summed[:T], summed[T:]
        d_rate = keep * (d_write * keep - d_log)
        d_logits = d_rate / (1.0 + jnp.exp(-logits))
        d_low = jnp.where(iota((T, T), 1) < H, d_logits, 0.0).astype(BF16)
        k = proj_scr[layer][:, :C]
        q = proj_scr[layer][:, C:]
        inv = lax.rsqrt(jnp.sum(k * k, axis=1, keepdims=True) + 1e-06)
        d_q = nn(d_scores, tile4((k * inv).astype(BF16)))
        d_unit = tn(d_scores, q.astype(BF16))
        d_unit = d_unit[:T] + d_unit[T : 2 * T] + d_unit[2 * T : 3 * T] + d_unit[3 * T :]
        d_k = inv * d_unit - k * (inv * inv * inv * jnp.sum(d_unit * k, axis=1, keepdims=True))
        d_keyq = jnp.concatenate([d_k, d_q], axis=1).astype(BF16)
        through = jnp.concatenate([nt(d_keyq, keys_of(layer, m)) for m in range(BLOCKS)], axis=1)
        d_normed = d_values + through + nn(d_low, rows_low)
        inv_rms = lax.rsqrt(jnp.sum(x_f * x_f, axis=1, keepdims=True) * (1.0 / D) + 1e-05)
        x_hat = x_f * inv_rms
        d_gain = jnp.sum(d_normed * x_hat, axis=0, keepdims=True)
        d_hat = d_normed * gain
        mean = jnp.sum(d_hat * x_hat, axis=1, keepdims=True) * (1.0 / D)
        sent_ref[layer, TOK : TOK + T, :256] = d_keyq
        sent_ref[layer, TOK : TOK + T, 256:] = jnp.concatenate(
            [d_low, jnp.zeros((T, 96), BF16)], axis=1
        )
        sent_ref[layer, TOK + T :] = jnp.concatenate(
            [d[:, BLOCK * i : BLOCK * (i + 1)] for d in (d_gain, d_scale) for i in range(8)], axis=0
        ).astype(BF16)
        send(layer, pl.ds(TOK, T + 16))
        return (dy + inv_rms * (d_hat - x_hat * mean)).astype(BF16)

    cot = jnp.where(section < SEQS, first_scr[1].astype(F32), 0.0).astype(BF16)
    lax.fori_loop(0, LAYERS, backward, cot, unroll=2)
    pltpu.make_async_copy(sent_ref, out_ref, sem_out).wait()


def weight_kernel(got_ref, keep_ref, send_ref, got, scr, sem_in, sem):
    y, c, zh = (lax.axis_index(a) for a in ("y", "c", "zh"))
    loads = []
    for m in list(range(BLOCKS)) + [BLOCKS]:
        at = pl.ds(T * m, T if m < BLOCKS else T + 16)
        loads.append(pltpu.make_async_copy(got_ref.at[:, at], got.at[:, at], sem_in.at[m]))
    loads[-1].start()
    for copy in loads[:-1]:
        copy.start()

    def slot(there, here, core):
        bits = gray(jnp.int32(there)) ^ gray(here)
        return bits if core else (bits & 1) * 2 + (bits >> 1)

    loads[-1].wait()
    tokens = jnp.concatenate([got[s, TOK : TOK + T] for s in range(LAYERS)], axis=0)
    extra = sum(got[s, TOK + T :].astype(F32) for s in range(LAYERS))
    bias = jnp.sum(tokens[:, 256:].astype(F32), axis=0, keepdims=True)
    bias = jnp.concatenate([bias[:, :ROWS]] * 4, axis=1)
    for m in range(BLOCKS):
        loads[m].wait()
        normed = jnp.concatenate([got[s, T * m : T * (m + 1)] for s in range(LAYERS)], axis=0)
        keys = tn(normed, tokens[:, :256])
        rates = tn(tokens[:, 256:], normed)[:H]
        rows = jnp.concatenate(
            [rates, extra[m : m + 1], extra[m + 8 : m + 9], bias, jnp.zeros((5, BLOCK), F32)],
            axis=0,
        )
        low = cut_rows(rows)
        for i in range(4):
            d = 4 * m + i
            y_at, z_at = slot(d // 2 % 4, y, d % 2), slot(d // 8, zh, d % 2)
            c_at = (d + c) % 2
            scr[c_at, y_at, z_at, :ROWS] = keys[ROWS * i : ROWS * (i + 1)].astype(BF16)
            scr[c_at, y_at, z_at, ROWS:] = low[i].astype(BF16)
        if m % 2:
            for core in range(2):
                z_at = slot(m // 2, zh, core)
                for i, ref in enumerate((keep_ref, send_ref)):

                    @pl.when((core + c) % 2 == i)
                    def _(i=i, ref=ref, z_at=z_at):
                        pltpu.make_async_copy(scr.at[i, :, z_at], ref.at[:, z_at], sem.at[i]).start()

    for i, ref in enumerate((keep_ref, send_ref)):
        pltpu.make_async_copy(scr.at[i], ref, sem.at[i]).wait()


def final_kernel(a_ref, b_ref, c_ref, d_ref, scales_ref, keys_ref, rates_ref, bias_ref):
    total = a_ref[...].astype(F32) + b_ref[...].astype(F32)
    total = total + c_ref[...].astype(F32) + d_ref[...].astype(F32)
    keys_ref[...] = total[:ROWS]
    rates = jnp.concatenate([total[ROWS:, :C], total[ROWS:, C:]], axis=0)
    rates_ref[...] = rates[:H, :ROWS]
    scales_ref[...] = rates[24:26, :ROWS]
    bias_ref[...] = rates[26:27, :H]


ANY = pl.BlockSpec(memory_space=pl.ANY)
VMEM = pl.BlockSpec(memory_space=pltpu.VMEM)
PARAMS = pltpu.CompilerParams(vmem_limit_bytes=30 * 1024 * 1024)


def shape(*dims, dtype=BF16):
    return jax.ShapeDtypeStruct(dims, dtype)


def call(kernel, outs, ins, scratch, out_spec=None, cost=None):
    flops, moved = cost
    return pl.pallas_call(
        kernel,
        out_shape=outs,
        in_specs=ins,
        out_specs=out_spec or [VMEM] * len(outs),
        scratch_shapes=scratch,
        compiler_params=PARAMS,
        cost_estimate=pl.CostEstimate(flops=flops, bytes_accessed=moved, transcendentals=0),
    )


def ring_pairs(first):
    pairs = []
    for i in range(4):
        for c in range(2):
            to = i ^ 1 if (c == 0) == first else 3 - i
            pairs.append((i * 2 + c, to * 2 + c))
    return pairs


def swap(array, axis, first):
    return lax.ppermute(array, (axis, "c"), ring_pairs(first))


def other_core(array):
    return lax.ppermute(array, "c", [(0, 1), (1, 0)])


def opposite(array, axis):
    return lax.ppermute(array, axis, [(i, i ^ 2) for i in range(4)])


def gather_ring(array, axis, direct=False):
    one = swap(array, axis, True)
    two = swap(array, axis, False)
    return [array, one, two, opposite(array, axis) if direct else swap(one, axis, False)]


def add(a, b):
    return (a.astype(F32) + b.astype(F32)).astype(BF16)


def per_device(entries, cotangents, scales, key_weight, rate_weight, rate_bias):
    x, zl, zh, y, c = (lax.axis_index(a) for a in ("x", "zl", "zh", "y", "c"))
    rates = rate_weight[0].T

    def put(a, row, lane):
        pads = (row, PIECE - row - a.shape[0], 0), (lane, 256 - lane - a.shape[1], 0)
        return lax.pad(a, jnp.zeros((), BF16), pads)

    shifted = put(rates, ROWS - 16, C)
    shifted = jnp.where(iota((PIECE, 256), 0) >= ROWS, shifted, jnp.zeros_like(shifted))
    packed = put(key_weight[0], 0, 0) + put(rates, ROWS, 0) + shifted
    packed = packed + put(scales[0], ROWS + 8, C) + put(rate_bias, ROWS + 10, C)

    along = jnp.stack(gather_ring(packed, "zh", direct=True))
    first, second = partner(zh, c, True), partner(zh, c, False)
    across = partner(second, c, True)
    order = [jnp.where(j == first, 1, jnp.where(j == second, 2, jnp.where(j == across, 3, 0))) for j in range(4)]
    along = jnp.take(along, jnp.stack(order), axis=0)
    pairs = []
    for z in range(8):
        for core in range(2):
            to = z ^ 1 if core == 0 else (z + 1 if z % 2 else z - 1) % 8
            pairs.append(tuple(((i % 2) * 4 + i // 2) * 2 + core for i in (z, to)))
    other = lax.ppermute(along, ("zl", "zh", "c"), pairs)
    both = jnp.where(zl == 0, jnp.stack([along, other]), jnp.stack([other, along]))

    left = jnp.stack(gather_ring(both[..., :C], "x"))
    right = jnp.stack(gather_ring(both[..., C:], "y"))
    left = gather_ring(left, "y")
    right = gather_ring(right, "x")
    left = left + [other_core(a) for a in left]
    right = right + [other_core(a) for a in right]

    sent = call(
        sequence_kernel,
        [shape(LAYERS, SENT, BLOCK)],
        [ANY] * 18,
        [
            pltpu.VMEM((LAYERS, 4, 4, 2, PIECE, 256), BF16),
            pltpu.VMEM((LAYERS, T, D), BF16),
            pltpu.VMEM((LAYERS, T, D), BF16),
            pltpu.VMEM((LAYERS, T, D), BF16),
            pltpu.VMEM((LAYERS, T, D), BF16),
            pltpu.VMEM((LAYERS, T, W), F32),
            pltpu.VMEM((LAYERS, 1, W), F32),
            pltpu.VMEM((LAYERS, T, 256), F32),
            pltpu.VMEM((LAYERS, T, 256), F32),
            pltpu.VMEM((2, T, D), BF16),
            pltpu.VMEM((LAYERS, SENT, BLOCK), BF16),
            pltpu.SemaphoreType.DMA((4,)),
            pltpu.SemaphoreType.DMA((4,)),
            pltpu.SemaphoreType.DMA((2,)),
            pltpu.SemaphoreType.DMA,
        ],
        [ANY],
        cost=(8_000_000_000, 30_000_000),
    )(*left, *right, entries, cotangents)[0]

    groups = [
        [
            (((i * 4) + (z - i % 2 * core) % 4) * 4 + row) * 2 + core
            for i in range(LAYERS)
        ]
        for z in range(4)
        for row in range(4)
        for core in range(2)
    ]
    got = lax.all_to_all(
        sent, ("x", "zl", "zh", "y", "c"), 0, 0, axis_index_groups=groups, tiled=True
    )
    half = shape(4, 4, PIECE, 256)
    keep, send = call(
        weight_kernel,
        [half, half],
        [ANY],
        [
            pltpu.VMEM((LAYERS, SENT, BLOCK), BF16),
            pltpu.VMEM((2, 4, 4, PIECE, 256), BF16),
            pltpu.SemaphoreType.DMA((BLOCKS + 1,)),
            pltpu.SemaphoreType.DMA((2,)),
        ],
        [ANY] * 2,
        cost=(600_000_000, 4_000_000),
    )(got)
    got = other_core(send)
    got = swap(add(keep[2:], got[2:]), "y", True), keep[:2], got[:2]
    keep = add(got[1], got[2])
    got = got[0]
    got, keep = swap(add(keep[1], got[1]), "y", False), add(keep[0], got[0])
    got = add(keep, got)
    parts = [
        got[0],
        swap(got[2], "zh", True),
        swap(got[1], "zh", False),
        opposite(got[3], "zh"),
    ]
    g_scales, g_keys, g_rates, g_bias = call(
        final_kernel,
        [
            shape(2, ROWS, dtype=F32),
            shape(ROWS, 256, dtype=F32),
            shape(H, ROWS, dtype=F32),
            shape(1, H, dtype=F32),
        ],
        [VMEM] * 4,
        [],
        cost=(0, 500_000),
    )(*parts)
    return g_scales[None], g_keys[None], g_rates.T[None], g_bias


def solution(mesh):
    fine = Mesh(mesh.devices.reshape(4, 2, 4, 4, 2), ("x", "zl", "zh", "y", "c"))
    placed = (
        P(None, None, DP, None),
        P(None, None, DP, None),
        P(SECTION, None, DP),
        P(SECTION, DP, None),
        P(SECTION, DP, None),
        P(SECTION, None),
    )
    return jax.shard_map(
        per_device,
        mesh=fine,
        in_specs=placed,
        out_specs=(
            P(SECTION, None, DP),
            P(SECTION, DP, None),
            P(SECTION, DP, None),
            P(SECTION, None),
        ),
        check_vma=False,
    )
```

```python
import jax
import jax.numpy as jnp
from jax import lax
from jax.experimental import pallas as pl
from jax.experimental.pallas import tpu as pltpu
from jax.sharding import Mesh, PartitionSpec as P

F32 = jnp.float32
BF16 = jnp.bfloat16
SECTION = ("x", "zl")
DP = ("zh", "y", "c")

T = 32
D = 3072
C = 128
H = 24
GROUPS = H // 4
W = H * T
LAYERS = 8
SEQS = 6
ROWS = 96
PIECE = 112
TOK = LAYERS * T
BLOCK = 384
BLOCKS = D // BLOCK
SENT = BLOCKS * T + T + 16


def iota(shape, axis):
    return lax.broadcasted_iota(jnp.int32, shape, axis)


def nt(a, b):
    return lax.dot_general(
        a, b, (((1,), (1,)), ((), ())), preferred_element_type=F32
    )


def tn(a, b):
    return lax.dot_general(
        a, b, (((0,), (0,)), ((), ())), preferred_element_type=F32
    )


def nn(a, b):
    return jnp.dot(a, b, preferred_element_type=F32)


def split3(a):
    hi = a.astype(BF16)
    rest = a - hi.astype(F32)
    mid = rest.astype(BF16)
    low = (rest - mid.astype(F32)).astype(BF16)
    return jnp.concatenate([hi, mid, low, jnp.zeros_like(hi)], axis=1)


def masks():
    row = iota((T, W), 0)
    col = iota((T, W), 1) % T
    spread = (iota((C, W), 0) % T == iota((C, W), 1) // T) & (iota((C, W), 0) < 3 * T)
    spread = jnp.where(spread, 1.0, 0.0).astype(BF16)
    block = iota((C, C), 0) // T == iota((C, C), 1) // T
    tri = jnp.where(iota((T, T), 0) >= iota((T, T), 1), 1.0, 0.0).astype(BF16)
    tri_back = jnp.where(iota((T, T), 0) <= iota((T, T), 1), 1.0, 0.0).astype(BF16)
    return row >= col, row == col, spread, block, tri, tri_back


def tile4(a):
    return jnp.concatenate([a] * 4, axis=0)


def stack_heads(a, g):
    return jnp.concatenate([a[:, C * (4 * g + j) : C * (4 * g + j + 1)] for j in range(4)], axis=0)


def unstack_heads(parts):
    return jnp.concatenate([p[T * j : T * (j + 1)] for p in parts for j in range(4)], axis=1)


def block_diag(mixing, g, block):
    return jnp.where(block, tile4(mixing[:, C * g : C * (g + 1)]), 0.0).astype(BF16)


def assemble_rows(piece):
    out = []
    lane = iota((T, C), 1)
    for m in range(8):
        p = []
        for i in range(4):
            z = piece(4 * m + i).astype(F32)
            p.append(jnp.concatenate([z[:, :C], z[:, C:]], axis=0))
        p1 = pltpu.roll(p[1], 96, 1)
        p2 = pltpu.roll(p[2], 64, 1)
        p3 = pltpu.roll(p[3], 32, 1)
        out.append(jnp.where(lane < 96, p[0], p1))
        out.append(jnp.where(lane < 64, p1, p2))
        out.append(jnp.where(lane < 32, p2, p3))
    return jnp.concatenate(out, axis=1)


def cut_rows(rows):
    lane = iota((T, C), 1)
    a, b, c = rows[:, :C], rows[:, C : 2 * C], rows[:, 2 * C :]
    one = jnp.where(lane < 32, pltpu.roll(a, 32, 1), pltpu.roll(b, 32, 1))
    two = jnp.where(lane < 64, pltpu.roll(b, 64, 1), pltpu.roll(c, 64, 1))
    parts = [a, one, two, pltpu.roll(c, 96, 1)]
    return [jnp.concatenate([p[:16], p[16:]], axis=1) for p in parts]


def gray(i):
    return jnp.where(i >= 2, 5 - i, i)


def partner(i, c, first):
    return jnp.where((c == 0) == first, i ^ 1, 3 - i)


def sequence_kernel(*refs):
    left, right = refs[:8], refs[8:16]
    entry_ref, cot_ref, sent_ref = refs[16:19]
    w_scr, rows_scr, xs, ns, mixed_scr, decay_scr, write_scr, small_scr, proj_scr = refs[19:28]
    first_scr, sem_c = refs[28:]

    x, y, c = (lax.axis_index(a) for a in ("x", "y", "c"))
    section = x * 2 + lax.axis_index("zl")
    mine = jnp.minimum(section, SEQS - 1)
    loads = []
    for i, ref in enumerate((entry_ref, cot_ref)):
        copy = pltpu.make_async_copy(
            ref.at[mine // 3, mine % 3], first_scr.at[i], sem_c.at[i]
        )
        copy.start()
        loads.append(copy)

    def ring(i, core):
        one, two = partner(i, core, True), partner(i, core, False)
        return [i, one, two, partner(two, core, True)]

    for kc in range(2):
        cc = (c + kc) % 2
        ys, xx = ring(y, cc), ring(x, cc)
        for i in range(4):
            for j in range(4):
                w_scr[pl.ds(2 * xx[j], 2), :, ys[i], cc, :, :C] = left[kc * 4 + i][j]
                w_scr[pl.ds(2 * xx[i], 2), :, ys[j], cc, :, C:] = right[kc * 4 + i][j]

    causal, diag, spread, block, tri, tri_back = masks()

    def keys_of(layer, m):
        parts = [w_scr[layer, m // 2, (m % 2) * 2 + i // 2, i % 2, :ROWS] for i in range(4)]
        return jnp.concatenate(parts, axis=0)

    def forward(layer, stream):
        rows = assemble_rows(lambda d: w_scr[layer, d // 8, d // 2 % 4, d % 2, ROWS:])
        rows_low = rows.astype(BF16)
        rows_scr[layer] = rows_low
        gain, scale, bias = rows[24:25], rows[25:26], rows[26:27, :T]
        xs[layer] = stream
        x_f = stream.astype(F32)
        inv_rms = lax.rsqrt(jnp.sum(x_f * x_f, axis=1, keepdims=True) * (1.0 / D) + 1e-05)
        normed = (x_f * inv_rms * gain).astype(BF16)
        ns[layer] = normed
        for m in range(BLOCKS):
            sent_ref[layer, T * m : T * (m + 1)] = normed[:, BLOCK * m : BLOCK * (m + 1)]
        logits = nt(normed, rows_low) + bias
        key_query = sum(
            nn(normed[:, BLOCK * m : BLOCK * (m + 1)], keys_of(layer, m)) for m in range(BLOCKS)
        )
        head = iota((T, T), 1) < H
        rate = jnp.maximum(logits, 0.0) + jnp.log1p(jnp.exp(-jnp.abs(logits)))
        rate = jnp.where(head, rate, 0.0)
        keep = 1.0 / (1.0 + rate)
        write = rate * keep
        total = nn(tri, split3(-jnp.log1p(rate)))
        total = total[:, :T] + total[:, T : 2 * T] + total[:, 2 * T : 3 * T]
        wide = nn(jnp.concatenate([split3(total), split3(write)], axis=0), spread)
        total_t, write_t = wide[:T], wide[T:]
        total_s = jnp.sum(jnp.where(diag, total_t, 0.0), axis=0, keepdims=True)
        write_s = jnp.sum(jnp.where(diag, write_t, 0.0), axis=0, keepdims=True)
        decay = jnp.where(causal, jnp.exp(jnp.where(causal, total_t - total_s, 0.0)), 0.0)
        k = key_query[:, :C]
        q = key_query[:, C:]
        inv = lax.rsqrt(jnp.sum(k * k, axis=1, keepdims=True) + 1e-06)
        scores = nt(q.astype(BF16), tile4((k * inv).astype(BF16)))
        decay_scr[layer] = decay
        write_scr[layer] = write_s
        proj_scr[layer] = key_query
        small_scr[layer] = jnp.concatenate([scores, logits, keep, jnp.zeros((T, 64), F32)], axis=1)
        mixing = decay * write_s * jnp.concatenate([scores] * GROUPS, axis=1)
        mixed = unstack_heads(
            [nn(block_diag(mixing, g, block), stack_heads(normed, g)) for g in range(GROUPS)]
        )
        mixed_scr[layer] = mixed.astype(BF16)
        return (x_f + scale * mixed).astype(BF16)

    loads[0].wait()
    loads[1].wait()
    lax.fori_loop(0, LAYERS, forward, first_scr[0], unroll=2)

    def backward(step, back):
        layer = LAYERS - 1 - step
        x_f = xs[layer].astype(F32)
        normed = ns[layer]
        rows_low = rows_scr[layer]
        rows = rows_low[16:].astype(F32)
        gain, scale = rows[8:9], rows[9:10]
        dy = back.astype(F32)
        decay = decay_scr[layer]
        write_s = write_scr[layer]
        small = small_scr[layer]
        scores, logits, keep = small[:, :C], small[:, C : C + T], small[:, C + T : C + 2 * T]
        scores6 = jnp.concatenate([scores] * GROUPS, axis=1)
        mixing = decay * write_s * scores6
        d_scale = jnp.sum(dy * mixed_scr[layer].astype(F32), axis=0, keepdims=True)
        d_out = (dy * scale).astype(BF16)
        d_mix = []
        d_values = []
        for g in range(GROUPS):
            grad = stack_heads(d_out, g)
            full = jnp.where(block, nt(grad, stack_heads(normed, g)), 0.0)
            d_mix.append(full[:T] + full[T : 2 * T] + full[2 * T : 3 * T] + full[3 * T :])
            d_values.append(tn(block_diag(mixing, g, block), grad))
        d_mix = jnp.concatenate(d_mix, axis=1)
        d_values = unstack_heads(d_values)
        near = d_mix * decay
        scored = near * scores6
        d_write_s = jnp.sum(scored, axis=0, keepdims=True)
        weighted = near * write_s
        d_scores = sum(weighted[:, C * g : C * (g + 1)] for g in range(GROUPS)).astype(BF16)
        later = jnp.where(causal & ~diag, nn(tri_back, (scored * write_s).astype(BF16)), 0.0)
        own = jnp.where(diag, d_write_s, 0.0)
        summed = nt(jnp.concatenate([later.astype(BF16), own.astype(BF16)], axis=0), spread[:T])
        d_log, d_write = summed[:T], summed[T:]
        d_rate = keep * (d_write * keep - d_log)
        d_logits = d_rate / (1.0 + jnp.exp(-logits))
        d_low = jnp.where(iota((T, T), 1) < H, d_logits, 0.0).astype(BF16)
        k = proj_scr[layer][:, :C]
        q = proj_scr[layer][:, C:]
        inv = lax.rsqrt(jnp.sum(k * k, axis=1, keepdims=True) + 1e-06)
        d_q = nn(d_scores, tile4((k * inv).astype(BF16)))
        d_unit = tn(d_scores, q.astype(BF16))
        d_unit = d_unit[:T] + d_unit[T : 2 * T] + d_unit[2 * T : 3 * T] + d_unit[3 * T :]
        d_k = inv * d_unit - k * (inv * inv * inv * jnp.sum(d_unit * k, axis=1, keepdims=True))
        d_keyq = jnp.concatenate([d_k, d_q], axis=1).astype(BF16)
        through = jnp.concatenate([nt(d_keyq, keys_of(layer, m)) for m in range(BLOCKS)], axis=1)
        d_normed = d_values + through + nn(d_low, rows_low)
        inv_rms = lax.rsqrt(jnp.sum(x_f * x_f, axis=1, keepdims=True) * (1.0 / D) + 1e-05)
        x_hat = x_f * inv_rms
        d_gain = jnp.sum(d_normed * x_hat, axis=0, keepdims=True)
        d_hat = d_normed * gain
        mean = jnp.sum(d_hat * x_hat, axis=1, keepdims=True) * (1.0 / D)
        sent_ref[layer, TOK : TOK + T, :256] = d_keyq
        sent_ref[layer, TOK : TOK + T, 256:] = jnp.concatenate(
            [d_low, jnp.zeros((T, 96), BF16)], axis=1
        )
        sent_ref[layer, TOK + T :] = jnp.concatenate(
            [d[:, BLOCK * i : BLOCK * (i + 1)] for d in (d_gain, d_scale) for i in range(8)], axis=0
        ).astype(BF16)
        return (dy + inv_rms * (d_hat - x_hat * mean)).astype(BF16)

    cot = jnp.where(section < SEQS, first_scr[1].astype(F32), 0.0).astype(BF16)
    lax.fori_loop(0, LAYERS, backward, cot, unroll=2)


def weight_kernel(got_ref, keep_ref, send_ref, got, scr, sem_in, sem):
    y, c, zh = (lax.axis_index(a) for a in ("y", "c", "zh"))
    loads = []
    for m in list(range(BLOCKS)) + [BLOCKS]:
        at = pl.ds(T * m, T if m < BLOCKS else T + 16)
        loads.append(pltpu.make_async_copy(got_ref.at[:, at], got.at[:, at], sem_in.at[m]))
    loads[-1].start()
    for copy in loads[:-1]:
        copy.start()

    def slot(there, here, core):
        bits = gray(jnp.int32(there)) ^ gray(here)
        return bits if core else (bits & 1) * 2 + (bits >> 1)

    loads[-1].wait()
    tokens = jnp.concatenate([got[s, TOK : TOK + T] for s in range(LAYERS)], axis=0)
    extra = sum(got[s, TOK + T :].astype(F32) for s in range(LAYERS))
    bias = jnp.sum(tokens[:, 256:].astype(F32), axis=0, keepdims=True)
    bias = jnp.concatenate([bias[:, :ROWS]] * 4, axis=1)
    for m in range(BLOCKS):
        loads[m].wait()
        normed = jnp.concatenate([got[s, T * m : T * (m + 1)] for s in range(LAYERS)], axis=0)
        keys = tn(normed, tokens[:, :256])
        rates = tn(tokens[:, 256:], normed)[:H]
        rows = jnp.concatenate(
            [rates, extra[m : m + 1], extra[m + 8 : m + 9], bias, jnp.zeros((5, BLOCK), F32)],
            axis=0,
        )
        low = cut_rows(rows)
        for i in range(4):
            d = 4 * m + i
            y_at, z_at = slot(d // 2 % 4, y, d % 2), slot(d // 8, zh, d % 2)
            c_at = (d + c) % 2
            scr[c_at, y_at, z_at, :ROWS] = keys[ROWS * i : ROWS * (i + 1)].astype(BF16)
            scr[c_at, y_at, z_at, ROWS:] = low[i].astype(BF16)
        if m % 2:
            for core in range(2):
                z_at = slot(m // 2, zh, core)
                for i, ref in enumerate((keep_ref, send_ref)):

                    @pl.when((core + c) % 2 == i)
                    def _(i=i, ref=ref, z_at=z_at):
                        pltpu.make_async_copy(scr.at[i, :, z_at], ref.at[:, z_at], sem.at[i]).start()

    for i, ref in enumerate((keep_ref, send_ref)):
        pltpu.make_async_copy(scr.at[i], ref, sem.at[i]).wait()


def final_kernel(a_ref, b_ref, c_ref, d_ref, scales_ref, keys_ref, rates_ref, bias_ref):
    total = a_ref[...].astype(F32) + b_ref[...].astype(F32)
    total = total + c_ref[...].astype(F32) + d_ref[...].astype(F32)
    keys_ref[...] = total[:ROWS]
    rates = jnp.concatenate([total[ROWS:, :C], total[ROWS:, C:]], axis=0)
    rates_ref[...] = rates[:H, :ROWS]
    scales_ref[...] = rates[24:26, :ROWS]
    bias_ref[...] = rates[26:27, :H]


ANY = pl.BlockSpec(memory_space=pl.ANY)
VMEM = pl.BlockSpec(memory_space=pltpu.VMEM)
PARAMS = pltpu.CompilerParams(vmem_limit_bytes=30 * 1024 * 1024)


def shape(*dims, dtype=BF16):
    return jax.ShapeDtypeStruct(dims, dtype)


def call(kernel, outs, ins, scratch, out_spec=None, cost=None):
    flops, moved = cost
    return pl.pallas_call(
        kernel,
        out_shape=outs,
        in_specs=ins,
        out_specs=out_spec or [VMEM] * len(outs),
        scratch_shapes=scratch,
        compiler_params=PARAMS,
        cost_estimate=pl.CostEstimate(flops=flops, bytes_accessed=moved, transcendentals=0),
    )


def ring_pairs(first):
    pairs = []
    for i in range(4):
        for c in range(2):
            to = i ^ 1 if (c == 0) == first else 3 - i
            pairs.append((i * 2 + c, to * 2 + c))
    return pairs


def swap(array, axis, first):
    return lax.ppermute(array, (axis, "c"), ring_pairs(first))


def other_core(array):
    return lax.ppermute(array, "c", [(0, 1), (1, 0)])


def opposite(array, axis):
    return lax.ppermute(array, axis, [(i, i ^ 2) for i in range(4)])


def gather_ring(array, axis, direct=False):
    one = swap(array, axis, True)
    two = swap(array, axis, False)
    return [array, one, two, opposite(array, axis) if direct else swap(one, axis, False)]


def add(a, b):
    return (a.astype(F32) + b.astype(F32)).astype(BF16)


def per_device(entries, cotangents, scales, key_weight, rate_weight, rate_bias):
    x, zl, zh, y, c = (lax.axis_index(a) for a in ("x", "zl", "zh", "y", "c"))
    rates = rate_weight[0].T

    def put(a, row, lane):
        pads = (row, PIECE - row - a.shape[0], 0), (lane, 256 - lane - a.shape[1], 0)
        return lax.pad(a, jnp.zeros((), BF16), pads)

    shifted = put(rates, ROWS - 16, C)
    shifted = jnp.where(iota((PIECE, 256), 0) >= ROWS, shifted, jnp.zeros_like(shifted))
    packed = put(key_weight[0], 0, 0) + put(rates, ROWS, 0) + shifted
    packed = packed + put(scales[0], ROWS + 8, C) + put(rate_bias, ROWS + 10, C)

    along = jnp.stack(gather_ring(packed, "zh", direct=True))
    first, second = partner(zh, c, True), partner(zh, c, False)
    across = partner(second, c, True)
    order = [jnp.where(j == first, 1, jnp.where(j == second, 2, jnp.where(j == across, 3, 0))) for j in range(4)]
    along = jnp.take(along, jnp.stack(order), axis=0)
    pairs = []
    for z in range(8):
        for core in range(2):
            to = z ^ 1 if core == 0 else (z + 1 if z % 2 else z - 1) % 8
            pairs.append(tuple(((i % 2) * 4 + i // 2) * 2 + core for i in (z, to)))
    other = lax.ppermute(along, ("zl", "zh", "c"), pairs)
    both = jnp.where(zl == 0, jnp.stack([along, other]), jnp.stack([other, along]))

    left = jnp.stack(gather_ring(both[..., :C], "x"))
    right = jnp.stack(gather_ring(both[..., C:], "y"))
    left = gather_ring(left, "y")
    right = gather_ring(right, "x")
    left = left + [other_core(a) for a in left]
    right = right + [other_core(a) for a in right]

    sent = call(
        sequence_kernel,
        [shape(LAYERS, SENT, BLOCK)],
        [VMEM] * 16 + [ANY] * 2,
        [
            pltpu.VMEM((LAYERS, 4, 4, 2, PIECE, 256), BF16),
            pltpu.VMEM((LAYERS, T, D), BF16),
            pltpu.VMEM((LAYERS, T, D), BF16),
            pltpu.VMEM((LAYERS, T, D), BF16),
            pltpu.VMEM((LAYERS, T, D), BF16),
            pltpu.VMEM((LAYERS, T, W), F32),
            pltpu.VMEM((LAYERS, 1, W), F32),
            pltpu.VMEM((LAYERS, T, 256), F32),
            pltpu.VMEM((LAYERS, T, 256), F32),
            pltpu.VMEM((2, T, D), BF16),
            pltpu.SemaphoreType.DMA((2,)),
        ],
        cost=(8_000_000_000, 30_000_000),
    )(*left, *right, entries, cotangents)[0]

    groups = [
        [
            (((i * 4) + (z - i % 2 * core) % 4) * 4 + row) * 2 + core
            for i in range(LAYERS)
        ]
        for z in range(4)
        for row in range(4)
        for core in range(2)
    ]
    got = lax.all_to_all(
        sent, ("x", "zl", "zh", "y", "c"), 0, 0, axis_index_groups=groups, tiled=True
    )
    half = shape(4, 4, PIECE, 256)
    keep, send = call(
        weight_kernel,
        [half, half],
        [ANY],
        [
            pltpu.VMEM((LAYERS, SENT, BLOCK), BF16),
            pltpu.VMEM((2, 4, 4, PIECE, 256), BF16),
            pltpu.SemaphoreType.DMA((BLOCKS + 1,)),
            pltpu.SemaphoreType.DMA((2,)),
        ],
        [ANY] * 2,
        cost=(600_000_000, 4_000_000),
    )(got)
    got = other_core(send)
    got = swap(add(keep[2:], got[2:]), "y", True), keep[:2], got[:2]
    keep = add(got[1], got[2])
    got = got[0]
    got, keep = swap(add(keep[1], got[1]), "y", False), add(keep[0], got[0])
    got = add(keep, got)
    parts = [
        got[0],
        swap(got[2], "zh", True),
        swap(got[1], "zh", False),
        opposite(got[3], "zh"),
    ]
    g_scales, g_keys, g_rates, g_bias = call(
        final_kernel,
        [
            shape(2, ROWS, dtype=F32),
            shape(ROWS, 256, dtype=F32),
            shape(H, ROWS, dtype=F32),
            shape(1, H, dtype=F32),
        ],
        [VMEM] * 4,
        [],
        cost=(0, 500_000),
    )(*parts)
    return g_scales[None], g_keys[None], g_rates.T[None], g_bias


def solution(mesh):
    fine = Mesh(mesh.devices.reshape(4, 2, 4, 4, 2), ("x", "zl", "zh", "y", "c"))
    placed = (
        P(None, None, DP, None),
        P(None, None, DP, None),
        P(SECTION, None, DP),
        P(SECTION, DP, None),
        P(SECTION, DP, None),
        P(SECTION, None),
    )
    return jax.shard_map(
        per_device,
        mesh=fine,
        in_specs=placed,
        out_specs=(
            P(SECTION, None, DP),
            P(SECTION, DP, None),
            P(SECTION, DP, None),
            P(SECTION, None),
        ),
        check_vma=False,
    )
```

```python
import jax
import jax.numpy as jnp
from jax import lax
from jax.experimental import pallas as pl
from jax.experimental.pallas import tpu as pltpu
from jax.sharding import Mesh, PartitionSpec as P

F32 = jnp.float32
BF16 = jnp.bfloat16
SECTION = ("x", "zl")
DP = ("zh", "y", "c")

T = 32
D = 3072
C = 128
H = 24
GROUPS = H // 4
W = H * T
LAYERS = 8
SEQS = 6
ROWS = 96
PIECE = 112
TOK = LAYERS * T
BLOCK = 384
BLOCKS = D // BLOCK
SENT = BLOCKS * T + T + 16


def iota(shape, axis):
    return lax.broadcasted_iota(jnp.int32, shape, axis)


def nt(a, b):
    return lax.dot_general(
        a, b, (((1,), (1,)), ((), ())), preferred_element_type=F32
    )


def tn(a, b):
    return lax.dot_general(
        a, b, (((0,), (0,)), ((), ())), preferred_element_type=F32
    )


def nn(a, b):
    return jnp.dot(a, b, preferred_element_type=F32)


def split3(a):
    hi = a.astype(BF16)
    rest = a - hi.astype(F32)
    mid = rest.astype(BF16)
    low = (rest - mid.astype(F32)).astype(BF16)
    return jnp.concatenate([hi, mid, low, jnp.zeros_like(hi)], axis=1)


def masks():
    row = iota((T, W), 0)
    col = iota((T, W), 1) % T
    spread = (iota((C, W), 0) % T == iota((C, W), 1) // T) & (iota((C, W), 0) < 3 * T)
    spread = jnp.where(spread, 1.0, 0.0).astype(BF16)
    block = iota((C, C), 0) // T == iota((C, C), 1) // T
    tri = jnp.where(iota((T, T), 0) >= iota((T, T), 1), 1.0, 0.0).astype(BF16)
    tri_back = jnp.where(iota((T, T), 0) <= iota((T, T), 1), 1.0, 0.0).astype(BF16)
    return row >= col, row == col, spread, block, tri, tri_back


def tile4(a):
    return jnp.concatenate([a] * 4, axis=0)


def stack_heads(a, g):
    return jnp.concatenate([a[:, C * (4 * g + j) : C * (4 * g + j + 1)] for j in range(4)], axis=0)


def unstack_heads(parts):
    return jnp.concatenate([p[T * j : T * (j + 1)] for p in parts for j in range(4)], axis=1)


def block_diag(mixing, g, block):
    return jnp.where(block, tile4(mixing[:, C * g : C * (g + 1)]), 0.0).astype(BF16)


def assemble_rows(piece):
    out = []
    lane = iota((T, C), 1)
    for m in range(8):
        p = []
        for i in range(4):
            z = piece(4 * m + i).astype(F32)
            p.append(jnp.concatenate([z[:, :C], z[:, C:]], axis=0))
        p1 = pltpu.roll(p[1], 96, 1)
        p2 = pltpu.roll(p[2], 64, 1)
        p3 = pltpu.roll(p[3], 32, 1)
        out.append(jnp.where(lane < 96, p[0], p1))
        out.append(jnp.where(lane < 64, p1, p2))
        out.append(jnp.where(lane < 32, p2, p3))
    return jnp.concatenate(out, axis=1)


def cut_rows(rows):
    lane = iota((T, C), 1)
    a, b, c = rows[:, :C], rows[:, C : 2 * C], rows[:, 2 * C :]
    one = jnp.where(lane < 32, pltpu.roll(a, 32, 1), pltpu.roll(b, 32, 1))
    two = jnp.where(lane < 64, pltpu.roll(b, 64, 1), pltpu.roll(c, 64, 1))
    parts = [a, one, two, pltpu.roll(c, 96, 1)]
    return [jnp.concatenate([p[:16], p[16:]], axis=1) for p in parts]


def gray(i):
    return jnp.where(i >= 2, 5 - i, i)


def partner(i, c, first):
    return jnp.where((c == 0) == first, i ^ 1, 3 - i)


def sequence_kernel(*refs):
    left, right = refs[:8], refs[8:16]
    entry_ref, cot_ref, sent_ref = refs[16:19]
    w_scr, rows_scr, xs, ns, mixed_scr, decay_scr, write_scr, small_scr, proj_scr = refs[19:28]
    first_scr, sem_c = refs[28:]

    x, y, c = (lax.axis_index(a) for a in ("x", "y", "c"))
    section = x * 2 + lax.axis_index("zl")
    mine = jnp.minimum(section, SEQS - 1)
    loads = []
    for i, ref in enumerate((entry_ref, cot_ref)):
        copy = pltpu.make_async_copy(
            ref.at[mine // 3, mine % 3], first_scr.at[i], sem_c.at[i]
        )
        copy.start()
        loads.append(copy)

    def ring(i, core):
        one, two = partner(i, core, True), partner(i, core, False)
        return [i, one, two, partner(two, core, True)]

    for kc in range(2):
        cc = (c + kc) % 2
        ys, xx = ring(y, cc), ring(x, cc)
        for i in range(4):
            for j in range(4):
                w_scr[pl.ds(2 * xx[j], 2), :, ys[i], cc, :, :C] = left[kc * 4 + i][j]
                w_scr[pl.ds(2 * xx[i], 2), :, ys[j], cc, :, C:] = right[kc * 4 + i][j]

    causal, diag, spread, block, tri, tri_back = masks()

    def keys_of(layer, m):
        parts = [w_scr[layer, m // 2, (m % 2) * 2 + i // 2, i % 2, :ROWS] for i in range(4)]
        return jnp.concatenate(parts, axis=0)

    def forward(layer, stream):
        rows = assemble_rows(lambda d: w_scr[layer, d // 8, d // 2 % 4, d % 2, ROWS:])
        rows_low = rows.astype(BF16)
        rows_scr[layer] = rows_low
        gain, scale, bias = rows[24:25], rows[25:26], rows[26:27, :T]
        xs[layer] = stream
        x_f = stream.astype(F32)
        inv_rms = lax.rsqrt(jnp.sum(x_f * x_f, axis=1, keepdims=True) * (1.0 / D) + 1e-05)
        normed = (x_f * inv_rms * gain).astype(BF16)
        ns[layer] = normed
        for m in range(BLOCKS):
            sent_ref[layer, T * m : T * (m + 1)] = normed[:, BLOCK * m : BLOCK * (m + 1)]
        logits = nt(normed, rows_low) + bias
        key_query = sum(
            nn(normed[:, BLOCK * m : BLOCK * (m + 1)], keys_of(layer, m)) for m in range(BLOCKS)
        )
        head = iota((T, T), 1) < H
        rate = jnp.maximum(logits, 0.0) + jnp.log1p(jnp.exp(-jnp.abs(logits)))
        rate = jnp.where(head, rate, 0.0)
        keep = 1.0 / (1.0 + rate)
        write = rate * keep
        total = nn(tri, split3(-jnp.log1p(rate)))
        total = total[:, :T] + total[:, T : 2 * T] + total[:, 2 * T : 3 * T]
        wide = nn(jnp.concatenate([split3(total), split3(write)], axis=0), spread)
        total_t, write_t = wide[:T], wide[T:]
        total_s = jnp.sum(jnp.where(diag, total_t, 0.0), axis=0, keepdims=True)
        write_s = jnp.sum(jnp.where(diag, write_t, 0.0), axis=0, keepdims=True)
        decay = jnp.where(causal, jnp.exp(jnp.where(causal, total_t - total_s, 0.0)), 0.0)
        k = key_query[:, :C]
        q = key_query[:, C:]
        inv = lax.rsqrt(jnp.sum(k * k, axis=1, keepdims=True) + 1e-06)
        scores = nt(q.astype(BF16), tile4((k * inv).astype(BF16)))
        decay_scr[layer] = decay
        write_scr[layer] = write_s
        proj_scr[layer] = key_query
        small_scr[layer] = jnp.concatenate([scores, logits, keep, jnp.zeros((T, 64), F32)], axis=1)
        mixing = decay * write_s * jnp.concatenate([scores] * GROUPS, axis=1)
        mixed = unstack_heads(
            [nn(block_diag(mixing, g, block), stack_heads(normed, g)) for g in range(GROUPS)]
        )
        mixed_scr[layer] = mixed.astype(BF16)
        return (x_f + scale * mixed).astype(BF16)

    loads[0].wait()
    loads[1].wait()
    lax.fori_loop(0, LAYERS, forward, first_scr[0], unroll=2)

    def backward(step, back):
        layer = LAYERS - 1 - step
        x_f = xs[layer].astype(F32)
        normed = ns[layer]
        rows_low = rows_scr[layer]
        rows = rows_low[16:].astype(F32)
        gain, scale = rows[8:9], rows[9:10]
        dy = back.astype(F32)
        decay = decay_scr[layer]
        write_s = write_scr[layer]
        small = small_scr[layer]
        scores, logits, keep = small[:, :C], small[:, C : C + T], small[:, C + T : C + 2 * T]
        scores6 = jnp.concatenate([scores] * GROUPS, axis=1)
        mixing = decay * write_s * scores6
        d_scale = jnp.sum(dy * mixed_scr[layer].astype(F32), axis=0, keepdims=True)
        d_out = (dy * scale).astype(BF16)
        d_mix = []
        d_values = []
        for g in range(GROUPS):
            grad = stack_heads(d_out, g)
            full = jnp.where(block, nt(grad, stack_heads(normed, g)), 0.0)
            d_mix.append(full[:T] + full[T : 2 * T] + full[2 * T : 3 * T] + full[3 * T :])
            d_values.append(tn(block_diag(mixing, g, block), grad))
        d_mix = jnp.concatenate(d_mix, axis=1)
        d_values = unstack_heads(d_values)
        near = d_mix * decay
        scored = near * scores6
        d_write_s = jnp.sum(scored, axis=0, keepdims=True)
        weighted = near * write_s
        d_scores = sum(weighted[:, C * g : C * (g + 1)] for g in range(GROUPS)).astype(BF16)
        later = jnp.where(causal & ~diag, nn(tri_back, (scored * write_s).astype(BF16)), 0.0)
        own = jnp.where(diag, d_write_s, 0.0)
        summed = nt(jnp.concatenate([later.astype(BF16), own.astype(BF16)], axis=0), spread[:T])
        d_log, d_write = summed[:T], summed[T:]
        d_rate = keep * (d_write * keep - d_log)
        d_logits = d_rate / (1.0 + jnp.exp(-logits))
        d_low = jnp.where(iota((T, T), 1) < H, d_logits, 0.0).astype(BF16)
        k = proj_scr[layer][:, :C]
        q = proj_scr[layer][:, C:]
        inv = lax.rsqrt(jnp.sum(k * k, axis=1, keepdims=True) + 1e-06)
        d_q = nn(d_scores, tile4((k * inv).astype(BF16)))
        d_unit = tn(d_scores, q.astype(BF16))
        d_unit = d_unit[:T] + d_unit[T : 2 * T] + d_unit[2 * T : 3 * T] + d_unit[3 * T :]
        d_k = inv * d_unit - k * (inv * inv * inv * jnp.sum(d_unit * k, axis=1, keepdims=True))
        d_keyq = jnp.concatenate([d_k, d_q], axis=1).astype(BF16)
        through = jnp.concatenate([nt(d_keyq, keys_of(layer, m)) for m in range(BLOCKS)], axis=1)
        d_normed = d_values + through + nn(d_low, rows_low)
        inv_rms = lax.rsqrt(jnp.sum(x_f * x_f, axis=1, keepdims=True) * (1.0 / D) + 1e-05)
        x_hat = x_f * inv_rms
        d_gain = jnp.sum(d_normed * x_hat, axis=0, keepdims=True)
        d_hat = d_normed * gain
        mean = jnp.sum(d_hat * x_hat, axis=1, keepdims=True) * (1.0 / D)
        sent_ref[layer, TOK : TOK + T, :256] = d_keyq
        sent_ref[layer, TOK : TOK + T, 256:] = jnp.concatenate(
            [d_low, jnp.zeros((T, 96), BF16)], axis=1
        )
        sent_ref[layer, TOK + T :] = jnp.concatenate(
            [d[:, BLOCK * i : BLOCK * (i + 1)] for d in (d_gain, d_scale) for i in range(8)], axis=0
        ).astype(BF16)
        return (dy + inv_rms * (d_hat - x_hat * mean)).astype(BF16)

    cot = jnp.where(section < SEQS, first_scr[1].astype(F32), 0.0).astype(BF16)
    lax.fori_loop(0, LAYERS, backward, cot, unroll=2)


def weight_kernel(got_ref, keep_ref, send_ref, got, scr, sem_in, sem):
    y, c, zh = (lax.axis_index(a) for a in ("y", "c", "zh"))
    loads = []
    for m in list(range(BLOCKS)) + [BLOCKS]:
        at = pl.ds(T * m, T if m < BLOCKS else T + 16)
        loads.append(pltpu.make_async_copy(got_ref.at[:, at], got.at[:, at], sem_in.at[m]))
    loads[-1].start()
    for copy in loads[:-1]:
        copy.start()

    def slot(there, here, core):
        bits = gray(jnp.int32(there)) ^ gray(here)
        return bits if core else (bits & 1) * 2 + (bits >> 1)

    loads[-1].wait()
    tokens = jnp.concatenate([got[s, TOK : TOK + T] for s in range(LAYERS)], axis=0)
    extra = sum(got[s, TOK + T :].astype(F32) for s in range(LAYERS))
    bias = jnp.sum(tokens[:, 256:].astype(F32), axis=0, keepdims=True)
    bias = jnp.concatenate([bias[:, :ROWS]] * 4, axis=1)
    for m in range(BLOCKS):
        loads[m].wait()
        normed = jnp.concatenate([got[s, T * m : T * (m + 1)] for s in range(LAYERS)], axis=0)
        keys = tn(normed, tokens[:, :256])
        rates = tn(tokens[:, 256:], normed)[:H]
        rows = jnp.concatenate(
            [rates, extra[m : m + 1], extra[m + 8 : m + 9], bias, jnp.zeros((5, BLOCK), F32)],
            axis=0,
        )
        low = cut_rows(rows)
        for i in range(4):
            d = 4 * m + i
            y_at, z_at = slot(d // 2 % 4, y, d % 2), slot(d // 8, zh, d % 2)
            c_at = (d + c) % 2
            scr[c_at, y_at, z_at, :ROWS] = keys[ROWS * i : ROWS * (i + 1)].astype(BF16)
            scr[c_at, y_at, z_at, ROWS:] = low[i].astype(BF16)
        if m % 2:
            for core in range(2):
                z_at = slot(m // 2, zh, core)
                for i, ref in enumerate((keep_ref, send_ref)):

                    @pl.when((core + c) % 2 == i)
                    def _(i=i, ref=ref, z_at=z_at):
                        pltpu.make_async_copy(scr.at[i, :, z_at], ref.at[:, z_at], sem.at[i]).start()

    for i, ref in enumerate((keep_ref, send_ref)):
        pltpu.make_async_copy(scr.at[i], ref, sem.at[i]).wait()


def final_kernel(a_ref, b_ref, c_ref, d_ref, scales_ref, keys_ref, rates_ref, bias_ref):
    total = a_ref[...].astype(F32) + b_ref[...].astype(F32)
    total = total + c_ref[...].astype(F32) + d_ref[...].astype(F32)
    keys_ref[...] = total[:ROWS]
    rates = jnp.concatenate([total[ROWS:, :C], total[ROWS:, C:]], axis=0)
    rates_ref[...] = rates[:H, :ROWS]
    scales_ref[...] = rates[24:26, :ROWS]
    bias_ref[...] = rates[26:27, :H]


ANY = pl.BlockSpec(memory_space=pl.ANY)
VMEM = pl.BlockSpec(memory_space=pltpu.VMEM)
PARAMS = pltpu.CompilerParams(vmem_limit_bytes=30 * 1024 * 1024)


def shape(*dims, dtype=BF16):
    return jax.ShapeDtypeStruct(dims, dtype)


def call(kernel, outs, ins, scratch, out_spec=None, cost=None):
    flops, moved = cost
    return pl.pallas_call(
        kernel,
        out_shape=outs,
        in_specs=ins,
        out_specs=out_spec or [VMEM] * len(outs),
        scratch_shapes=scratch,
        compiler_params=PARAMS,
        cost_estimate=pl.CostEstimate(flops=flops, bytes_accessed=moved, transcendentals=0),
    )


def ring_pairs(first):
    pairs = []
    for i in range(4):
        for c in range(2):
            to = i ^ 1 if (c == 0) == first else 3 - i
            pairs.append((i * 2 + c, to * 2 + c))
    return pairs


def swap(array, axis, first):
    return lax.ppermute(array, (axis, "c"), ring_pairs(first))


def other_core(array):
    return lax.ppermute(array, "c", [(0, 1), (1, 0)])


def opposite(array, axis):
    return lax.ppermute(array, axis, [(i, i ^ 2) for i in range(4)])


def gather_ring(array, axis, direct=False):
    one = swap(array, axis, True)
    two = swap(array, axis, False)
    return [array, one, two, opposite(array, axis) if direct else swap(one, axis, False)]


def add(a, b):
    return (a.astype(F32) + b.astype(F32)).astype(BF16)


def per_device(entries, cotangents, scales, key_weight, rate_weight, rate_bias):
    x, zl, zh, y, c = (lax.axis_index(a) for a in ("x", "zl", "zh", "y", "c"))
    rates = rate_weight[0].T

    def put(a, row, lane):
        pads = (row, PIECE - row - a.shape[0], 0), (lane, 256 - lane - a.shape[1], 0)
        return lax.pad(a, jnp.zeros((), BF16), pads)

    shifted = put(rates, ROWS - 16, C)
    shifted = jnp.where(iota((PIECE, 256), 0) >= ROWS, shifted, jnp.zeros_like(shifted))
    packed = put(key_weight[0], 0, 0) + put(rates, ROWS, 0) + shifted
    packed = packed + put(scales[0], ROWS + 8, C) + put(rate_bias, ROWS + 10, C)

    along = jnp.stack(gather_ring(packed, "zh", direct=True))
    first, second = partner(zh, c, True), partner(zh, c, False)
    across = partner(second, c, True)
    order = [jnp.where(j == first, 1, jnp.where(j == second, 2, jnp.where(j == across, 3, 0))) for j in range(4)]
    along = jnp.take(along, jnp.stack(order), axis=0)
    pairs = []
    for z in range(8):
        for core in range(2):
            to = z ^ 1 if core == 0 else (z + 1 if z % 2 else z - 1) % 8
            pairs.append(tuple(((i % 2) * 4 + i // 2) * 2 + core for i in (z, to)))
    other = lax.ppermute(along, ("zl", "zh", "c"), pairs)
    both = jnp.where(zl == 0, jnp.stack([along, other]), jnp.stack([other, along]))

    left = jnp.stack(gather_ring(both[..., :C], "x", direct=True))
    right = jnp.stack(gather_ring(both[..., C:], "y", direct=True))
    left = gather_ring(left, "y")
    right = gather_ring(right, "x")
    left = left + [other_core(a) for a in left]
    right = right + [other_core(a) for a in right]

    sent = call(
        sequence_kernel,
        [shape(LAYERS, SENT, BLOCK)],
        [VMEM] * 16 + [ANY] * 2,
        [
            pltpu.VMEM((LAYERS, 4, 4, 2, PIECE, 256), BF16),
            pltpu.VMEM((LAYERS, T, D), BF16),
            pltpu.VMEM((LAYERS, T, D), BF16),
            pltpu.VMEM((LAYERS, T, D), BF16),
            pltpu.VMEM((LAYERS, T, D), BF16),
            pltpu.VMEM((LAYERS, T, W), F32),
            pltpu.VMEM((LAYERS, 1, W), F32),
            pltpu.VMEM((LAYERS, T, 256), F32),
            pltpu.VMEM((LAYERS, T, 256), F32),
            pltpu.VMEM((2, T, D), BF16),
            pltpu.SemaphoreType.DMA((2,)),
        ],
        cost=(8_000_000_000, 30_000_000),
    )(*left, *right, entries, cotangents)[0]

    groups = [
        [
            (((i * 4) + (z - i % 2 * core) % 4) * 4 + row) * 2 + core
            for i in range(LAYERS)
        ]
        for z in range(4)
        for row in range(4)
        for core in range(2)
    ]
    got = lax.all_to_all(
        sent, ("x", "zl", "zh", "y", "c"), 0, 0, axis_index_groups=groups, tiled=True
    )
    half = shape(4, 4, PIECE, 256)
    keep, send = call(
        weight_kernel,
        [half, half],
        [ANY],
        [
            pltpu.VMEM((LAYERS, SENT, BLOCK), BF16),
            pltpu.VMEM((2, 4, 4, PIECE, 256), BF16),
            pltpu.SemaphoreType.DMA((BLOCKS + 1,)),
            pltpu.SemaphoreType.DMA((2,)),
        ],
        [ANY] * 2,
        cost=(600_000_000, 4_000_000),
    )(got)
    got = other_core(send)
    got = swap(add(keep[2:], got[2:]), "y", True), keep[:2], got[:2]
    keep = add(got[1], got[2])
    got = got[0]
    got, keep = swap(add(keep[1], got[1]), "y", False), add(keep[0], got[0])
    got = add(keep, got)
    parts = [
        got[0],
        swap(got[2], "zh", True),
        swap(got[1], "zh", False),
        opposite(got[3], "zh"),
    ]
    g_scales, g_keys, g_rates, g_bias = call(
        final_kernel,
        [
            shape(2, ROWS, dtype=F32),
            shape(ROWS, 256, dtype=F32),
            shape(H, ROWS, dtype=F32),
            shape(1, H, dtype=F32),
        ],
        [VMEM] * 4,
        [],
        cost=(0, 500_000),
    )(*parts)
    return g_scales[None], g_keys[None], g_rates.T[None], g_bias


def solution(mesh):
    fine = Mesh(mesh.devices.reshape(4, 2, 4, 4, 2), ("x", "zl", "zh", "y", "c"))
    placed = (
        P(None, None, DP, None),
        P(None, None, DP, None),
        P(SECTION, None, DP),
        P(SECTION, DP, None),
        P(SECTION, DP, None),
        P(SECTION, None),
    )
    return jax.shard_map(
        per_device,
        mesh=fine,
        in_specs=placed,
        out_specs=(
            P(SECTION, None, DP),
            P(SECTION, DP, None),
            P(SECTION, DP, None),
            P(SECTION, None),
        ),
        check_vma=False,
    )
```
